32 devices in a mesh: tower: 2 (over core), rows: 16 (over z, y, x).
Axes of the slice: x: 2, y: 2, z: 4, core: 2. Of those that a mesh axis runs over, the one named last changes fastest.
Arguments:
- hidden_in: bfloat16 [2, 16, 512, 768], P('tower', 'rows'), may hold values from -6 to 6
- segment_ids: int32 [2, 16, 512], P('tower', 'rows'), may hold values from 0 to 7, never falling along the last dimension, each value on 1 to 128 neighbouring positions
- positives: int32 [128], P('rows'), may hold values from 0 to 127, each once
- attn_gain: bfloat16 [768], replicated, may hold values from 0.5 to 1.5
- w_query: bfloat16 [768, 768], replicated, may hold values from -0.109375 to 0.109375
- w_key: bfloat16 [768, 768], replicated, may hold values from -0.109375 to 0.109375
- w_value: bfloat16 [768, 768], replicated, may hold values from -0.21875 to 0.21875
- w_attn_out: bfloat16 [768, 768], replicated, may hold values from -0.875 to 0.875
- rel_table: bfloat16 [32, 12], replicated, may hold values from -4 to 4
- ffn_gain: bfloat16 [768], replicated, may hold values from 0.5 to 1.5
- w_ffn_in: bfloat16 [768, 3072], replicated, may hold values from -0.21875 to 0.21875
- w_ffn_out: bfloat16 [3072, 768], replicated, may hold values from -0.15625 to 0.15625
- final_gain: bfloat16 [768], replicated, may hold values from 0.5 to 1.5
Outputs:
- embeddings: float32 [2, 128, 768], P('tower', 'rows')
- query_loss: float32 [16, 2, 4], P('rows', 'tower')
- grad_hidden: float32 [2, 16, 512, 768], P('tower', 'rows')
- grad_attn_gain: float32 [768], P('rows')
- grad_query: float32 [768, 768], P('rows')
- grad_key: float32 [768, 768], P('rows')
- grad_value: float32 [768, 768], P('rows')
- grad_attn_out: float32 [768, 768], P('rows')
- grad_rel_table: float32 [32, 12], replicated
- grad_ffn_gain: float32 [768], P('rows')
- grad_ffn_in: float32 [768, 3072], P('rows')
- grad_ffn_out: float32 [3072, 768], P('rows')
- grad_final_gain: float32 [768], P('rows')
The draws below stay inside these ranges and needn't reach their ends.
Inputs may be any that keep to these rules, and one draw needn't show every extreme that they name: `segment_ids`: in every row the ids run from 0 to 7, never falling, and each id is present; an item has 1 to 128 tokens and some row holds an item of exactly 128 tokens. `positives`: every document is the positive of exactly one query.
All inputs are finite; a program needn't handle non-finite values.
Results may differ from the reference program's by a relative error of at most 0.013.
The reference program's roundings to bfloat16 on the way count: a program that leaves them out, or rounds other values in their place, can miss the bound.
Values sent between devices are 32-bit elements; how exact they have to be, the bound alone decides.
A program may use at most 256 MiB of HBM per device.

```python
import math
import jax
import jax.numpy as jnp
import numpy as np
from jax import lax

D = 768
HEADS = 12
HEAD_DIM = 64
FF = 3072
BUCKETS = 32
MAX_DIST = 128
SEQ = 512
ITEM_ROW = 8
MOST_LEN = 128
ROWS = 16
ITEM_DEV = 8
ITEMS = 128
N_ROWS = 16


def block_scale(own_key, shape, shards, smallest, largest):
    level = 1.0
    for dim, shards_of in shards:
        heights = jax.random.uniform(jax.random.fold_in(jax.random.fold_in(own_key, 6), dim), (shards_of,), jnp.float32, smallest / len(shards), largest / len(shards))
        level = level * jnp.repeat(jnp.exp(heights), shape[dim] // shards_of).reshape((-1,) + (1,) * (len(shape) - 1 - dim))
    return level


def length_profile(count, total, limit, lean):
    weights = [(1 << 20) // math.isqrt(grade ** lean) + 1 for grade in range(2, count + 1)]
    surplus, given = total - limit - (count - 1), [1] * (count - 1)
    while surplus > 0:
        candidates = [i for i in range(count - 1) if given[i] < limit]
        whole, remaining = sum([weights[i] for i in candidates]), surplus
        for i in candidates:
            addition = min(limit - given[i], max(1, remaining * weights[i] // whole), surplus)
            given[i] = given[i] + addition
            surplus = surplus - addition
    return np.array([limit] + given)


def ragged(stream_key, amount, total, reach, lean):
    if amount == 2:
        one = jax.random.randint(stream_key, (), max(1, total - reach), min(reach, total - 1) + 1)
        return jnp.stack([one, total - one])
    sizes = jnp.asarray(length_profile(amount, total, reach, lean), jnp.int32)
    couples = (amount - 1) // 2
    source_of, sink = sizes[1:1 + 2 * couples:2], sizes[2:2 + 2 * couples:2]
    margin = jnp.minimum(source_of - 1, reach - sink)
    passed = jax.random.randint(jax.random.fold_in(stream_key, 1), (couples,), 0, 1 << 20) % (margin + 1)
    sizes = sizes.at[1:1 + 2 * couples:2].set(source_of - passed).at[2:2 + 2 * couples:2].set(sink + passed)
    return sizes[jax.random.permutation(jax.random.fold_in(stream_key, 2), amount)]


def centred(key, extent, width, limit, split=(), kind=jnp.bfloat16):
    entries = width * jax.random.normal(key, extent, jnp.float32)
    if split:
        entries = entries * block_scale(key, extent, split, -0.22, 0.18)
    return jnp.clip(entries, -limit, limit).astype(kind)


def setup_inputs(seed: int = 0) -> dict:
    streams_of = jax.random.split(jax.random.key(seed), 14)
    return {
        "hidden_in": centred(streams_of[0], (2, ROWS, SEQ, D), 1.0, 6.0, ((0, 2), (1, 16))),
        "segment_ids": jax.vmap(lambda own: jnp.searchsorted(jnp.cumsum(ragged(own, ITEM_ROW, SEQ, MOST_LEN, 2)), jnp.arange(SEQ), side="right"))(jax.random.split(streams_of[1], 2 * ROWS)).reshape((2, ROWS, SEQ)).astype(jnp.int32),
        "positives": jax.random.permutation(streams_of[2], ITEMS).astype(jnp.int32),
        "attn_gain": jnp.clip(1.0 + 0.1 * jax.random.normal(streams_of[3], (D,), jnp.float32), 0.5, 1.5).astype(jnp.bfloat16),
        "w_query": centred(streams_of[4], (D, D), (4 * D) ** -0.5, 0.109375),
        "w_key": centred(streams_of[5], (D, D), (4 * D) ** -0.5, 0.109375),
        "w_value": centred(streams_of[6], (D, D), D ** -0.5, 0.21875),
        "w_attn_out": centred(streams_of[7], (D, D), (D // 16) ** -0.5, 0.875),
        "rel_table": centred(streams_of[8], (BUCKETS, HEADS), 1.0, 4.0),
        "ffn_gain": jnp.clip(1.0 + 0.1 * jax.random.normal(streams_of[9], (D,), jnp.float32), 0.5, 1.5).astype(jnp.bfloat16),
        "w_ffn_in": centred(streams_of[10], (D, FF), D ** -0.5, 0.21875),
        "w_ffn_out": centred(streams_of[11], (FF, D), (FF // 2) ** -0.5, 0.15625),
        "final_gain": jnp.clip(1.0 + 0.1 * jax.random.normal(streams_of[12], (D,), jnp.float32), 0.5, 1.5).astype(jnp.bfloat16),
    }


epsilon = 1e-06
logit_divisor = 0.01
loss_scale = 16.0
far_below = -1000000000.0
peak_similarity = lax.Precision.HIGHEST

@jax.custom_vjp
def low(v):
    return lax.optimization_barrier(v.astype(jnp.bfloat16)).astype(jnp.float32)

@jax.custom_vjp
def low_back(v):
    return v

def low_keep(v):
    return (low(v), None)

def low_pass(kept, grad):
    return (grad,)

def back_keep(v):
    return (v, None)

def back_low(kept, grad):
    return (low(grad),)
low.defvjp(low_keep, low_pass)
low_back.defvjp(back_keep, back_low)

def bucket_onehot(seq_len, bucket_count, max_distance):
    half_count = bucket_count // 2
    exact_count = half_count // 2
    log_steps = half_count - exact_count
    bounds = []
    for section_index in range(1, log_steps):
        target = exact_count ** (log_steps - section_index) * max_distance ** section_index
        lowest = exact_count
        while lowest ** log_steps < target:
            lowest = lowest + 1
        bounds.append(lowest)
    onehot = np.zeros((2 * seq_len - 1, bucket_count), np.float32)
    for offset in range(2 * seq_len - 1):
        relative = offset - (seq_len - 1)
        distance = abs(relative)
        bucket = half_count if relative > 0 else 0
        if distance < exact_count:
            bucket = bucket + distance
        else:
            bucket = bucket + exact_count + len([boundary for boundary in bounds if distance >= boundary])
        onehot[offset, bucket] = 1.0
    return onehot

def rms_scale(values, gain):
    return values * lax.rsqrt(lax.optimization_barrier(jnp.mean(values * values, axis=-1, keepdims=True)) + epsilon) * gain

def matmul(left_side, right_side):
    return jnp.dot(left_side, right_side, precision=peak_similarity)

def position_bias(rel_table):
    onehot = jnp.asarray(bucket_onehot(SEQ, BUCKETS, MAX_DIST))
    by_offset = jnp.dot(onehot, rel_table, precision=peak_similarity)
    offsets = np.arange(SEQ)[None, :] - np.arange(SEQ)[:, None] + SEQ - 1
    return jnp.transpose(by_offset[offsets], (2, 0, 1))

def group_forward(params, bias_full, rows_x, rows_seg):
    attn_gain, w_query, w_key, w_value, w_attn_out, ffn_gain, w_ffn_in, w_ffn_out, final_gain = params
    group_rows = rows_x.shape[0]

    def split_heads(values):
        return values.reshape(group_rows, SEQ, HEADS, HEAD_DIM)
    normed_one = low(rms_scale(rows_x, attn_gain))
    query_proj = split_heads(low(low_back(matmul(normed_one, w_query))))
    key_proj = split_heads(low(low_back(matmul(normed_one, w_key))))
    value_proj = split_heads(low(low_back(matmul(normed_one, w_value))))
    raw_scores = low_back(jnp.einsum('gshd,gthd->ghst', query_proj, key_proj, precision=peak_similarity))
    same_item = (rows_seg[:, :, None] == rows_seg[:, None, :])[:, None]
    masked_scores = jnp.where(same_item, raw_scores + bias_full[None], far_below)
    row_peak = lax.optimization_barrier(jnp.max(masked_scores, axis=-1, keepdims=True))
    exp_terms = jnp.exp(masked_scores - row_peak)
    attn_probs = exp_terms / lax.optimization_barrier(jnp.sum(exp_terms, axis=-1, keepdims=True))
    combined_attention_output = jnp.einsum('ghst,gthd->gshd', low(attn_probs), value_proj, precision=peak_similarity)
    attended = low(low_back(combined_attention_output)).reshape(group_rows, SEQ, HEADS * HEAD_DIM)
    middle = rows_x + low_back(matmul(attended, w_attn_out))
    normed_two = low(rms_scale(middle, ffn_gain))
    inner = low_back(matmul(normed_two, w_ffn_in))
    hidden = low(jax.nn.gelu(inner, approximate=True))
    final_sum = middle + low_back(matmul(hidden, w_ffn_out))
    normed_three = rms_scale(final_sum, final_gain)
    member = (rows_seg[:, None, :] == jnp.arange(ITEM_ROW, dtype=jnp.int32)[None, :, None]).astype(jnp.float32)
    counts = lax.optimization_barrier(jnp.sum(member, axis=-1, keepdims=True))
    return jnp.einsum('gis,gsd->gid', member, normed_three, precision=peak_similarity) / counts

def reference(hidden_in, segment_ids, positives, attn_gain, w_query, w_key, w_value, w_attn_out, rel_table, ffn_gain, w_ffn_in, w_ffn_out, final_gain):
    total_rows = 2 * hidden_in.shape[1]
    group_rows = math.gcd(total_rows, max(1, 4096 // SEQ))
    group_total = total_rows // group_rows
    rows_seg = segment_ids.reshape(group_total, group_rows, SEQ)

    def forward(tokens, attn_gain, w_query, w_key, w_value, w_attn_out, rel_table, ffn_gain, w_ffn_in, w_ffn_out, final_gain):
        bias_full = position_bias(rel_table)
        params = (attn_gain, w_query, w_key, w_value, w_attn_out, ffn_gain, w_ffn_in, w_ffn_out, final_gain)
        rows_x = tokens.reshape(group_total, group_rows, SEQ, D)

        def group_step(carry_value, packed):
            return (carry_value, jax.checkpoint(group_forward)(params, bias_full, packed[0], packed[1]))
        carry_out, pooled = lax.scan(group_step, jnp.zeros((), jnp.float32), (rows_x, rows_seg))
        pooled = pooled.reshape(2, ITEMS, D)
        inverse = lax.rsqrt(lax.optimization_barrier(jnp.sum(pooled * pooled, axis=-1, keepdims=True)) + epsilon)
        encoded_vector_list = pooled * inverse
        similarity_table = jnp.dot(encoded_vector_list[0], encoded_vector_list[1].T, precision=peak_similarity) / logit_divisor
        row_peak = lax.optimization_barrier(jnp.max(similarity_table, axis=1, keepdims=True))
        summed = lax.optimization_barrier(jnp.sum(jnp.exp(similarity_table - row_peak), axis=1))
        chosen = jnp.take_along_axis(similarity_table, positives[:, None], axis=1)[:, 0]
        losses = row_peak[:, 0] + jnp.log(summed) - chosen
        return (loss_scale * jnp.sum(losses), (encoded_vector_list, losses))
    floats = (hidden_in.astype(jnp.float32), attn_gain.astype(jnp.float32), w_query.astype(jnp.float32), w_key.astype(jnp.float32), w_value.astype(jnp.float32), w_attn_out.astype(jnp.float32), rel_table.astype(jnp.float32), ffn_gain.astype(jnp.float32), w_ffn_in.astype(jnp.float32), w_ffn_out.astype(jnp.float32), final_gain.astype(jnp.float32))
    objective, pullback, extras = jax.vjp(forward, *floats, has_aux=True)
    grads = pullback(jnp.ones_like(objective))
    encoded_vector_list, losses = extras
    return (encoded_vector_list, losses.reshape(N_ROWS, 2, ITEM_DEV // 2), grads[0], grads[1], grads[2], grads[3], grads[4], grads[5], grads[6], grads[7], grads[8], grads[9], grads[10])
```

```python
import functools
import math

import jax
import jax.numpy as jnp
import numpy as np
from jax import lax
from jax.experimental import pallas as pl
from jax.experimental.pallas import tpu as pltpu
from jax.sharding import PartitionSpec as P

BUCKETS = 32
MAX_DIST = 128
ITEM_ROW = 8
BLOCK = 128

epsilon = 1e-06
logit_divisor = 0.01
loss_scale = 16.0
far_below = -1000000000.0
exact = lax.Precision.HIGHEST
gelu_cubic = 0.044715
gelu_factor = math.sqrt(2.0 / math.pi)
f32 = jnp.float32
bf16 = jnp.bfloat16
VMEM = pltpu.VMEM
VMEM_LIMIT = 60 * 2**20


def dot_nn(a, b, precision=None):
    return lax.dot_general(
        a, b, (((1,), (0,)), ((), ())), precision=precision, preferred_element_type=f32
    )


def dot_nt(a, b, precision=None):
    return lax.dot_general(
        a, b, (((1,), (1,)), ((), ())), precision=precision, preferred_element_type=f32
    )


def dot_tn(a, b, precision=None):
    return lax.dot_general(
        a, b, (((0,), (0,)), ((), ())), precision=precision, preferred_element_type=f32
    )


def bucket_of(relative, bucket_count, max_distance):
    half_count = bucket_count // 2
    exact_count = half_count // 2
    log_steps = half_count - exact_count
    bounds = []
    for section_index in range(1, log_steps):
        target = exact_count ** (log_steps - section_index) * max_distance**section_index
        lowest = exact_count
        while lowest**log_steps < target:
            lowest = lowest + 1
        bounds.append(lowest)
    distance = abs(relative)
    bucket = half_count if relative > 0 else 0
    if distance < exact_count:
        return bucket + distance
    return bucket + exact_count + len([b for b in bounds if distance >= b])


def lane_buckets():
    width = 4 * BLOCK
    onehot = np.zeros((BUCKETS, width), np.float32)
    for m in range(width):
        relative = (m if m < 3 * BLOCK else m - width) - BLOCK
        onehot[bucket_of(relative, BUCKETS, MAX_DIST), m] = 1.0
    return onehot


def row_of_gain(ref):
    return ref[...].astype(f32).reshape(1, ref.shape[0])


def rms_inverse(values):
    return lax.rsqrt(jnp.mean(values * values, axis=-1, keepdims=True) + epsilon)


def build_bias(table_ref, lanes_ref, by_offset, bias):
    heads = table_ref.shape[0]
    by_offset[0:heads, :] = dot_nn(table_ref[...], lanes_ref[...])

    def one(h, carry):
        row = jnp.broadcast_to(by_offset[pl.ds(h, 1), :], (BLOCK, 4 * BLOCK))
        bias[h] = pltpu.roll(row, 0, 1, stride=1, stride_axis=0)[:, : 3 * BLOCK]
        return carry

    lax.fori_loop(0, heads, one, 0)


def column_of(row):
    return jnp.broadcast_to(row, (8, row.shape[1])).T[:, 0:1]


def key_range(block, blocks):
    return max(block - 1, 0) * BLOCK, min(block + 2, blocks) * BLOCK


def forward_kernel(
    x_ref, seg_ref, g1_ref, g2_ref, g3_ref, table_ref, lanes_ref,
    wq_hbm, wk_hbm, wv_hbm, wo_hbm, w1_hbm, w2_hbm,
    q_ref, k_ref, v_ref, att_ref, mid_ref, inner_ref, hid_ref, fin_ref, pooled_ref,
    wq, wk, wv, wo, w1, w2, by_offset, bias, sems,
):
    pairs = [(wq_hbm, wq), (wk_hbm, wk), (wv_hbm, wv), (wo_hbm, wo), (w1_hbm, w1), (w2_hbm, w2)]
    copies = [pltpu.make_async_copy(a, b, sems.at[i]) for i, (a, b) in enumerate(pairs)]
    for c in copies:
        c.start()
    seq, width = x_ref.shape
    heads = table_ref.shape[0]
    blocks = seq // BLOCK
    build_bias(table_ref, lanes_ref, by_offset, bias)
    x = x_ref[...].astype(f32)
    normed = ((x * rms_inverse(x)) * row_of_gain(g1_ref)).astype(bf16)
    for i, (w, out) in enumerate(((wq, q_ref), (wk, k_ref), (wv, v_ref))):
        copies[i].wait()
        out[...] = dot_nn(normed, w[...]).astype(bf16)
    seg_row = seg_ref[...].astype(f32)
    seg_col = column_of(seg_row)
    low_half = lax.broadcasted_iota(jnp.int32, (seq, BLOCK), 1) < BLOCK // 2

    def pair(p, carry):
        lanes = pl.ds(pl.multiple_of(p * BLOCK, BLOCK), BLOCK)
        qp, kp, vp = q_ref[:, lanes], k_ref[:, lanes], v_ref[:, lanes]
        zero = jnp.zeros_like(qp)
        qe = (jnp.where(low_half, qp, zero), jnp.where(low_half, zero, qp))
        for b in range(blocks):
            lo, hi = key_range(b, blocks)
            mine = slice(b * BLOCK, (b + 1) * BLOCK)
            same = seg_col[mine] == seg_row[:, lo:hi]
            first = lo - (b - 1) * BLOCK
            outs = []
            for e in range(2):
                s = dot_nt(qe[e][mine], kp[lo:hi])
                s = s + bias[2 * p + e, :, first : first + hi - lo]
                s = jnp.where(same, s, far_below)
                terms = jnp.exp(s - jnp.max(s, axis=-1, keepdims=True))
                scale = 1.0 / jnp.sum(terms, axis=-1, keepdims=True)
                outs.append(dot_nn((terms * scale).astype(bf16), vp[lo:hi]))
            att_ref[mine, lanes] = jnp.where(low_half[mine], outs[0], outs[1]).astype(bf16)
        return carry

    lax.fori_loop(0, heads // 2, pair, 0)
    copies[3].wait()
    middle = x + dot_nn(att_ref[...], wo[...])
    mid_ref[...] = middle
    normed_two = ((middle * rms_inverse(middle)) * row_of_gain(g2_ref)).astype(bf16)
    copies[4].wait()
    part = 512
    for c in range(0, w1.shape[1], part):
        v = dot_nn(normed_two, w1[:, c : c + part])
        inner_ref[:, c : c + part] = v
        t = jnp.tanh(gelu_factor * (v + gelu_cubic * (v * v * v)))
        hid_ref[:, c : c + part] = (v * (0.5 * (1.0 + t))).astype(bf16)
    copies[5].wait()
    final = mid_ref[...] + dot_nn(hid_ref[...], w2[...])
    fin_ref[...] = final
    normed_three = (final * rms_inverse(final)) * row_of_gain(g3_ref)
    items = lax.broadcasted_iota(jnp.int32, (ITEM_ROW, seq), 0).astype(f32)
    member = (items == seg_row).astype(f32)
    counts = jnp.sum(member, axis=-1, keepdims=True)
    pooled_ref[...] = dot_nn(member, normed_three, exact) / counts


def forward_call(x, seg, g1, g2, g3, table, lanes, wq, wk, wv, wo, w1, w2):
    seq, width = x.shape
    ff = w1.shape[1]
    heads = table.shape[0]
    any_spec = pl.BlockSpec(memory_space=pl.ANY)
    vm = pl.BlockSpec(memory_space=VMEM)
    s = jax.ShapeDtypeStruct
    return pl.pallas_call(
        forward_kernel,
        name="layer_forward",
        out_shape=[
            s((seq, width), bf16), s((seq, width), bf16), s((seq, width), bf16),
            s((seq, width), bf16), s((seq, width), f32), s((seq, ff), f32),
            s((seq, ff), bf16), s((seq, width), f32), s((ITEM_ROW, width), f32),
        ],
        in_specs=[vm] * 7 + [any_spec] * 6,
        out_specs=[vm] * 9,
        scratch_shapes=[
            VMEM((width, width), bf16), VMEM((width, width), bf16), VMEM((width, width), bf16),
            VMEM((width, width), bf16), VMEM((width, ff), bf16), VMEM((ff, width), bf16),
            VMEM((16, 4 * BLOCK), f32), VMEM((heads, BLOCK, 3 * BLOCK), f32),
            pltpu.SemaphoreType.DMA((6,)),
        ],
        compiler_params=pltpu.CompilerParams(vmem_limit_bytes=VMEM_LIMIT),
    )(x, seg, g1, g2, g3, table, lanes, wq, wk, wv, wo, w1, w2)


MESH_IDS = pl.DeviceIdType.MESH


class Axis:

    def __init__(self, size, stride):
        self.size, self.stride = size, stride

    def place(self, row):
        return lax.rem(lax.div(row, self.stride), self.size)


UNIT = 128
SLOTS = 2
JOBS = {
    "out_0": ("zxy", (("out", 0, 0), ("out", 0, 1), ("out", 0, 2), ("out", 0, 3),)),
    "out_1": ("yzx", (("out", 1, 0), ("out", 1, 1), ("out", 1, 2), ("out", 1, 3),)),
    "out_2": ("xyz", (("out", 2, 0), ("out", 2, 1), ("out", 2, 2), ("out", 2, 3),)),
    "in_0": ("yzx", (("in", 0, 0), ("in", 1, 0), ("in", 2, 0), ("in", 3, 0),)),
    "in_1": ("xyz", (("in", 4, 0), ("in", 5, 0), ("in", 6, 0), ("in", 7, 0),)),
    "in_2": ("xyz", (("in", 8, 0), ("in", 9, 0), ("in", 10, 0), ("in", 11, 0),)),
    "attn_0": ("yzx", (("attn", 0, 0), ("attn", 1, 0),)),
    "attn_1": ("zxy", (("attn", 2, 0),)),
    "qkv0_0": ("xyz", (("value", 0, 0), ("query", 0, 0), ("key", 0, 0),)),
    "qkv1_0": ("yzx", (("value", 1, 0), ("query", 1, 0),)),
    "qkv1_1": ("xyz", (("key", 1, 0),)),
    "qkv2_0": ("xzy", (("value", 2, 0),)),
    "qkv2_1": ("yxz", (("query", 2, 0),)),
    "qkv2_2": ("xyz", (("key", 2, 0),)),
}
STEPS_SIZES = (2, 2, 4)
STEPS = (
    ("send", "out_0"), ("send", "out_1"), ("out_0", "own", 0), ("out_0", 0, 0), ("send", "out_2"),
    ("out_1", "own", 0), ("out_1", 0, 0), ("inner", 0), ("inner", 1), ("out_2", "own", 0), ("out_2", 0, 0),
    ("inner", 2), ("inner", 3), ("inner", 4), ("inner", 5), ("send", "in_0"), ("send", "in_1"),
    ("in_0", "own", 0), ("in_0", 0, 0), ("out_0", 0, 1), ("send", "in_2"), ("in_1", "own", 0), ("in_1", 0, 0),
    ("out_1", 0, 1), ("out_1", 1, 0), ("two", 0), ("out_2", 0, 1), ("out_2", 1, 0), ("out_0", 0, 2),
    ("in_2", "own", 0), ("in_2", 0, 0), ("send", "attn_0"), ("send", "attn_1"), ("normed", 0),
    ("attended", 0), ("heads", 0), ("out_1", 1, 1), ("out_0", 0, 3), ("out_0", 1, 0), ("in_0", 0, 1),
    ("in_0", 1, 0), ("attn_0", "own", 0), ("attn_0", 0, 0), ("attn_1", "own", 0), ("attn_1", 0, 0),
    ("heads", 3), ("out_1", 1, 2), ("in_1", 0, 1), ("in_1", 1, 0), ("send", "qkv0_0"), ("out_2", 1, 1),
    ("out_2", 2, 0), ("heads", 1), ("out_1", 1, 3), ("out_1", 2, 0), ("in_0", 1, 1), ("qkv0_0", "own", 0),
    ("qkv0_0", 0, 0), ("heads", 4), ("attn_0", 0, 1), ("attn_0", 1, 0), ("attn_1", 0, 1), ("in_0", 1, 2),
    ("in_2", 0, 1), ("in_2", 1, 0), ("send", "qkv1_0"), ("send", "qkv1_1"), ("heads", 2), ("out_2", 2, 1),
    ("attn_1", 0, 2), ("out_1", 2, 1), ("in_1", 1, 1), ("in_1", 2, 0), ("in_0", 1, 3), ("in_0", 2, 0),
    ("out_0", 1, 1), ("out_0", 2, 0), ("qkv1_0", "own", 0), ("qkv1_0", 0, 0), ("out_2", 2, 2),
    ("attn_1", 0, 3), ("attn_1", 1, 0), ("attn_0", 1, 1), ("qkv1_1", "own", 0), ("qkv1_1", 0, 0),
    ("out_1", "end", 0), ("heads", 5), ("out_2", 2, 3), ("in_1", 2, 1), ("in_2", 1, 1), ("in_2", 2, 0),
    ("attn_0", 1, 2), ("out_0", 2, 1), ("out_2", "end", 0), ("send", "qkv2_0"), ("qkv0_0", 0, 1),
    ("qkv0_0", 1, 0), ("out_0", "end", 0), ("send", "qkv2_1"), ("in_1", 2, 2), ("send", "qkv2_2"),
    ("in_0", 2, 1), ("attn_0", 1, 3), ("attn_0", 2, 0), ("qkv2_0", "own", 0), ("qkv2_0", 0, 0),
    ("attn_1", 1, 1), ("attn_1", 2, 0), ("in_2", 2, 1), ("in_1", 2, 3), ("qkv1_0", 0, 1), ("qkv1_0", 1, 0),
    ("qkv2_1", "own", 0), ("qkv2_1", 0, 0), ("qkv2_2", "own", 0), ("qkv2_2", 0, 0), ("in_0", "end", 0),
    ("in_1", "end", 0), ("one", 0), ("qkv1_0", 1, 1), ("attn_0", 2, 1), ("in_2", 2, 2), ("qkv0_0", 1, 1),
    ("qkv0_0", 2, 0), ("attn_1", 2, 1), ("qkv2_0", 0, 1), ("qkv2_0", 1, 0), ("qkv1_1", 0, 1),
    ("qkv1_1", 1, 0), ("attn_0", "end", 0), ("attn_1", "end", 0), ("small", 0), ("qkv1_0", 1, 2),
    ("in_2", 2, 3), ("small", 1, 0), ("qkv0_0", 2, 1), ("qkv2_1", 0, 1), ("qkv2_1", 1, 0), ("in_2", "end", 0),
    ("qkv2_2", 0, 1), ("qkv2_2", 1, 0), ("qkv1_0", 1, 3), ("qkv1_0", 2, 0), ("qkv1_1", 1, 1),
    ("qkv1_1", 2, 0), ("qkv0_0", 2, 2), ("qkv2_0", 1, 1), ("qkv0_0", 2, 3), ("qkv2_1", 1, 1),
    ("qkv2_1", 2, 0), ("qkv1_1", 2, 1), ("qkv2_0", 1, 2), ("qkv2_2", 1, 1), ("qkv2_2", 2, 0), ("small", 2, 0),
    ("qkv1_1", 2, 2), ("qkv1_0", 2, 1), ("qkv2_1", 2, 1), ("qkv2_0", 1, 3), ("qkv2_0", 2, 0),
    ("qkv0_0", "end", 0), ("qkv1_0", "end", 0), ("qkv2_2", 2, 1), ("qkv2_0", 2, 1), ("qkv2_0", "end", 0),
    ("qkv2_1", 2, 2), ("qkv1_1", 2, 3), ("qkv2_2", 2, 2), ("qkv1_1", "end", 0), ("qkv2_1", 2, 3),
    ("qkv2_2", 2, 3), ("qkv2_1", "end", 0), ("small", 3, 0), ("qkv2_2", "end", 0),
)

GIVEN = (
    "pooled", "seg", "pos", "g1", "g2", "g3", "table", "lanes", "x_h", "q_h", "k_h", "v_h", "att_h",
    "mid_h", "inner_h", "hid_h", "fin_h", "wq_h", "wk_h", "wv_h", "wo_h", "w1_h", "w2_h",
)
MADE = (
    "emb_o", "loss_o", "small_o", "gh_o",
)
HELD = (
    "all_e", "gs", "hid", "ig", "chunk", "wslot", "x", "q", "k", "v", "att", "mid", "fin", "nrm",
    "br2", "br1", "by_offset", "d_all", "dq", "dk", "dv", "sm", "sm_core", "sm_plane", "sm_line",
    "stg",
)
SIGNALS = (
    "load_sem", "ag_s", "ag_r", "sm_s", "sm_r", "tow_s", "tow_r", "end_s", "end_r", "end_l",
    "line_s", "line_r",
)


def backward_kernel(rows_axes, *refs):
    names = [*GIVEN, *MADE, *("res_" + j for j in JOBS), *HELD]
    for j in JOBS:
        names += ["acc_" + j, "r0_" + j, "r1_" + j, "r2_" + j]
    names += SIGNALS
    R = dict(zip(names, refs, strict=True))
    g = lambda n: R[n]
    load_sem = g("load_sem")

    t = lax.axis_index("tower")
    row = lax.axis_index("rows")
    place = {a: ax.place(row) for a, ax in rows_axes.items()}
    nx, ny, nz = (rows_axes[a].size for a in "xyz")
    plane_size = nx * ny
    plane = place["y"] * nx + place["x"]
    sx, sy, sz = (rows_axes[a].stride for a in "xyz")
    row_of = lambda w, z: lax.rem(w, nx) * sx + lax.div(w, nx) * sy + z * sz
    spot = plane * nz + place["z"]
    z_peers = [(t, row_of(plane, lax.rem(place["z"] + m, nz))) for m in range(1, nz)]
    plane_peers = [(t, row_of(lax.rem(plane + m, plane_size), place["z"])) for m in range(1, plane_size)]
    partner = (1 - t, row)

    barrier = pltpu.get_barrier_semaphore()
    for peer in z_peers + plane_peers + [partner]:
        pl.semaphore_signal(barrier, inc=1, device_id=peer, device_id_type=MESH_IDS)

    def load(i, src, dst):
        return pltpu.make_async_copy(src, dst, load_sem.at[i])

    def remote(src, dst, ss, rs, to):
        return pltpu.make_async_remote_copy(
            src_ref=src, dst_ref=dst, send_sem=ss, recv_sem=rs, device_id=to, device_id_type=MESH_IDS
        )

    seq, width = g("x").shape
    heads = g("table").shape[0]
    ff = g("hid").shape[1]
    piece = 512
    chunk_loads = [
        load(c % 2, g("inner_h").at[:, pl.ds(c * piece, piece)], g("chunk").at[c % 2]) for c in range(ff // piece)
    ]
    plain = {
        n: load(2 + i, g(n + "_h"), g(n)) for i, n in enumerate(("mid", "fin", "hid", "x", "q", "k", "v", "att"))
    }
    w2_load = load(10, g("w2_h"), g("wslot"))
    w1_loads = [
        load(11 + c, g("w1_h").at[:, pl.ds(c * width, width)], g("wslot").at[pl.ds(c * width, width)])
        for c in range(ff // width)
    ]
    late_loads = [
        load(15 + i, g(n + "_h"), g("wslot").at[pl.ds(i * width, width)]) for i, n in enumerate(("wq", "wk", "wv", "wo"))
    ]
    gh_store = load(19, g("fin"), g("gh_o"))
    for n in plain:
        plain[n].start()
    w2_load.start()
    chunk_loads[0].start()
    chunk_loads[1].start()

    all_e = g("all_e")
    pooled = g("pooled")[...]
    inverse_pool = lax.rsqrt(jnp.sum(pooled * pooled, axis=-1, keepdims=True) + epsilon)
    own_e = pooled * inverse_pool
    g("emb_o")[...] = own_e
    own_rows = pl.ds(pl.multiple_of(spot * ITEM_ROW, ITEM_ROW), ITEM_ROW)
    bits = lambda n: n.bit_length() - 1
    p = g("pos")[...]
    of_row = p >> bits(ITEM_ROW)
    at = lambda s, n: (of_row >> bits(s)) & (n - 1)
    p = ((at(sy, ny) * nx + at(sx, nx)) * nz + at(sz, nz)) * ITEM_ROW + (p & (ITEM_ROW - 1))
    i8 = lax.broadcasted_iota(jnp.int32, (ITEM_ROW, ITEM_ROW), 0)
    j8 = lax.broadcasted_iota(jnp.int32, (ITEM_ROW, ITEM_ROW), 1)
    diag = jnp.where(i8 == j8, jnp.broadcast_to(p.astype(f32), (ITEM_ROW, ITEM_ROW)), 0.0)
    pos_col = jnp.sum(diag, axis=-1, keepdims=True)
    all_e[t, own_rows, 0:width] = own_e
    all_e[t, own_rows, width : width + UNIT] = jnp.broadcast_to(pos_col, (ITEM_ROW, UNIT))

    pl.semaphore_wait(barrier, len(z_peers) + len(plane_peers) + 1)

    def column_rows(w):
        return pl.ds(pl.multiple_of(w * (nz * ITEM_ROW), ITEM_ROW), nz * ITEM_ROW)

    ag_s, ag_r = g("ag_s"), g("ag_r")
    sent = []
    first = []
    for m, peer in enumerate(z_peers):
        block = all_e.at[t, own_rows]
        first.append(remote(block, block, ag_s.at[m], ag_r.at[m], peer))
        first[-1].start()
    plain["mid"].wait()
    middle = g("mid")[...]
    g("nrm")[...] = ((middle * rms_inverse(middle)) * row_of_gain(g("g2"))).astype(bf16)
    for c in first:
        c.wait_recv()
    sent += first
    n1 = len(z_peers)
    second = []
    mine = all_e.at[t, column_rows(plane)]
    for m, peer in enumerate(plane_peers):
        second.append(remote(mine, mine, ag_s.at[n1 + m], ag_r.at[n1 + m], peer))
        second[-1].start()
    n2 = n1 + len(plane_peers)
    third = [remote(mine, mine, ag_s.at[n2], ag_r.at[n2], partner)]
    third[0].start()
    for m in range(1, plane_size):
        second[m - 1].wait_recv()
        block = all_e.at[t, column_rows(lax.rem(plane + plane_size - m, plane_size))]
        third.append(remote(block, block, ag_s.at[n2 + m], ag_r.at[n2 + m], partner))
        third[-1].start()
    sent += second
    for c in third:
        c.wait_recv()
    sent += third

    queries, docs = all_e[0, :, 0:width], all_e[1, :, 0:width]
    items = queries.shape[0]
    scores = dot_nt(queries, docs, exact) / logit_divisor
    top = jnp.max(scores, axis=1, keepdims=True)
    terms = jnp.exp(scores - top)
    summed = jnp.sum(terms, axis=1, keepdims=True)
    chosen = (
        lax.broadcasted_iota(jnp.int32, (items, items), 1).astype(f32) == all_e[0, :, width : width + 1]
    ).astype(f32)
    losses = top + jnp.log(summed) - jnp.sum(scores * chosen, axis=1, keepdims=True)
    loss_row = jnp.broadcast_to(losses, (items, UNIT)).T[0:8, :]
    pick = (
        lax.broadcasted_iota(jnp.int32, (items, UNIT), 0)
        == lax.broadcasted_iota(jnp.int32, (items, UNIT), 1) + spot * ITEM_ROW + t * (ITEM_ROW // 2)
    ).astype(f32)
    g("loss_o")[...] = dot_nn(loss_row, pick, exact)
    slope = loss_scale * (terms / summed - chosen)

    @pl.when(t == 0)
    def _():
        g("gs")[...] = slope

    @pl.when(t == 1)
    def _():
        g("gs")[...] = slope.T

    embed_grad = dot_nn(g("gs")[own_rows, :], all_e[1 - t, :, 0:width], exact) / logit_divisor
    inner_dot = jnp.sum(own_e * embed_grad, axis=-1, keepdims=True)
    pooled_grad = inverse_pool * (embed_grad - own_e * inner_dot)

    member = (lax.broadcasted_iota(jnp.int32, (ITEM_ROW, seq), 0).astype(f32) == g("seg")[...].astype(f32)).astype(f32)
    counts = jnp.sum(member, axis=-1, keepdims=True)
    three_grad = dot_tn(member, pooled_grad / counts, exact)
    plain["fin"].wait()
    final = g("fin")[...]
    inverse = rms_inverse(final)
    unit = final * inverse
    sm = g("sm")
    sm[...] = jnp.zeros_like(sm)
    sm[0:1, 0:width] = jnp.sum(three_grad * unit, axis=0, keepdims=True)
    u = three_grad * row_of_gain(g("g3"))
    final_grad = inverse * (u - unit * jnp.mean(u * unit, axis=-1, keepdims=True))
    g("fin")[...] = final_grad
    g("br2")[...] = final_grad.astype(bf16)
    plain["hid"].wait()

    stg, tow_s, tow_r = g("stg"), g("tow_s"), g("tow_r")
    line_s, line_r = g("line_s"), g("line_r")
    chunk_rows = width // (nx * ny * nz)
    job_index = {n: i for i, n in enumerate(JOBS)}
    slot_user = {}
    unwaited = []
    sides = {
        "out": ("hid", "br2"), "in": ("nrm", "ig"), "attn": ("att", "br1"),
        "value": ("nrm", "v"), "query": ("nrm", "q"), "key": ("nrm", "k"),
    }

    def spots(path):
        found = {}
        for r in range(nx * ny * nz):
            number = 0
            for a in path:
                number = number * rows_axes[a].size + (r // rows_axes[a].stride) % rows_axes[a].size
            found[r] = number * chunk_rows
        return found

    def product(job, half):
        path, parts = JOBS[job]
        lhs = g(sides[parts[0][0]][0])
        stripes = list(dict.fromkeys((target, block) for target, block, _ in parts))
        right = []
        for target, block in stripes:
            rhs = g(sides[target][1])
            lane = half * (rhs.shape[1] // 2) + block * UNIT
            right.append(rhs[:, pl.ds(pl.multiple_of(lane, UNIT), UNIT)])
        value = dot_tn(lhs[...], jnp.concatenate(right, axis=1) if len(right) > 1 else right[0])
        subs = lhs.shape[1] // width
        for r, at_row in spots(path).items():
            for n, (target, block, sub) in enumerate(parts):
                low = (r * subs + sub) * chunk_rows
                lane = stripes.index((target, block)) * UNIT
                yield n, at_row, value[low : low + chunk_rows, lane : lane + UNIT]

    def tower_copy(job, slot):
        units, j = len(JOBS[job][1]), job_index[job]
        return remote(stg.at[slot, pl.ds(0, units)], g("acc_" + job), tow_s.at[j], tow_r.at[j], partner)

    def send_half(job):
        slot = len(slot_user) % SLOTS
        before = [n for n, s in slot_user.items() if s == slot]
        if before:
            tower_copy(before[-1], slot).wait_send()
            unwaited.remove(before[-1])
        for n, at_row, value in product(job, 1 - t):
            stg[slot, n, at_row : at_row + chunk_rows, :] = value
        tower_copy(job, slot).start()
        slot_user[job] = slot
        unwaited.append(job)

    def geometry(job, k):
        path = JOBS[job][0]
        low, size = 0, width
        for a in path[:k]:
            size = size // rows_axes[a].size
            low = low + place[a] * size
        return low, size // rows_axes[path[k]].size, rows_axes[path[k]], place[path[k]]

    def landing(count, block, side):
        if count == 2:
            return 0
        return block if side == "left" else count

    def line_copy(job, k, i, block):
        low, size, axis, _ = geometry(job, k)
        n, j = axis.size, job_index[job]
        if block > i:
            to, slot = (t, row + axis.stride), (0 if n == 2 else block)
        else:
            to, slot = (t, row - axis.stride), (0 if n == 2 else n if block == i - 1 else block)
        at_row = pl.multiple_of(low + block * size, 8)
        return remote(
            g("acc_" + job).at[:, pl.ds(at_row, size)], g(f"r{k}_{job}").at[slot],
            line_s.at[j, k, block], line_r.at[j, k, slot], to,
        )

    def take(job, k, block, slot):
        low, size, axis, _ = geometry(job, k)
        at_row = pl.multiple_of(low + block * size, 8)
        acc, landed = g("acc_" + job), g(f"r{k}_{job}")
        j = job_index[job]
        remote(landed.at[slot], landed.at[slot], line_s.at[j, k, block], line_r.at[j, k, slot], partner).wait_recv()
        acc[:, pl.ds(at_row, size), :] = acc[:, pl.ds(at_row, size), :] + landed[slot]

    def line_step(job, k, s):
        _, _, axis, my_place = geometry(job, k)
        n = axis.size
        for i in range(n):
            from_left = s == i and i < n - 1
            from_right = s == n - 1 - i and i > 0
            last = s == n - 1
            if not (from_left or from_right or last):
                continue

            @pl.when(my_place == i)
            def _():
                if from_left:
                    for block in range(n - 1, i, -1):
                        if i > 0:
                            take(job, k, block, block)
                        line_copy(job, k, i, block).start()
                if from_right:
                    for block in range(i):
                        if i < n - 1:
                            take(job, k, block, block)
                        line_copy(job, k, i, block).start()
                if last:
                    if n == 2:
                        take(job, k, i, 0)
                    else:
                        if i > 0:
                            take(job, k, i, i)
                        if i < n - 1:
                            take(job, k, i, n)

    def line_drain(job, k):
        _, _, axis, my_place = geometry(job, k)
        for i in range(axis.size):

            @pl.when(my_place == i)
            def _():
                for block in range(axis.size):
                    if block != i:
                        line_copy(job, k, i, block).wait_send()

    def end_copy(job, to_partner):
        low, size, _, my_place = geometry(job, 2)
        at_row = pl.multiple_of(low + my_place * size, 8)
        src = g("acc_" + job).at[:, pl.ds(at_row, size)]
        dst = g("res_" + job).at[t]
        j = job_index[job]
        if to_partner:
            return remote(src, dst, g("end_s").at[j], g("end_r").at[j], partner)
        return pltpu.make_async_copy(src, dst, g("end_l").at[j])

    def take_own(job):
        acc = g("acc_" + job)
        tower_copy(job, 0).wait_recv()
        for n, at_row, value in product(job, t):
            span = slice(at_row, at_row + chunk_rows)
            acc[n, span, :] = acc[n, span, :] + value

    def line_event(job, k, s):
        line_step(job, k, s)
        if s == rows_axes[JOBS[job][0][k]].size - 1:
            if k == 2:
                end_copy(job, True).start()
                end_copy(job, False).start()

    def inner_step(c):
        if c == 0:
            w2_load.wait()
        chunk_loads[c].wait()
        v = g("chunk")[c % 2]
        grad = dot_nt(g("br2")[...], g("wslot")[c * piece : (c + 1) * piece, :])
        tangent = jnp.tanh(gelu_factor * (v + gelu_cubic * (v * v * v)))
        ahead = 0.5 * (1.0 + tangent) + 0.5 * v * (1.0 - tangent * tangent) * gelu_factor * (
            1.0 + 3.0 * gelu_cubic * v * v
        )
        g("ig")[:, c * piece : (c + 1) * piece] = (grad * ahead).astype(bf16)
        if c + 2 < len(chunk_loads):
            chunk_loads[c + 2].start()
        if c == len(chunk_loads) - 1:
            for w in w1_loads:
                w.start()

    def norm_back(grad, values, gain, small_row):
        inverse = rms_inverse(values)
        unit = values * inverse
        total = jnp.sum(grad * unit, axis=0, keepdims=True)
        w = grad * gain
        return inverse * (w - unit * jnp.mean(w * unit, axis=-1, keepdims=True)), total

    tokens = 256

    def two_step():
        for w in w1_loads:
            w.wait()
        gain = row_of_gain(g("g2"))
        for low in range(0, seq, tokens):
            part = slice(low, low + tokens)
            grad = dot_nt(g("ig")[part, 0:width], g("wslot")[0:width, :])
            for c in range(1, ff // width):
                lanes = slice(c * width, (c + 1) * width)
                grad = grad + dot_nt(g("ig")[part, lanes], g("wslot")[lanes, :])
            back, total = norm_back(grad, g("mid")[part, :], gain, 1)
            sm[1:2, 0:width] = sm[1:2, 0:width] + total
            middle_grad = g("fin")[part, :] + back
            g("mid")[part, :] = middle_grad
            g("br1")[part, :] = middle_grad.astype(bf16)
        for w in late_loads:
            w.start()
        plain["att"].wait()

    def attended_step():
        for w in late_loads:
            w.wait()
        g("br2")[...] = dot_nt(g("br1")[...], g("wslot")[3 * width : 4 * width, :]).astype(bf16)
        for n in "qkv":
            plain[n].wait()
        table, by_offset = g("table"), g("by_offset")
        by_offset[0:heads, :] = dot_nn(table[...], g("lanes")[...])
        g("d_all")[...] = jnp.zeros_like(g("d_all"))

    seg_row = g("seg")[...].astype(f32)
    low_half = lax.broadcasted_iota(jnp.int32, (seq, UNIT), 1) < UNIT // 2
    blocks = seq // BLOCK
    turned = [lax.broadcasted_iota(jnp.int32, (BLOCK, BLOCK), n) for n in range(2)]
    upside = (turned[0] + turned[1] == BLOCK - 1).astype(f32)

    def heads_step(pair):
        lanes = slice(pair * UNIT, (pair + 1) * UNIT)
        seg_col = column_of(seg_row)
        dk, dv = g("dk"), g("dv")
        dk[...] = jnp.zeros_like(dk)
        dv[...] = jnp.zeros_like(dv)
        kp, vp = g("k")[:, lanes], g("v")[:, lanes]
        for e in range(2):
            h = 2 * pair + e
            keep = low_half if e == 0 else jnp.logical_not(low_half)
            row_bias = jnp.broadcast_to(g("by_offset")[h : h + 1, :], (BLOCK, 4 * BLOCK))
            bias = pltpu.roll(row_bias, 0, 1, stride=1, stride_axis=0)[:, : 3 * BLOCK]
            columns = [jnp.zeros((BLOCK, BLOCK), f32) for _ in range(3)]
            for b in range(blocks):
                lo, hi = key_range(b, blocks)
                mine = slice(b * BLOCK, (b + 1) * BLOCK)
                first = lo - (b - 1) * BLOCK
                qb = g("q")[mine, lanes]
                ob = g("br2")[mine, lanes]
                qe = jnp.where(keep[mine], qb, jnp.zeros_like(qb))
                oe = jnp.where(keep[mine], ob, jnp.zeros_like(ob))
                same = seg_col[mine] == seg_row[:, lo:hi]
                s = dot_nt(qe, kp[lo:hi]) + bias[:, first : first + hi - lo]
                s = jnp.where(same, s, far_below)
                terms = jnp.exp(s - jnp.max(s, axis=-1, keepdims=True))
                probs = terms * (1.0 / jnp.sum(terms, axis=-1, keepdims=True))
                pg = dot_nt(oe, vp[lo:hi])
                ds = probs * (pg - jnp.sum(probs * pg, axis=-1, keepdims=True))
                for n in range((hi - lo) // BLOCK):
                    m = first // BLOCK + n
                    columns[m] = columns[m] + ds[:, n * BLOCK : (n + 1) * BLOCK]
                rounded = ds.astype(bf16)
                dq = dot_nn(rounded, kp[lo:hi])
                dk[lo:hi, :] = dk[lo:hi, :] + dot_tn(rounded, qe)
                dv[lo:hi, :] = dv[lo:hi, :] + dot_tn(probs.astype(bf16), oe)
                g("dq")[mine, :] = dq if e == 0 else jnp.where(low_half[mine], g("dq")[mine, :], dq)
            wide = jnp.concatenate(columns + [jnp.zeros((BLOCK, BLOCK), f32)], axis=1)
            skewed = pltpu.roll(
                dot_nn(upside, wide, exact), 3 * BLOCK + 1, 1, stride=1, stride_axis=0
            )
            g("d_all")[h : h + 1, :] = jnp.sum(skewed, axis=0, keepdims=True)
        g("q")[:, lanes] = g("dq")[...].astype(bf16)
        g("k")[:, lanes] = dk[...].astype(bf16)
        g("v")[:, lanes] = dv[...].astype(bf16)

    def normed_step():
        plain["x"].wait()
        x = g("x")[...].astype(f32)
        g("nrm")[...] = ((x * rms_inverse(x)) * row_of_gain(g("g1"))).astype(bf16)

    def one_step():
        gain = row_of_gain(g("g1"))
        for low in range(0, seq, tokens):
            part = slice(low, low + tokens)
            grad = dot_nt(g("q")[part, :], g("wslot")[0:width, :])
            grad = grad + dot_nt(g("k")[part, :], g("wslot")[width : 2 * width, :])
            grad = grad + dot_nt(g("v")[part, :], g("wslot")[2 * width : 3 * width, :])
            back, total = norm_back(grad, g("x")[part, :].astype(f32), gain, 2)
            sm[2:3, 0:width] = sm[2:3, 0:width] + total
            g("fin")[part, :] = g("mid")[part, :] + back
        gh_store.start()

    sm_core, sm_plane, sm_line = g("sm_core"), g("sm_plane"), g("sm_line")
    sm_s, sm_r = g("sm_s"), g("sm_r")
    small_sent = []
    small_first = [remote(sm, sm_core, sm_s.at[0], sm_r.at[0], partner)]
    small_second = [
        remote(sm_plane.at[plane], sm_plane.at[plane], sm_s.at[1 + m], sm_r.at[1 + m], peer)
        for m, peer in enumerate(plane_peers)
    ]
    base = 1 + len(plane_peers)
    small_third = [
        remote(sm_line.at[place["z"]], sm_line.at[place["z"]], sm_s.at[base + m], sm_r.at[base + m], peer)
        for m, peer in enumerate(z_peers)
    ]

    def small_step(s):
        if s == 0:
            table_grad = dot_nt(g("d_all")[...], g("lanes")[...].astype(f32), exact)
            for n in range(2):
                sm[:, width + n * UNIT : width + n * UNIT + BUCKETS] = table_grad[8 * n : 8 * n + 8, :]
            small_first[0].start()
        elif s == 1:
            small_first[0].wait()
            sm_plane[plane] = sm[...] + sm_core[...]
            for c in small_second:
                c.start()
        elif s == 2:
            for c in small_second:
                c.wait()
            total = sm_plane[0]
            for w in range(1, plane_size):
                total = total + sm_plane[w]
            sm_line[place["z"]] = total
            for c in small_third:
                c.start()
        else:
            for c in small_third:
                c.wait()
            total = sm_line[0]
            for w in range(1, nz):
                total = total + sm_line[w]
            g("small_o")[...] = total

    for step in STEPS:
        if step[0] == "send":
            send_half(step[1])
        elif step[0] == "inner":
            inner_step(step[1])
        elif step[0] == "two":
            two_step()
        elif step[0] == "attended":
            attended_step()
        elif step[0] == "heads":
            heads_step(step[1])
        elif step[0] == "normed":
            normed_step()
        elif step[0] == "one":
            one_step()
        elif step[0] == "small":
            small_step(step[1])
        elif step[1] == "own":
            take_own(step[0])
        elif step[1] == "end":
            end_copy(step[0], True).wait_recv()
            end_copy(step[0], False).wait()
        else:
            line_event(*step)
    for c in sent:
        c.wait_send()
    for job in list(unwaited):
        tower_copy(job, slot_user[job]).wait_send()
    for job in JOBS:
        for k in range(3):
            line_drain(job, k)
        end_copy(job, True).wait_send()
    gh_store.wait()


def backward_call(axes, args):
    seq, width = args[8].shape
    ff = args[15].shape[1]
    nx, ny, nz = (axes[a].size for a in "xyz")
    rows = nx * ny * nz
    chunk_rows = width // rows
    s = jax.ShapeDtypeStruct
    vm, hbm = pl.BlockSpec(memory_space=VMEM), pl.BlockSpec(memory_space=pl.ANY)
    small = (8, width + 2 * UNIT)
    outs = [s((ITEM_ROW, width), f32), s((8, UNIT), f32), s(small, f32), s((seq, width), f32)]
    outs += [s((2, len(parts), chunk_rows, UNIT), f32) for _, parts in JOBS.values()]
    scratch = [
        VMEM((2, rows * ITEM_ROW, width + UNIT), f32), VMEM((rows * ITEM_ROW, rows * ITEM_ROW), f32),
        VMEM((seq, ff), bf16), VMEM((seq, ff), bf16), VMEM((2, seq, 512), f32), VMEM((ff, width), bf16),
    ]
    scratch += [VMEM((seq, width), bf16)] * 5 + [VMEM((seq, width), f32)] * 2 + [VMEM((seq, width), bf16)] * 3
    scratch += [
        VMEM((16, 4 * BLOCK), f32), VMEM((16, 4 * BLOCK), f32),
        VMEM((seq, UNIT), f32), VMEM((seq, UNIT), f32), VMEM((seq, UNIT), f32),
        VMEM(small, f32), VMEM(small, f32), VMEM((nx * ny, *small), f32), VMEM((nz, *small), f32),
        VMEM((SLOTS, 4, width, UNIT), f32),
    ]
    for path, parts in JOBS.values():
        units = len(parts)
        scratch.append(VMEM((units, width, UNIT), f32))
        size = width
        for a in path:
            n = axes[a].size
            size = size // n
            scratch.append(VMEM((1 if n == 2 else n + 1, units, size, UNIT), f32))
    dma = pltpu.SemaphoreType.DMA
    jobs, most = len(JOBS), max(nx, ny, nz)
    gathers = nz - 1 + nx * ny - 1 + nx * ny
    scratch += [
        dma((20,)), dma((gathers,)), dma((gathers,)), dma((nz + nx * ny,)), dma((nz + nx * ny,)),
        dma((jobs,)), dma((jobs,)), dma((jobs,)), dma((jobs,)), dma((jobs,)),
        dma((jobs, 3, most)), dma((jobs, 3, most + 1)),
    ]
    return pl.pallas_call(
        functools.partial(backward_kernel, axes),
        name="layer_backward",
        out_shape=outs,
        in_specs=[vm] * 8 + [hbm] * 15,
        out_specs=[vm] * 3 + [hbm] * (1 + len(JOBS)),
        scratch_shapes=scratch,
        compiler_params=pltpu.CompilerParams(
            collective_id=0, has_side_effects=True, vmem_limit_bytes=VMEM_LIMIT
        ),
    )(*args)


def place_kernel(emb, loss, small, gh, *refs):
    res = dict(zip(JOBS, refs[: len(JOBS)], strict=True))
    (
        emb_o, loss_o, gh_o, attn_gain_o, query_o, key_o, value_o, attn_o, table_o, ffn_gain_o, in_o, out_o, final_gain_o,
    ) = refs[len(JOBS) :]
    row = lax.axis_index("rows")
    targets = {"out": out_o, "in": in_o, "attn": attn_o, "value": value_o, "query": query_o, "key": key_o}
    emb_o[0] = emb[...]
    gh_o[0, 0] = gh[...]
    for job, (_, parts) in JOBS.items():
        for n, (target, block, sub) in enumerate(parts):
            out, height = targets[target], res[job].shape[2]
            for t in range(2):
                low = t * (out.shape[1] // 2) + block * UNIT
                out[sub * height : (sub + 1) * height, low : low + UNIT] = res[job][t, n]
    loss_o[0] = loss[0:1, 0 : loss_o.shape[2]]
    width = gh.shape[1]
    share = attn_gain_o.shape[0]
    pick = (
        lax.broadcasted_iota(jnp.int32, (width, UNIT), 0)
        == lax.broadcasted_iota(jnp.int32, (width, UNIT), 1) + row * share
    ).astype(f32)
    gains = dot_nn(small[:, 0:width], pick, exact)
    for n, out in enumerate((final_gain_o, ffn_gain_o, attn_gain_o)):
        out[...] = gains[n, 0:share]
    heads = table_o.shape[0]
    for low in range(0, heads, 8):
        lane = width + low // 8 * UNIT
        high = min(low + 8, heads)
        table_o[low:high, :] = small[0 : high - low, lane : lane + BUCKETS]


def place_call(axes, heads, emb, loss, small, gh, res):
    seq, width = gh.shape
    ff = 4 * width
    rows = math.prod(a.size for a in axes.values())
    share = width // rows
    s = jax.ShapeDtypeStruct
    vm = pl.BlockSpec(memory_space=VMEM)
    weight = s((share, width), f32)
    outs = [
        s((1, *emb.shape), f32), s((1, 1, ITEM_ROW // 2), f32), s((1, 1, seq, width), f32), s((share,), f32),
        weight, weight, weight, weight, s((heads, BUCKETS), f32), s((share,), f32),
        s((share, ff), f32), s((ff // rows, width), f32), s((share,), f32),
    ]
    return pl.pallas_call(
        place_kernel,
        name="place_outputs",
        out_shape=outs,
        in_specs=[vm] * (4 + len(JOBS)),
        out_specs=[vm] * len(outs),
        compiler_params=pltpu.CompilerParams(vmem_limit_bytes=VMEM_LIMIT),
    )(emb, loss, small, gh, *res)


def rows_axes(mesh):
    rows = mesh.shape["rows"]
    line = mesh.devices.reshape(-1, rows)[0]
    places = [tuple(getattr(d, "coords", (i % 2, i // 2 % 2, i // 4))) for i, d in enumerate(line)]
    axes = {}
    for n, name in enumerate("xyz"):
        values = sorted({p[n] for p in places})
        stride = next((i for i, p in enumerate(places) if p[n] != places[0][n]), 1)
        axes[name] = Axis(len(values), stride)
    return axes


def fused(axes, hidden_in, segment_ids, positives, attn_gain, w_query, w_key, w_value, w_attn_out, rel_table, ffn_gain, w_ffn_in, w_ffn_out, final_gain):
    seq, width = hidden_in.shape[2:]
    x = hidden_in.reshape(seq, width)
    seg = segment_ids.reshape(1, seq)
    pos = positives.reshape(1, -1)
    gains = (attn_gain, ffn_gain, final_gain)
    lanes = jnp.asarray(lane_buckets(), bf16)
    table = rel_table.T
    weights = (w_query, w_key, w_value, w_attn_out, w_ffn_in, w_ffn_out)
    q, k, v, att, mid, inner, hid, fin, pooled = forward_call(x, seg, *gains, table, lanes, *weights)
    emb, loss, small, gh, *res = backward_call(
        axes, (pooled, seg, pos, *gains, table, lanes, x, q, k, v, att, mid, inner, hid, fin, *weights)
    )
    outs = list(place_call(axes, rel_table.shape[1], emb, loss, small, gh, res))
    outs[8] = outs[8].T
    return tuple(outs)


def from_partner(block, axis, bit):
    count = lax.axis_size(axis)
    route = []
    for low in range(count):
        high = low | 1 << bit
        if high != low and high < count:
            route += [(low, high), (high, low)]
    return lax.ppermute(block, axis, route)


def bucket_onehot(seq_len, bucket_count, max_distance):
    half_count = bucket_count // 2
    exact_count = half_count // 2
    log_steps = half_count - exact_count
    bounds = []
    for section_index in range(1, log_steps):
        target = exact_count ** (log_steps - section_index) * max_distance**section_index
        lowest = exact_count
        while lowest**log_steps < target:
            lowest = lowest + 1
        bounds.append(lowest)
    onehot = np.zeros((2 * seq_len - 1, bucket_count), np.float32)
    for offset in range(2 * seq_len - 1):
        relative = offset - (seq_len - 1)
        distance = abs(relative)
        bucket = half_count if relative > 0 else 0
        if distance < exact_count:
            bucket = bucket + distance
        else:
            bucket = (
                bucket
                + exact_count
                + len([boundary for boundary in bounds if distance >= boundary])
            )
        onehot[offset, bucket] = 1.0
    return onehot


def matmul(left_side, right_side):
    return jnp.dot(left_side, right_side, preferred_element_type=jnp.float32)


def contract_rows(left_side, right_side):
    return lax.dot_general(
        left_side, right_side, (((0,), (0,)), ((), ())), preferred_element_type=jnp.float32
    )


def contract_cols(left_side, right_side):
    return lax.dot_general(
        left_side, right_side, (((1,), (1,)), ((), ())), preferred_element_type=jnp.float32
    )


def gelu_slope(values):
    factor = math.sqrt(2.0 / math.pi)
    tangent = jnp.tanh(factor * (values + gelu_cubic * values * values * values))
    return 0.5 * (1.0 + tangent) + 0.5 * values * (1.0 - tangent * tangent) * factor * (
        1.0 + 3.0 * gelu_cubic * values * values
    )


def rms_parts(values):
    inverse = lax.rsqrt(jnp.mean(values * values, axis=-1, keepdims=True) + epsilon)
    return (values * inverse, inverse)


def rms_back(unit_grad, unit_values, inverse):
    return inverse * (
        unit_grad - unit_values * jnp.mean(unit_grad * unit_values, axis=-1, keepdims=True)
    )


def position_bias(rel_table, onehot, seq_len):
    head_count = rel_table.shape[1]
    by_offset = lax.dot_general(
        rel_table.astype(jnp.float32), onehot, (((0,), (1,)), ((), ())), precision=exact
    )
    rolled = jnp.concatenate([by_offset[:, seq_len - 1 :], by_offset[:, : seq_len - 1]], axis=1)
    repeated = jnp.tile(rolled, (1, seq_len))[:, : seq_len * (2 * seq_len - 2)]
    return repeated.reshape(head_count, seq_len, 2 * seq_len - 2)[:, :, :seq_len]


def diagonal_sums(matrix, seq_len):
    head_count = matrix.shape[0]
    flipped = matrix[:, :, ::-1]
    padded = jnp.pad(flipped, ((0, 0), (0, 0), (0, seq_len)))
    skewed = padded.reshape(head_count, 2 * seq_len * seq_len)[:, : seq_len * (2 * seq_len - 1)]
    skewed = skewed.reshape(head_count, seq_len, 2 * seq_len - 1)
    return jnp.sum(skewed, axis=1)[:, ::-1]


def on_device(
    hidden_in,
    segment_ids,
    positives,
    attn_gain,
    w_query,
    w_key,
    w_value,
    w_attn_out,
    rel_table,
    ffn_gain,
    w_ffn_in,
    w_ffn_out,
    final_gain,
):
    row_count = hidden_in.shape[1]
    seq_len = hidden_in.shape[2]
    model_width = hidden_in.shape[3]
    head_count = rel_table.shape[1]
    head_width = model_width // head_count
    token_count = row_count * seq_len
    tokens = hidden_in.reshape(token_count, model_width).astype(jnp.float32)
    segments = segment_ids.reshape(row_count, seq_len)
    gain_one = attn_gain.astype(jnp.float32)
    gain_two = ffn_gain.astype(jnp.float32)
    gain_three = final_gain.astype(jnp.float32)
    onehot = jnp.asarray(bucket_onehot(seq_len, BUCKETS, MAX_DIST))
    unit_one, inverse_one = rms_parts(tokens)
    normed_one = (unit_one * gain_one).astype(jnp.bfloat16)
    query_proj = matmul(normed_one, w_query).astype(jnp.bfloat16)
    key_proj = matmul(normed_one, w_key).astype(jnp.bfloat16)
    value_proj = matmul(normed_one, w_value).astype(jnp.bfloat16)
    bias_full = position_bias(rel_table, onehot, seq_len)

    def split_heads(values):
        return values.reshape(row_count, seq_len, head_count, head_width)

    def row_scores(row_query, row_key, row_seg):
        same_item = row_seg[:, None] == row_seg[None, :]
        similarity_table = jnp.einsum(
            "shd,thd->hst", row_query, row_key, preferred_element_type=jnp.float32
        )
        return jnp.where(same_item[None], similarity_table + bias_full, far_below)

    def forward_row(packed):
        row_query, row_key, row_value, row_seg = packed
        masked_scores = row_scores(row_query, row_key, row_seg)
        row_peak = jnp.max(masked_scores, axis=-1, keepdims=True)
        exp_terms = jnp.exp(masked_scores - row_peak)
        summed = jnp.sum(exp_terms, axis=-1, keepdims=True)
        attn_probs = (exp_terms / summed).astype(jnp.bfloat16)
        combined_attention_output = jnp.einsum(
            "hst,thd->shd", attn_probs, row_value, preferred_element_type=jnp.float32
        )
        return (
            combined_attention_output.astype(jnp.bfloat16),
            (row_peak + jnp.log(summed))[:, :, 0],
        )

    attended, log_norms = lax.map(
        forward_row,
        (split_heads(query_proj), split_heads(key_proj), split_heads(value_proj), segments),
    )
    attended = attended.reshape(token_count, model_width)
    middle = tokens + matmul(attended, w_attn_out)
    unit_two, inverse_two = rms_parts(middle)
    normed_two = (unit_two * gain_two).astype(jnp.bfloat16)
    inner = matmul(normed_two, w_ffn_in)
    hidden = jax.nn.gelu(inner, approximate=True).astype(jnp.bfloat16)
    final_sum = middle + matmul(hidden, w_ffn_out)
    unit_three, inverse_three = rms_parts(final_sum)
    normed_three = unit_three * gain_three
    member = (segments[:, None, :] == jnp.arange(ITEM_ROW, dtype=jnp.int32)[None, :, None]).astype(
        jnp.float32
    )
    counts = jnp.sum(member, axis=-1, keepdims=True)
    pooled = (
        jnp.einsum(
            "ris,rsd->rid",
            member,
            normed_three.reshape(row_count, seq_len, model_width),
            precision=exact,
        )
        / counts
    )
    item_count = row_count * ITEM_ROW
    pooled = pooled.reshape(item_count, model_width)
    inverse_pool = lax.rsqrt(jnp.sum(pooled * pooled, axis=-1, keepdims=True) + epsilon)
    encoded_vector_list = pooled * inverse_pool
    half_items = item_count // 2
    tower_index = lax.axis_index("tower")
    rows_size = lax.axis_size("rows")
    is_query = tower_index == 0
    first_half = encoded_vector_list[:half_items]
    second_half = encoded_vector_list[half_items:]
    outgoing = jnp.where(is_query, second_half, first_half)
    incoming = from_partner(outgoing, "tower", 0)
    my_queries = jnp.where(is_query, first_half, incoming)
    local_passages = jnp.where(is_query, incoming, second_half)
    passage_list = lax.all_gather(local_passages, ("tower", "rows"), axis=0, tiled=True)
    total_items = passage_list.shape[0]
    similarity_table = (
        lax.dot_general(
            my_queries, passage_list, (((1,), (1,)), ((), ())), precision=exact
        )
        / logit_divisor
    )
    my_positive = lax.dynamic_slice_in_dim(positives, tower_index * half_items, half_items)
    column = (
        my_positive // half_items % 2 * (rows_size * half_items)
        + my_positive // item_count * half_items
        + my_positive % half_items
    )
    chosen_mask = (jnp.arange(total_items, dtype=jnp.int32)[None, :] == column[:, None]).astype(
        jnp.float32
    )
    row_peak = jnp.max(similarity_table, axis=1, keepdims=True)
    exp_terms = jnp.exp(similarity_table - row_peak)
    summed = jnp.sum(exp_terms, axis=1, keepdims=True)
    losses = (
        row_peak[:, 0] + jnp.log(summed[:, 0]) - jnp.sum(similarity_table * chosen_mask, axis=1)
    )
    similarity_derivative = loss_scale * (exp_terms / summed - chosen_mask)
    query_embedding_gradient = (
        jnp.dot(similarity_derivative, passage_list, precision=exact) / logit_divisor
    )
    doc_embed_grad = lax.psum_scatter(
        lax.dot_general(
            similarity_derivative, my_queries, (((0,), (0,)), ((), ())), precision=exact
        )
        / logit_divisor,
        ("tower", "rows"),
        scatter_dimension=0,
        tiled=True,
    )
    sendback = jnp.where(is_query, doc_embed_grad, query_embedding_gradient)
    received = from_partner(sendback, "tower", 0)
    embed_grad = jnp.where(
        is_query,
        jnp.concatenate([query_embedding_gradient, received], axis=0),
        jnp.concatenate([received, doc_embed_grad], axis=0),
    )
    inner_dot = jnp.sum(encoded_vector_list * embed_grad, axis=-1, keepdims=True)
    pooled_grad = inverse_pool * (embed_grad - encoded_vector_list * inner_dot)
    spread = member / counts
    three_grad = jnp.einsum(
        "ris,rid->rsd",
        spread,
        pooled_grad.reshape(row_count, ITEM_ROW, model_width),
        precision=exact,
    )
    three_grad = three_grad.reshape(token_count, model_width)
    final_gain_grad = jnp.sum(three_grad * unit_three, axis=0)
    final_grad = rms_back(three_grad * gain_three, unit_three, inverse_three)
    branch_two_grad = final_grad.astype(jnp.bfloat16)
    ffn_out_grad = contract_rows(hidden, branch_two_grad)
    inner_grad = (contract_cols(branch_two_grad, w_ffn_out) * gelu_slope(inner)).astype(
        jnp.bfloat16
    )
    ffn_in_grad = contract_rows(normed_two, inner_grad)
    two_grad = contract_cols(inner_grad, w_ffn_in)
    ffn_gain_grad = jnp.sum(two_grad * unit_two, axis=0)
    middle_grad = final_grad + rms_back(two_grad * gain_two, unit_two, inverse_two)
    branch_one_grad = middle_grad.astype(jnp.bfloat16)
    attn_out_grad = contract_rows(attended, branch_one_grad)
    attended_grad = contract_cols(branch_one_grad, w_attn_out).astype(jnp.bfloat16)

    def backward_row(bias_total, packed):
        row_query, row_key, row_value, row_seg, row_norm, row_grad = packed
        masked_scores = row_scores(row_query, row_key, row_seg)
        attn_probs = jnp.exp(masked_scores - row_norm[:, :, None])
        probs_grad = jnp.einsum(
            "shd,thd->hst", row_grad, row_value, preferred_element_type=jnp.float32
        )
        value_grad = jnp.einsum(
            "hst,shd->thd",
            attn_probs.astype(jnp.bfloat16),
            row_grad,
            preferred_element_type=jnp.float32,
        )
        score_part_grad = attn_probs * (
            probs_grad - jnp.sum(attn_probs * probs_grad, axis=-1, keepdims=True)
        )
        rounded = score_part_grad.astype(jnp.bfloat16)
        query_grad = jnp.einsum(
            "hst,thd->shd", rounded, row_key, preferred_element_type=jnp.float32
        )
        key_grad = jnp.einsum(
            "hst,shd->thd", rounded, row_query, preferred_element_type=jnp.float32
        )
        return (
            bias_total + score_part_grad,
            (
                query_grad.astype(jnp.bfloat16),
                key_grad.astype(jnp.bfloat16),
                value_grad.astype(jnp.bfloat16),
            ),
        )

    bias_total, head_grads = lax.scan(
        backward_row,
        jnp.zeros((head_count, seq_len, seq_len), jnp.float32),
        (
            split_heads(query_proj),
            split_heads(key_proj),
            split_heads(value_proj),
            segments,
            log_norms,
            split_heads(attended_grad),
        ),
    )
    query_grad = head_grads[0].reshape(token_count, model_width)
    key_grad = head_grads[1].reshape(token_count, model_width)
    value_grad = head_grads[2].reshape(token_count, model_width)
    table_local = jnp.einsum(
        "ib,hi->bh", onehot, diagonal_sums(bias_total, seq_len), precision=exact
    )
    query_w_grad = contract_rows(normed_one, query_grad)
    key_w_grad = contract_rows(normed_one, key_grad)
    value_w_grad = contract_rows(normed_one, value_grad)
    one_grad = (
        contract_cols(query_grad, w_query)
        + contract_cols(key_grad, w_key)
        + contract_cols(value_grad, w_value)
    )
    attn_gain_grad = jnp.sum(one_grad * unit_one, axis=0)
    input_grad = middle_grad + rms_back(one_grad * gain_one, unit_one, inverse_one)
    table_grad = lax.psum(table_local, ("tower", "rows"))
    shares = (
        lax.psum_scatter(attn_gain_grad, "rows", scatter_dimension=0, tiled=True),
        lax.psum_scatter(query_w_grad, "rows", scatter_dimension=0, tiled=True),
        lax.psum_scatter(key_w_grad, "rows", scatter_dimension=0, tiled=True),
        lax.psum_scatter(value_w_grad, "rows", scatter_dimension=0, tiled=True),
        lax.psum_scatter(attn_out_grad, "rows", scatter_dimension=0, tiled=True),
        lax.psum_scatter(ffn_gain_grad, "rows", scatter_dimension=0, tiled=True),
        lax.psum_scatter(ffn_in_grad, "rows", scatter_dimension=0, tiled=True),
        lax.psum_scatter(ffn_out_grad, "rows", scatter_dimension=0, tiled=True),
        lax.psum_scatter(final_gain_grad, "rows", scatter_dimension=0, tiled=True),
    )
    summed_grads = lax.psum(
        (
            shares[0],
            shares[1],
            shares[2],
            shares[3],
            shares[4],
            shares[5],
            shares[6],
            shares[7],
            shares[8],
        ),
        "tower",
    )
    return (
        encoded_vector_list[None],
        losses.reshape(1, 1, half_items),
        input_grad.reshape(hidden_in.shape),
        summed_grads[0],
        summed_grads[1],
        summed_grads[2],
        summed_grads[3],
        summed_grads[4],
        table_grad,
        summed_grads[5],
        summed_grads[6],
        summed_grads[7],
        summed_grads[8],
    )


def solution(mesh):
    in_specs = (
        P("tower", "rows", None, None),
        P("tower", "rows", None),
        P("rows"),
        P(),
        P(),
        P(),
        P(),
        P(),
        P(),
        P(),
        P(),
        P(),
        P(),
    )
    out_specs = (
        P("tower", "rows", None),
        P("rows", "tower", None),
        P("tower", "rows", None, None),
        P("rows"),
        P("rows", None),
        P("rows", None),
        P("rows", None),
        P("rows", None),
        P(),
        P("rows"),
        P("rows", None),
        P("rows", None),
        P("rows"),
    )
    axes = rows_axes(mesh)
    sized = mesh.shape["tower"] == 2 and tuple(axes[a].size for a in "xyz") == STEPS_SIZES
    body = functools.partial(fused, axes) if sized else on_device
    return jax.shard_map(
        body, mesh=mesh, in_specs=in_specs, out_specs=out_specs, check_vma=False
    )
```

```python
import functools
import math

import jax
import jax.numpy as jnp
import numpy as np
from jax import lax
from jax.experimental import pallas as pl
from jax.experimental.pallas import tpu as pltpu
from jax.sharding import PartitionSpec as P

BUCKETS = 32
MAX_DIST = 128
ITEM_ROW = 8
BLOCK = 128

epsilon = 1e-06
logit_divisor = 0.01
loss_scale = 16.0
far_below = -1000000000.0
exact = lax.Precision.HIGHEST
gelu_cubic = 0.044715
gelu_factor = math.sqrt(2.0 / math.pi)
f32 = jnp.float32
bf16 = jnp.bfloat16
VMEM = pltpu.VMEM
VMEM_LIMIT = 62 * 2**20


def dot_nn(a, b, precision=None):
    return lax.dot_general(
        a, b, (((1,), (0,)), ((), ())), precision=precision, preferred_element_type=f32
    )


def dot_nt(a, b, precision=None):
    return lax.dot_general(
        a, b, (((1,), (1,)), ((), ())), precision=precision, preferred_element_type=f32
    )


def dot_tn(a, b, precision=None):
    return lax.dot_general(
        a, b, (((0,), (0,)), ((), ())), precision=precision, preferred_element_type=f32
    )


def bucket_of(relative, bucket_count, max_distance):
    half_count = bucket_count // 2
    exact_count = half_count // 2
    log_steps = half_count - exact_count
    bounds = []
    for section_index in range(1, log_steps):
        target = exact_count ** (log_steps - section_index) * max_distance**section_index
        lowest = exact_count
        while lowest**log_steps < target:
            lowest = lowest + 1
        bounds.append(lowest)
    distance = abs(relative)
    bucket = half_count if relative > 0 else 0
    if distance < exact_count:
        return bucket + distance
    return bucket + exact_count + len([b for b in bounds if distance >= b])


def lane_buckets():
    width = 4 * BLOCK
    onehot = np.zeros((BUCKETS, width), np.float32)
    for m in range(width):
        relative = (m if m < 3 * BLOCK else m - width) - BLOCK
        onehot[bucket_of(relative, BUCKETS, MAX_DIST), m] = 1.0
    return onehot


def row_of_gain(ref):
    return ref[...].astype(f32).reshape(1, ref.shape[0])


def rms_inverse(values):
    return lax.rsqrt(jnp.mean(values * values, axis=-1, keepdims=True) + epsilon)


def column_of(row):
    return jnp.broadcast_to(row, (8, row.shape[1])).T[:, 0:1]


def key_range(block, blocks):
    return max(block - 1, 0) * BLOCK, min(block + 2, blocks) * BLOCK


MESH_IDS = pl.DeviceIdType.MESH
OUT, IN, ATTN, VALUE, QUERY, KEY = range(6)
OWN, END, SEND = 3, 4, 5
INNER, TWO, ATTENDED, HEADS, NORMED, ONE, SMALL = range(7)


class Axis:

    def __init__(self, size, stride):
        self.size, self.stride = size, stride

    def place(self, row):
        return lax.rem(lax.div(row, self.stride), self.size)


UNIT = 128
SLOTS = 3
JOBS = (
    ((2, 0, 1), ((OUT, 0, 0), (OUT, 0, 1),)),
    ((0, 2, 1), ((OUT, 0, 2), (OUT, 0, 3),)),
    ((0, 2, 1), ((OUT, 1, 0), (OUT, 1, 1),)),
    ((0, 1, 2), ((OUT, 1, 2), (OUT, 1, 3),)),
    ((1, 2, 0), ((OUT, 2, 0), (OUT, 2, 1), (OUT, 2, 2), (OUT, 2, 3),)),
    ((1, 0, 2), ((IN, 0, 0), (IN, 1, 0), (IN, 2, 0), (IN, 3, 0),)),
    ((0, 1, 2), ((IN, 4, 0), (IN, 5, 0), (IN, 6, 0), (IN, 7, 0),)),
    ((2, 0, 1), ((IN, 8, 0), (IN, 9, 0), (IN, 10, 0), (IN, 11, 0),)),
    ((0, 1, 2), ((ATTN, 0, 0), (ATTN, 1, 0), (ATTN, 2, 0),)),
    ((1, 0, 2), ((VALUE, 0, 0), (QUERY, 0, 0), (KEY, 0, 0),)),
    ((0, 1, 2), ((VALUE, 1, 0), (QUERY, 1, 0), (KEY, 1, 0),)),
    ((1, 2, 0), ((VALUE, 2, 0),)),
    ((1, 2, 0), ((QUERY, 2, 0),)),
    ((0, 1, 2), ((KEY, 2, 0),)),
)
STEPS_SIZES = (2, 2, 4)
STEPS = (
    (0, SEND, 0), (2, SEND, 0), (0, OWN, 0), (0, 0, 0), (2, OWN, 0), (2, 0, 0), (4, SEND, 0), (1, SEND, 0),
    (3, SEND, 0), (4, OWN, 0), (4, 0, 0), (1, OWN, 0), (1, 0, 0), (3, OWN, 0), (3, 0, 0), (0, 0, 1),
    (-1, INNER, 0), (2, 0, 1), (2, 1, 0), (-1, INNER, 1), (-1, INNER, 2), (-1, INNER, 3), (0, 0, 2),
    (-1, INNER, 4), (-1, INNER, 5), (2, 1, 1), (5, SEND, 0), (1, 0, 1), (1, 1, 0), (6, SEND, 0), (0, 0, 3),
    (0, 1, 0), (2, 1, 2), (5, OWN, 0), (5, 0, 0), (7, SEND, 0), (4, 0, 1), (4, 1, 0), (1, 1, 1), (6, OWN, 0),
    (6, 0, 0), (3, 0, 1), (3, 1, 0), (7, OWN, 0), (7, 0, 0), (0, 1, 1), (0, 2, 0), (1, 1, 2), (2, 1, 3),
    (2, 2, 0), (-1, TWO, 0), (1, 1, 3), (1, 2, 0), (4, 1, 1), (8, SEND, 0), (-1, NORMED, 0),
    (-1, ATTENDED, 0), (-1, HEADS, 0), (5, 0, 1), (5, 1, 0), (8, OWN, 0), (8, 0, 0), (4, 1, 2), (3, 1, 1),
    (3, 2, 0), (-1, HEADS, 3), (1, 2, 1), (0, 2, 1), (6, 0, 1), (6, 1, 0), (2, 2, 1), (1, END, 0),
    (0, END, 0), (9, SEND, 0), (4, 1, 3), (4, 2, 0), (2, END, 0), (-1, HEADS, 1), (9, OWN, 0), (9, 0, 0),
    (5, 1, 1), (5, 2, 0), (7, 0, 1), (-1, HEADS, 4), (6, 1, 1), (6, 2, 0), (10, SEND, 0), (-1, HEADS, 2),
    (10, OWN, 0), (10, 0, 0), (-1, HEADS, 5), (3, 2, 1), (8, 0, 1), (8, 1, 0), (7, 0, 2), (11, SEND, 0),
    (4, 2, 1), (12, SEND, 0), (13, SEND, 0), (11, OWN, 0), (11, 0, 0), (9, 0, 1), (9, 1, 0), (12, OWN, 0),
    (12, 0, 0), (13, OWN, 0), (13, 0, 0), (5, 2, 1), (4, END, 0), (-1, ONE, 0), (3, 2, 2), (-1, SMALL, 0),
    (8, 1, 1), (8, 2, 0), (6, 2, 1), (-1, SMALL, 1), (5, 2, 2), (3, 2, 3), (7, 0, 3), (7, 1, 0), (3, END, 0),
    (10, 0, 1), (10, 1, 0), (11, 0, 1), (11, 1, 0), (6, 2, 2), (8, 2, 1), (5, 2, 3), (5, END, 0), (6, 2, 3),
    (8, 2, 2), (12, 0, 1), (12, 1, 0), (11, 1, 1), (6, END, 0), (9, 1, 1), (9, 2, 0), (8, 2, 3), (11, 1, 2),
    (12, 1, 1), (8, END, 0), (11, 1, 3), (11, 2, 0), (12, 1, 2), (13, 0, 1), (13, 1, 0), (12, 1, 3),
    (12, 2, 0), (9, 2, 1), (10, 1, 1), (10, 2, 0), (9, 2, 2), (13, 1, 1), (13, 2, 0), (-1, SMALL, 2),
    (9, 2, 3), (7, 1, 1), (7, 2, 0), (10, 2, 1), (11, 2, 1), (9, END, 0), (12, 2, 1), (11, END, 0),
    (12, END, 0), (13, 2, 1), (7, 2, 1), (10, 2, 2), (7, END, 0), (13, 2, 2), (10, 2, 3), (13, 2, 3),
    (10, END, 0), (-1, SMALL, 3), (13, END, 0),
)


def layer_kernel(axes, *refs):
    jobs = len(JOBS)
    (
        x_ref, seg_ref, pos_ref, g1_ref, g2_ref, g3_ref, table_ref, lanes_ref,
        wq_h, wk_h, wv_h, wo_h, w1_h, w2_h,
        emb_o, loss_o, small_o, gh_o, inner_o,
    ) = refs[:19]
    res, refs = refs[19 : 19 + jobs], refs[19 + jobs :]
    (
        all_e, gs, hid, ig, chunk, wslot, q, k, v, att, nrm, br2, br1, mid, fin, by_offset, d_all,
        sm, sm_core, sm_plane, sm_line, stg,
    ) = refs[:22]
    accs, landings, refs = refs[22 : 22 + jobs], refs[22 + jobs : 22 + 4 * jobs], refs[22 + 4 * jobs :]
    load_sem, ag_s, ag_r, sm_s, sm_r, tow_s, tow_r, end_s, end_r, end_l, line_s, line_r = refs

    t = lax.axis_index("tower")
    row = lax.axis_index("rows")
    place = [ax.place(row) for ax in axes]
    nx, ny, nz = (ax.size for ax in axes)
    sx, sy, sz = (ax.stride for ax in axes)
    plane_size = nx * ny
    plane = place[1] * nx + place[0]
    spot = plane * nz + place[2]

    def row_of(w, z):
        return lax.rem(w, nx) * sx + lax.div(w, nx) * sy + z * sz

    z_peers = [(t, row_of(plane, lax.rem(place[2] + m, nz))) for m in range(1, nz)]
    plane_peers = [(t, row_of(lax.rem(plane + m, plane_size), place[2])) for m in range(1, plane_size)]
    partner = (1 - t, row)

    barrier = pltpu.get_barrier_semaphore()
    for peer in z_peers + plane_peers + [partner]:
        pl.semaphore_signal(barrier, inc=1, device_id=peer, device_id_type=MESH_IDS)

    def load(i, src, dst):
        return pltpu.make_async_copy(src, dst, load_sem.at[i])

    def remote(src, dst, ss, rs, to):
        return pltpu.make_async_remote_copy(
            src_ref=src, dst_ref=dst, send_sem=ss, recv_sem=rs, device_id=to, device_id_type=MESH_IDS
        )

    seq, width = x_ref.shape
    heads = table_ref.shape[0]
    ff = hid.shape[1]
    piece = 512
    pieces = ff // piece
    blocks = seq // BLOCK
    tail = width - seq
    square_loads = [
        load(i, w, wslot.at[pl.ds(i * width, width)]) for i, w in enumerate((wq_h, wk_h, wv_h, wo_h))
    ]
    ahead_loads = [load(4, w1_h.at[pl.ds(0, seq)], ig)]
    tails = []
    for c in range(ff // width):
        held = (br2 if c < 2 else br1).at[pl.ds(c % 2 * tail, tail)]
        tails.append(held)
        ahead_loads.append(load(5 + c, w1_h.at[pl.ds(seq, tail), pl.ds(c * width, width)], held))
    w2_load = load(9, w2_h, wslot)
    back_loads = [
        load(10 + c, w1_h.at[:, pl.ds(c * width, width)], wslot.at[pl.ds(c * width, width)])
        for c in range(ff // width)
    ]
    gh_store = load(14, fin, gh_o)
    kept = [load(15 + c, chunk.at[c % 2], inner_o.at[:, pl.ds(c * piece, piece)]) for c in range(pieces - 2)]
    fetched = [load(15 + c, inner_o.at[:, pl.ds(c * piece, piece)], chunk.at[c % 2]) for c in range(pieces - 2)]
    for w in square_loads[:3]:
        w.start()

    def normed(values, gain_ref):
        return ((values * rms_inverse(values)) * row_of_gain(gain_ref)).astype(bf16)

    nrm[...] = normed(x_ref[...].astype(f32), g1_ref)
    square_loads[3].start()
    for w in ahead_loads:
        w.start()
    for i, out in enumerate((q, k, v)):
        square_loads[i].wait()
        out[...] = dot_nn(nrm[...], wslot[i * width : (i + 1) * width, :]).astype(bf16)

    seg_row = seg_ref[...].astype(f32)
    low_half = lax.broadcasted_iota(jnp.int32, (BLOCK, BLOCK), 1) < BLOCK // 2

    def bias_tile(h, first, last):
        n = h % 4 * BLOCK
        if h < 8:
            lane = h // 4 * 3 * BLOCK
            return fin[n : n + BLOCK, lane + first : lane + last]
        return chunk[0, n : n + BLOCK, first:last]

    def build_tiles():
        by_offset[0:heads, :] = dot_nn(table_ref[...], lanes_ref[...])
        for h in range(heads):
            spread = jnp.broadcast_to(by_offset[h : h + 1, :], (BLOCK, 4 * BLOCK))
            tile = pltpu.roll(spread, 0, 1, stride=1, stride_axis=0)[:, : 3 * BLOCK]
            n = h % 4 * BLOCK
            if h < 8:
                lane = h // 4 * 3 * BLOCK
                fin[n : n + BLOCK, lane : lane + 3 * BLOCK] = tile
            else:
                chunk[0, n : n + BLOCK, 0 : 3 * BLOCK] = tile
        seg_col = column_of(seg_row)
        for b in range(blocks):
            lo, hi = key_range(b, blocks)
            first = lo - (b - 1) * BLOCK
            same = seg_col[b * BLOCK : (b + 1) * BLOCK] == seg_row[:, lo:hi]
            chunk[1, b * BLOCK : (b + 1) * BLOCK, first : first + hi - lo] = jnp.where(same, 0.0, far_below)

    def two_heads(values):
        zero = jnp.zeros_like(values)
        return jnp.concatenate([jnp.where(low_half, values, zero), jnp.where(low_half, zero, values)], axis=0)

    def probabilities(pair, b, both, keys):
        lo, hi = key_range(b, blocks)
        first = lo - (b - 1) * BLOCK
        last = first + hi - lo
        mask = chunk[1, b * BLOCK : (b + 1) * BLOCK, first:last]
        s = dot_nt(both, keys)
        parts = []
        for e in range(2):
            part = s[e * BLOCK : (e + 1) * BLOCK] + bias_tile(2 * pair + e, first, last) + mask
            terms = jnp.exp(part - jnp.max(part, axis=-1, keepdims=True))
            parts.append(terms * (1.0 / jnp.sum(terms, axis=-1, keepdims=True)))
        return parts

    build_tiles()
    for pair in range(heads // 2):
        lanes = slice(pair * UNIT, (pair + 1) * UNIT)
        for b in range(blocks):
            lo, hi = key_range(b, blocks)
            mine = slice(b * BLOCK, (b + 1) * BLOCK)
            parts = probabilities(pair, b, two_heads(q[mine, lanes]), k[lo:hi, lanes])
            probs = jnp.concatenate([part.astype(bf16) for part in parts], axis=0)
            out = dot_nn(probs, v[lo:hi, lanes])
            att[mine, lanes] = jnp.where(low_half, out[:BLOCK], out[BLOCK:]).astype(bf16)

    square_loads[3].wait()
    middle = x_ref[...].astype(f32) + dot_nn(att[...], wslot[3 * width : 4 * width, :])
    w2_load.start()
    mid[...] = middle
    nrm[...] = normed(middle, g2_ref)
    for w in ahead_loads:
        w.wait()
    for c in range(pieces):
        low = c * piece
        inner = dot_nn(nrm[:, 0:seq], ig[:, low : low + piece])
        rest = []
        while low < (c + 1) * piece:
            n = low // width
            high = min((c + 1) * piece, (n + 1) * width)
            rest.append(dot_nn(nrm[:, seq:width], tails[n][:, low - n * width : high - n * width]))
            low = high
        inner = inner + (jnp.concatenate(rest, axis=1) if len(rest) > 1 else rest[0])
        if c >= 2:
            kept[c - 2].wait()
        chunk[c % 2] = inner
        if c < pieces - 2:
            kept[c].start()
        tangent = jnp.tanh(gelu_factor * (inner + gelu_cubic * (inner * inner * inner)))
        hid[:, c * piece : (c + 1) * piece] = (inner * (0.5 * (1.0 + tangent))).astype(bf16)
    w2_load.wait()
    final = mid[...] + dot_nn(hid[...], wslot[...])
    fin[...] = final
    member = (lax.broadcasted_iota(jnp.int32, (ITEM_ROW, seq), 0).astype(f32) == seg_row).astype(f32)
    counts = jnp.sum(member, axis=-1, keepdims=True)
    pooled = dot_nn(member, (final * rms_inverse(final)) * row_of_gain(g3_ref), exact) / counts

    inverse_pool = lax.rsqrt(jnp.sum(pooled * pooled, axis=-1, keepdims=True) + epsilon)
    own_e = pooled * inverse_pool
    emb_o[...] = own_e
    own_rows = pl.ds(pl.multiple_of(spot * ITEM_ROW, ITEM_ROW), ITEM_ROW)

    def bits(n):
        return n.bit_length() - 1

    p = pos_ref[...]
    of_row = p >> bits(ITEM_ROW)

    def along(ax):
        return (of_row >> bits(ax.stride)) & (ax.size - 1)

    p = ((along(axes[1]) * nx + along(axes[0])) * nz + along(axes[2])) * ITEM_ROW + (p & (ITEM_ROW - 1))
    i8 = lax.broadcasted_iota(jnp.int32, (ITEM_ROW, ITEM_ROW), 0)
    j8 = lax.broadcasted_iota(jnp.int32, (ITEM_ROW, ITEM_ROW), 1)
    diag = jnp.where(i8 == j8, jnp.broadcast_to(p.astype(f32), (ITEM_ROW, ITEM_ROW)), 0.0)
    pos_col = jnp.sum(diag, axis=-1, keepdims=True)
    all_e[t, own_rows, 0:width] = own_e
    all_e[t, own_rows, width : width + UNIT] = jnp.broadcast_to(pos_col, (ITEM_ROW, UNIT))

    pl.semaphore_wait(barrier, len(z_peers) + len(plane_peers) + 1)

    def column_rows(w):
        return pl.ds(pl.multiple_of(w * (nz * ITEM_ROW), ITEM_ROW), nz * ITEM_ROW)

    first = []
    for m, peer in enumerate(z_peers):
        block = all_e.at[t, own_rows]
        first.append(remote(block, block, ag_s.at[m], ag_r.at[m], peer))
        first[-1].start()
    inverse = rms_inverse(fin[...])
    sm[...] = jnp.zeros_like(sm)
    for c in first:
        c.wait_recv()
    n1 = len(z_peers)
    second = []
    mine = all_e.at[t, column_rows(plane)]
    for m, peer in enumerate(plane_peers):
        second.append(remote(mine, mine, ag_s.at[n1 + m], ag_r.at[n1 + m], peer))
        second[-1].start()
    n2 = n1 + len(plane_peers)
    third = [remote(mine, mine, ag_s.at[n2], ag_r.at[n2], partner)]
    third[0].start()
    for m in range(1, plane_size):
        second[m - 1].wait_recv()
        block = all_e.at[t, column_rows(lax.rem(plane + plane_size - m, plane_size))]
        third.append(remote(block, block, ag_s.at[n2 + m], ag_r.at[n2 + m], partner))
        third[-1].start()
    for c in third:
        c.wait_recv()
    sent = first + second + third

    queries, docs = all_e[0, :, 0:width], all_e[1, :, 0:width]
    items = queries.shape[0]
    scores = dot_nt(queries, docs, exact) / logit_divisor
    top = jnp.max(scores, axis=1, keepdims=True)
    terms = jnp.exp(scores - top)
    summed = jnp.sum(terms, axis=1, keepdims=True)
    chosen = (
        lax.broadcasted_iota(jnp.int32, (items, items), 1).astype(f32) == all_e[0, :, width : width + 1]
    ).astype(f32)
    slope = loss_scale * (terms / summed - chosen)

    @pl.when(t == 0)
    def _():
        gs[...] = slope

    @pl.when(t == 1)
    def _():
        gs[...] = slope.T

    embed_grad = dot_nn(gs[own_rows, :], all_e[1 - t, :, 0:width], exact) / logit_divisor
    inner_dot = jnp.sum(own_e * embed_grad, axis=-1, keepdims=True)
    pooled_grad = inverse_pool * (embed_grad - own_e * inner_dot)

    three_grad = dot_tn(member, pooled_grad / counts, exact)
    unit = fin[...] * inverse
    sm[0:1, 0:width] = jnp.sum(three_grad * unit, axis=0, keepdims=True)
    u = three_grad * row_of_gain(g3_ref)
    final_grad = inverse * (u - unit * jnp.mean(u * unit, axis=-1, keepdims=True))
    fin[...] = final_grad
    br2[...] = final_grad.astype(bf16)

    def write_losses():
        losses = top + jnp.log(summed) - jnp.sum(scores * chosen, axis=1, keepdims=True)
        loss_row = jnp.broadcast_to(losses, (items, UNIT)).T[0:8, :]
        pick = (
            lax.broadcasted_iota(jnp.int32, (items, UNIT), 0)
            == lax.broadcasted_iota(jnp.int32, (items, UNIT), 1) + spot * ITEM_ROW + t * (ITEM_ROW // 2)
        ).astype(f32)
        loss_o[...] = dot_nn(loss_row, pick, exact)

    chunk_rows = width // (nx * ny * nz)
    lefts = (hid, nrm, att, nrm, nrm, nrm)
    rights = (br2, ig, br1, v, q, k)
    in_slot = {}
    unwaited = []

    def spots(path):
        found = {}
        for r in range(nx * ny * nz):
            number = 0
            for a in path:
                number = number * axes[a].size + (r // axes[a].stride) % axes[a].size
            found[r] = number * chunk_rows
        return found

    def product(job, half):
        path, parts = JOBS[job]
        lhs = lefts[parts[0][0]]
        stripes = list(dict.fromkeys((target, block) for target, block, _ in parts))
        right = []
        for target, block in stripes:
            rhs = rights[target]
            lane = half * (rhs.shape[1] // 2) + block * UNIT
            right.append(rhs[:, pl.ds(pl.multiple_of(lane, UNIT), UNIT)])
        value = dot_tn(lhs[...], jnp.concatenate(right, axis=1) if len(right) > 1 else right[0])
        subs = lhs.shape[1] // width
        for r, at_row in spots(path).items():
            for n, (target, block, sub) in enumerate(parts):
                low = (r * subs + sub) * chunk_rows
                lane = stripes.index((target, block)) * UNIT
                yield n, at_row, value[low : low + chunk_rows, lane : lane + UNIT]

    def tower_copy(job, slot):
        units = len(JOBS[job][1])
        return remote(stg.at[slot, pl.ds(0, units)], accs[job], tow_s.at[job], tow_r.at[job], partner)

    def send_half(job):
        slot = len(in_slot) % SLOTS
        before = [n for n, s in in_slot.items() if s == slot]
        if before:
            tower_copy(before[-1], slot).wait_send()
            unwaited.remove(before[-1])
        for n, at_row, value in product(job, 1 - t):
            stg[slot, n, at_row : at_row + chunk_rows, :] = value
        tower_copy(job, slot).start()
        in_slot[job] = slot
        unwaited.append(job)

    def take_own(job):
        acc = accs[job]
        made = list(product(job, t))
        tower_copy(job, 0).wait_recv()
        for n, at_row, value in made:
            span = slice(at_row, at_row + chunk_rows)
            acc[n, span, :] = acc[n, span, :] + value

    def geometry(job, leg):
        path = JOBS[job][0]
        low, size = 0, width
        for a in path[:leg]:
            size = size // axes[a].size
            low = low + place[a] * size
        return low, size // axes[path[leg]].size, axes[path[leg]], place[path[leg]]

    def line_copy(job, leg, i, block):
        low, size, axis, _ = geometry(job, leg)
        n = axis.size
        if block > i:
            to, slot = (t, row + axis.stride), (0 if n == 2 else block)
        else:
            to, slot = (t, row - axis.stride), (0 if n == 2 else n if block == i - 1 else block)
        at_row = pl.multiple_of(low + block * size, 8)
        return remote(
            accs[job].at[:, pl.ds(at_row, size)], landings[3 * job + leg].at[slot],
            line_s.at[job, leg, block], line_r.at[job, leg, slot], to,
        )

    def take(job, leg, block, slot):
        low, size, axis, _ = geometry(job, leg)
        at_row = pl.multiple_of(low + block * size, 8)
        acc, landed = accs[job], landings[3 * job + leg]
        remote(
            landed.at[slot], landed.at[slot], line_s.at[job, leg, block], line_r.at[job, leg, slot], partner
        ).wait_recv()
        acc[:, pl.ds(at_row, size), :] = acc[:, pl.ds(at_row, size), :] + landed[slot]

    def line_step(job, leg, s):
        _, _, axis, my_place = geometry(job, leg)
        n = axis.size
        for i in range(n):
            from_left = s == i and i < n - 1
            from_right = s == n - 1 - i and i > 0
            last = s == n - 1
            if not (from_left or from_right or last):
                continue

            @pl.when(my_place == i)
            def _():
                if from_left:
                    for block in range(n - 1, i, -1):
                        if i > 0:
                            take(job, leg, block, block)
                        line_copy(job, leg, i, block).start()
                if from_right:
                    for block in range(i):
                        if i < n - 1:
                            take(job, leg, block, block)
                        line_copy(job, leg, i, block).start()
                if last:
                    if n == 2:
                        take(job, leg, i, 0)
                    else:
                        if i > 0:
                            take(job, leg, i, i)
                        if i < n - 1:
                            take(job, leg, i, n)

        if s == n - 1 and leg == 2:
            end_copy(job, True).start()
            end_copy(job, False).start()

    def line_drain(job, leg):
        _, _, axis, my_place = geometry(job, leg)
        for i in range(axis.size):

            @pl.when(my_place == i)
            def _():
                for block in range(axis.size):
                    if block != i:
                        line_copy(job, leg, i, block).wait_send()

    def end_copy(job, to_partner):
        low, size, _, my_place = geometry(job, 2)
        at_row = pl.multiple_of(low + my_place * size, 8)
        src, dst = accs[job].at[:, pl.ds(at_row, size)], res[job].at[t]
        if to_partner:
            return remote(src, dst, end_s.at[job], end_r.at[job], partner)
        return pltpu.make_async_copy(src, dst, end_l.at[job])

    def inner_step(n):
        c = (n + pieces - 2) % pieces
        if n >= 2:
            fetched[c].wait()
        v_in = chunk[c % 2]
        grad = dot_nt(br2[...], wslot[c * piece : (c + 1) * piece, :])
        tangent = jnp.tanh(gelu_factor * (v_in + gelu_cubic * (v_in * v_in * v_in)))
        ahead = 0.5 * (1.0 + tangent) + 0.5 * v_in * (1.0 - tangent * tangent) * gelu_factor * (
            1.0 + 3.0 * gelu_cubic * v_in * v_in
        )
        ig[:, c * piece : (c + 1) * piece] = (grad * ahead).astype(bf16)
        if n + 2 < pieces:
            fetched[n].start()
        if n == pieces - 1:
            for w in back_loads:
                w.start()

    def norm_back(grad, values, gain):
        inverse = rms_inverse(values)
        unit = values * inverse
        total = jnp.sum(grad * unit, axis=0, keepdims=True)
        w = grad * gain
        return inverse * (w - unit * jnp.mean(w * unit, axis=-1, keepdims=True)), total

    tokens = 256

    def two_step():
        for w in back_loads:
            w.wait()
        gain = row_of_gain(g2_ref)
        for low in range(0, seq, tokens):
            part = slice(low, low + tokens)
            grad = dot_nt(ig[part, 0:width], wslot[0:width, :])
            for c in range(1, ff // width):
                lanes = slice(c * width, (c + 1) * width)
                grad = grad + dot_nt(ig[part, lanes], wslot[lanes, :])
            back, total = norm_back(grad, mid[part, :], gain)
            sm[1:2, 0:width] = sm[1:2, 0:width] + total
            middle_grad = fin[part, :] + back
            mid[part, :] = middle_grad
            br1[part, :] = middle_grad.astype(bf16)
        for w in square_loads:
            w.start()
        build_tiles()

    def attended_step():
        for w in square_loads:
            w.wait()
        br2[...] = dot_nt(br1[...], wslot[3 * width : 4 * width, :]).astype(bf16)
        d_all[...] = jnp.zeros_like(d_all)

    turned = [lax.broadcasted_iota(jnp.int32, (BLOCK, BLOCK), n) for n in range(2)]
    upside = (turned[0] + turned[1] == BLOCK - 1).astype(bf16)

    def upside_down(values):
        high = values.astype(bf16)
        rest = values - high.astype(f32)
        middle_part = rest.astype(bf16)
        low_part = (rest - middle_part.astype(f32)).astype(bf16)
        return dot_nn(upside, high) + (dot_nn(upside, middle_part) + dot_nn(upside, low_part))

    def heads_step(pair):
        lanes = slice(pair * UNIT, (pair + 1) * UNIT)
        columns = [[None] * 3, [None] * 3]
        key_grads, value_grads = [None] * blocks, [None] * blocks

        def put(held, n, value):
            held[n] = value if held[n] is None else held[n] + value

        for b in range(blocks):
            lo, hi = key_range(b, blocks)
            mine = slice(b * BLOCK, (b + 1) * BLOCK)
            first = lo - (b - 1) * BLOCK
            keys = k[lo:hi, lanes]
            both_q, both_o = two_heads(q[mine, lanes]), two_heads(br2[mine, lanes])
            probs = probabilities(pair, b, both_q, keys)
            pg = dot_nt(both_o, v[lo:hi, lanes])
            grads = []
            for e in range(2):
                ds = pg[e * BLOCK : (e + 1) * BLOCK]
                ds = probs[e] * (ds - jnp.sum(probs[e] * ds, axis=-1, keepdims=True))
                for n in range((hi - lo) // BLOCK):
                    put(columns[e], first // BLOCK + n, ds[:, n * BLOCK : (n + 1) * BLOCK])
                grads.append(ds.astype(bf16))
            rounded = jnp.concatenate(grads, axis=0)
            dq = dot_nn(rounded, keys)
            dk = dot_tn(rounded, both_q)
            dv = dot_tn(jnp.concatenate([part.astype(bf16) for part in probs], axis=0), both_o)
            for n in range((hi - lo) // BLOCK):
                rows = slice(n * BLOCK, (n + 1) * BLOCK)
                put(key_grads, lo // BLOCK + n, dk[rows])
                put(value_grads, lo // BLOCK + n, dv[rows])
            q[mine, lanes] = jnp.where(low_half, dq[:BLOCK], dq[BLOCK:]).astype(bf16)
        for b in range(blocks):
            mine = slice(b * BLOCK, (b + 1) * BLOCK)
            k[mine, lanes] = key_grads[b].astype(bf16)
            v[mine, lanes] = value_grads[b].astype(bf16)
        for e in range(2):
            wide = jnp.concatenate(columns[e] + [jnp.zeros((BLOCK, BLOCK), f32)], axis=1)
            skewed = pltpu.roll(upside_down(wide), 3 * BLOCK + 1, 1, stride=1, stride_axis=0)
            d_all[2 * pair + e : 2 * pair + e + 1, :] = jnp.sum(skewed, axis=0, keepdims=True)

    def normed_step():
        nrm[...] = normed(x_ref[...].astype(f32), g1_ref)

    def one_step():
        gain = row_of_gain(g1_ref)
        for low in range(0, seq, tokens):
            part = slice(low, low + tokens)
            grad = dot_nt(q[part, :], wslot[0:width, :])
            grad = grad + dot_nt(k[part, :], wslot[width : 2 * width, :])
            grad = grad + dot_nt(v[part, :], wslot[2 * width : 3 * width, :])
            back, total = norm_back(grad, x_ref[part, :].astype(f32), gain)
            sm[2:3, 0:width] = sm[2:3, 0:width] + total
            fin[part, :] = mid[part, :] + back
        gh_store.start()
        write_losses()

    small_first = remote(sm, sm_core, sm_s.at[0], sm_r.at[0], partner)
    base = 1 + len(plane_peers)
    own_plane, own_line = sm_plane.at[plane], sm_line.at[place[2]]
    small_second = [
        remote(own_plane, own_plane, sm_s.at[1 + m], sm_r.at[1 + m], peer) for m, peer in enumerate(plane_peers)
    ]
    small_third = [
        remote(own_line, own_line, sm_s.at[base + m], sm_r.at[base + m], peer) for m, peer in enumerate(z_peers)
    ]

    def small_step(s):
        if s == 0:
            table_grad = dot_nt(d_all[...], lanes_ref[...].astype(f32), exact)
            for n in range(2):
                sm[:, width + n * UNIT : width + n * UNIT + BUCKETS] = table_grad[8 * n : 8 * n + 8, :]
            small_first.start()
        elif s == 1:
            small_first.wait()
            sm_plane[plane] = sm[...] + sm_core[...]
            for c in small_second:
                c.start()
        elif s == 2:
            for c in small_second:
                c.wait()
            total = sm_plane[0]
            for w in range(1, plane_size):
                total = total + sm_plane[w]
            sm_line[place[2]] = total
            for c in small_third:
                c.start()
        else:
            for c in small_third:
                c.wait()
            total = sm_line[0]
            for w in range(1, nz):
                total = total + sm_line[w]
            small_o[...] = total

    layer_steps = {
        INNER: inner_step, TWO: lambda n: two_step(), ATTENDED: lambda n: attended_step(), HEADS: heads_step,
        NORMED: lambda n: normed_step(), ONE: lambda n: one_step(), SMALL: small_step,
    }
    for job, leg, s in STEPS:
        if job < 0:
            layer_steps[leg](s)
        elif leg == SEND:
            send_half(job)
        elif leg == OWN:
            take_own(job)
        elif leg == END:
            end_copy(job, True).wait_recv()
            end_copy(job, False).wait()
        else:
            line_step(job, leg, s)
    for c in sent:
        c.wait_send()
    for job in unwaited:
        tower_copy(job, in_slot[job]).wait_send()
    for job in range(jobs):
        for leg in range(3):
            line_drain(job, leg)
        end_copy(job, True).wait_send()
    gh_store.wait()


def layer_call(axes, args):
    seq, width = args[0].shape
    ff = args[12].shape[1]
    nx, ny, nz = (ax.size for ax in axes)
    rows = nx * ny * nz
    chunk_rows = width // rows
    s = jax.ShapeDtypeStruct
    vm, hbm = pl.BlockSpec(memory_space=VMEM), pl.BlockSpec(memory_space=pl.ANY)
    small = (8, width + 2 * UNIT)
    most_units = max(len(parts) for _, parts in JOBS)
    outs = [
        s((ITEM_ROW, width), f32), s((8, UNIT), f32), s(small, f32), s((seq, width), f32), s((seq, ff), f32),
    ]
    outs += [s((2, len(parts), chunk_rows, UNIT), f32) for _, parts in JOBS]
    scratch = [
        VMEM((2, rows * ITEM_ROW, width + UNIT), f32), VMEM((rows * ITEM_ROW, rows * ITEM_ROW), f32),
        VMEM((seq, ff), bf16), VMEM((seq, ff), bf16), VMEM((2, seq, 512), f32), VMEM((ff, width), bf16),
    ]
    scratch += [VMEM((seq, width), bf16)] * 7 + [VMEM((seq, width), f32)] * 2
    scratch += [
        VMEM((16, 4 * BLOCK), f32), VMEM((16, 4 * BLOCK), f32),
        VMEM(small, f32), VMEM(small, f32), VMEM((nx * ny, *small), f32), VMEM((nz, *small), f32),
        VMEM((SLOTS, most_units, width, UNIT), f32),
    ]
    scratch += [VMEM((len(parts), width, UNIT), f32) for _, parts in JOBS]
    for path, parts in JOBS:
        size = width
        for a in path:
            n = axes[a].size
            size = size // n
            scratch.append(VMEM((1 if n == 2 else n + 1, len(parts), size, UNIT), f32))
    dma = pltpu.SemaphoreType.DMA
    jobs, most = len(JOBS), max(nx, ny, nz)
    gathers = nz - 1 + nx * ny - 1 + nx * ny
    smalls = nz + nx * ny - 1
    scratch += [
        dma((19,)), dma((gathers,)), dma((gathers,)), dma((smalls,)), dma((smalls,)),
        dma((jobs,)), dma((jobs,)), dma((jobs,)), dma((jobs,)), dma((jobs,)),
        dma((jobs, 3, most)), dma((jobs, 3, most + 1)),
    ]
    return pl.pallas_call(
        functools.partial(layer_kernel, axes),
        name="layer",
        out_shape=outs,
        in_specs=[vm] * 8 + [hbm] * 6,
        out_specs=[vm] * 3 + [hbm] * (2 + jobs),
        scratch_shapes=scratch,
        compiler_params=pltpu.CompilerParams(
            collective_id=0, has_side_effects=True, vmem_limit_bytes=VMEM_LIMIT
        ),
    )(*args)


def place_kernel(emb, loss, small, gh, *refs):
    res = refs[: len(JOBS)]
    (
        emb_o, loss_o, gh_o, attn_gain_o, query_o, key_o, value_o, attn_o, table_o, ffn_gain_o, in_o, out_o, final_gain_o,
    ) = refs[len(JOBS) :]
    row = lax.axis_index("rows")
    targets = (out_o, in_o, attn_o, value_o, query_o, key_o)
    emb_o[0] = emb[...]
    gh_o[0, 0] = gh[...]
    for job, (_, parts) in enumerate(JOBS):
        for n, (target, block, sub) in enumerate(parts):
            out, height = targets[target], res[job].shape[2]
            for t in range(2):
                low = t * (out.shape[1] // 2) + block * UNIT
                out[sub * height : (sub + 1) * height, low : low + UNIT] = res[job][t, n]
    loss_o[0] = loss[0:1, 0 : loss_o.shape[2]]
    width = gh.shape[1]
    share = attn_gain_o.shape[0]
    pick = (
        lax.broadcasted_iota(jnp.int32, (width, UNIT), 0)
        == lax.broadcasted_iota(jnp.int32, (width, UNIT), 1) + row * share
    ).astype(f32)
    gains = dot_nn(small[:, 0:width], pick, exact)
    for n, out in enumerate((final_gain_o, ffn_gain_o, attn_gain_o)):
        out[...] = gains[n, 0:share]
    heads = table_o.shape[0]
    for low in range(0, heads, 8):
        lane = width + low // 8 * UNIT
        high = min(low + 8, heads)
        table_o[low:high, :] = small[0 : high - low, lane : lane + BUCKETS]


def place_call(axes, heads, emb, loss, small, gh, res):
    seq, width = gh.shape
    ff = 4 * width
    rows = math.prod(a.size for a in axes)
    share = width // rows
    s = jax.ShapeDtypeStruct
    vm = pl.BlockSpec(memory_space=VMEM)
    weight = s((share, width), f32)
    outs = [
        s((1, *emb.shape), f32), s((1, 1, ITEM_ROW // 2), f32), s((1, 1, seq, width), f32), s((share,), f32),
        weight, weight, weight, weight, s((heads, BUCKETS), f32), s((share,), f32),
        s((share, ff), f32), s((ff // rows, width), f32), s((share,), f32),
    ]
    return pl.pallas_call(
        place_kernel,
        name="place",
        out_shape=outs,
        in_specs=[vm] * (4 + len(JOBS)),
        out_specs=[vm] * len(outs),
        compiler_params=pltpu.CompilerParams(vmem_limit_bytes=VMEM_LIMIT),
    )(emb, loss, small, gh, *res)


def rows_axes(mesh):
    rows = mesh.shape["rows"]
    line = mesh.devices.reshape(-1, rows)[0]
    places = [tuple(getattr(d, "coords", (i % 2, i // 2 % 2, i // 4))) for i, d in enumerate(line)]
    axes = []
    for n in range(3):
        values = sorted({p[n] for p in places})
        stride = next((i for i, p in enumerate(places) if p[n] != places[0][n]), 1)
        axes.append(Axis(len(values), stride))
    return tuple(axes)


def fused(
    axes, hidden_in, segment_ids, positives, attn_gain, w_query, w_key, w_value, w_attn_out, rel_table,
    ffn_gain, w_ffn_in, w_ffn_out, final_gain,
):
    seq, width = hidden_in.shape[2:]
    lanes = jnp.asarray(lane_buckets(), bf16)
    emb, loss, small, gh, _, *res = layer_call(
        axes,
        (
            hidden_in.reshape(seq, width), segment_ids.reshape(1, seq), positives.reshape(1, -1),
            attn_gain, ffn_gain, final_gain, rel_table.T, lanes,
            w_query, w_key, w_value, w_attn_out, w_ffn_in, w_ffn_out,
        ),
    )
    outs = list(place_call(axes, rel_table.shape[1], emb, loss, small, gh, res))
    outs[8] = outs[8].T
    return tuple(outs)


def from_partner(block, axis, bit):
    count = lax.axis_size(axis)
    route = []
    for low in range(count):
        high = low | 1 << bit
        if high != low and high < count:
            route += [(low, high), (high, low)]
    return lax.ppermute(block, axis, route)


def bucket_onehot(seq_len, bucket_count, max_distance):
    half_count = bucket_count // 2
    exact_count = half_count // 2
    log_steps = half_count - exact_count
    bounds = []
    for section_index in range(1, log_steps):
        target = exact_count ** (log_steps - section_index) * max_distance**section_index
        lowest = exact_count
        while lowest**log_steps < target:
            lowest = lowest + 1
        bounds.append(lowest)
    onehot = np.zeros((2 * seq_len - 1, bucket_count), np.float32)
    for offset in range(2 * seq_len - 1):
        relative = offset - (seq_len - 1)
        distance = abs(relative)
        bucket = half_count if relative > 0 else 0
        if distance < exact_count:
            bucket = bucket + distance
        else:
            bucket = (
                bucket
                + exact_count
                + len([boundary for boundary in bounds if distance >= boundary])
            )
        onehot[offset, bucket] = 1.0
    return onehot


def matmul(left_side, right_side):
    return jnp.dot(left_side, right_side, preferred_element_type=jnp.float32)


def contract_rows(left_side, right_side):
    return lax.dot_general(
        left_side, right_side, (((0,), (0,)), ((), ())), preferred_element_type=jnp.float32
    )


def contract_cols(left_side, right_side):
    return lax.dot_general(
        left_side, right_side, (((1,), (1,)), ((), ())), preferred_element_type=jnp.float32
    )


def gelu_slope(values):
    factor = math.sqrt(2.0 / math.pi)
    tangent = jnp.tanh(factor * (values + gelu_cubic * values * values * values))
    return 0.5 * (1.0 + tangent) + 0.5 * values * (1.0 - tangent * tangent) * factor * (
        1.0 + 3.0 * gelu_cubic * values * values
    )


def rms_parts(values):
    inverse = lax.rsqrt(jnp.mean(values * values, axis=-1, keepdims=True) + epsilon)
    return (values * inverse, inverse)


def rms_back(unit_grad, unit_values, inverse):
    return inverse * (
        unit_grad - unit_values * jnp.mean(unit_grad * unit_values, axis=-1, keepdims=True)
    )


def position_bias(rel_table, onehot, seq_len):
    head_count = rel_table.shape[1]
    by_offset = lax.dot_general(
        rel_table.astype(jnp.float32), onehot, (((0,), (1,)), ((), ())), precision=exact
    )
    rolled = jnp.concatenate([by_offset[:, seq_len - 1 :], by_offset[:, : seq_len - 1]], axis=1)
    repeated = jnp.tile(rolled, (1, seq_len))[:, : seq_len * (2 * seq_len - 2)]
    return repeated.reshape(head_count, seq_len, 2 * seq_len - 2)[:, :, :seq_len]


def diagonal_sums(matrix, seq_len):
    head_count = matrix.shape[0]
    flipped = matrix[:, :, ::-1]
    padded = jnp.pad(flipped, ((0, 0), (0, 0), (0, seq_len)))
    skewed = padded.reshape(head_count, 2 * seq_len * seq_len)[:, : seq_len * (2 * seq_len - 1)]
    skewed = skewed.reshape(head_count, seq_len, 2 * seq_len - 1)
    return jnp.sum(skewed, axis=1)[:, ::-1]


def on_device(
    hidden_in,
    segment_ids,
    positives,
    attn_gain,
    w_query,
    w_key,
    w_value,
    w_attn_out,
    rel_table,
    ffn_gain,
    w_ffn_in,
    w_ffn_out,
    final_gain,
):
    row_count = hidden_in.shape[1]
    seq_len = hidden_in.shape[2]
    model_width = hidden_in.shape[3]
    head_count = rel_table.shape[1]
    head_width = model_width // head_count
    token_count = row_count * seq_len
    tokens = hidden_in.reshape(token_count, model_width).astype(jnp.float32)
    segments = segment_ids.reshape(row_count, seq_len)
    gain_one = attn_gain.astype(jnp.float32)
    gain_two = ffn_gain.astype(jnp.float32)
    gain_three = final_gain.astype(jnp.float32)
    onehot = jnp.asarray(bucket_onehot(seq_len, BUCKETS, MAX_DIST))
    unit_one, inverse_one = rms_parts(tokens)
    normed_one = (unit_one * gain_one).astype(jnp.bfloat16)
    query_proj = matmul(normed_one, w_query).astype(jnp.bfloat16)
    key_proj = matmul(normed_one, w_key).astype(jnp.bfloat16)
    value_proj = matmul(normed_one, w_value).astype(jnp.bfloat16)
    bias_full = position_bias(rel_table, onehot, seq_len)

    def split_heads(values):
        return values.reshape(row_count, seq_len, head_count, head_width)

    def row_scores(row_query, row_key, row_seg):
        same_item = row_seg[:, None] == row_seg[None, :]
        similarity_table = jnp.einsum(
            "shd,thd->hst", row_query, row_key, preferred_element_type=jnp.float32
        )
        return jnp.where(same_item[None], similarity_table + bias_full, far_below)

    def forward_row(packed):
        row_query, row_key, row_value, row_seg = packed
        masked_scores = row_scores(row_query, row_key, row_seg)
        row_peak = jnp.max(masked_scores, axis=-1, keepdims=True)
        exp_terms = jnp.exp(masked_scores - row_peak)
        summed = jnp.sum(exp_terms, axis=-1, keepdims=True)
        attn_probs = (exp_terms / summed).astype(jnp.bfloat16)
        combined_attention_output = jnp.einsum(
            "hst,thd->shd", attn_probs, row_value, preferred_element_type=jnp.float32
        )
        return (
            combined_attention_output.astype(jnp.bfloat16),
            (row_peak + jnp.log(summed))[:, :, 0],
        )

    attended, log_norms = lax.map(
        forward_row,
        (split_heads(query_proj), split_heads(key_proj), split_heads(value_proj), segments),
    )
    attended = attended.reshape(token_count, model_width)
    middle = tokens + matmul(attended, w_attn_out)
    unit_two, inverse_two = rms_parts(middle)
    normed_two = (unit_two * gain_two).astype(jnp.bfloat16)
    inner = matmul(normed_two, w_ffn_in)
    hidden = jax.nn.gelu(inner, approximate=True).astype(jnp.bfloat16)
    final_sum = middle + matmul(hidden, w_ffn_out)
    unit_three, inverse_three = rms_parts(final_sum)
    normed_three = unit_three * gain_three
    member = (segments[:, None, :] == jnp.arange(ITEM_ROW, dtype=jnp.int32)[None, :, None]).astype(
        jnp.float32
    )
    counts = jnp.sum(member, axis=-1, keepdims=True)
    pooled = (
        jnp.einsum(
            "ris,rsd->rid",
            member,
            normed_three.reshape(row_count, seq_len, model_width),
            precision=exact,
        )
        / counts
    )
    item_count = row_count * ITEM_ROW
    pooled = pooled.reshape(item_count, model_width)
    inverse_pool = lax.rsqrt(jnp.sum(pooled * pooled, axis=-1, keepdims=True) + epsilon)
    encoded_vector_list = pooled * inverse_pool
    half_items = item_count // 2
    tower_index = lax.axis_index("tower")
    rows_size = lax.axis_size("rows")
    is_query = tower_index == 0
    first_half = encoded_vector_list[:half_items]
    second_half = encoded_vector_list[half_items:]
    outgoing = jnp.where(is_query, second_half, first_half)
    incoming = from_partner(outgoing, "tower", 0)
    my_queries = jnp.where(is_query, first_half, incoming)
    local_passages = jnp.where(is_query, incoming, second_half)
    passage_list = lax.all_gather(local_passages, ("tower", "rows"), axis=0, tiled=True)
    total_items = passage_list.shape[0]
    similarity_table = (
        lax.dot_general(
            my_queries, passage_list, (((1,), (1,)), ((), ())), precision=exact
        )
        / logit_divisor
    )
    my_positive = lax.dynamic_slice_in_dim(positives, tower_index * half_items, half_items)
    column = (
        my_positive // half_items % 2 * (rows_size * half_items)
        + my_positive // item_count * half_items
        + my_positive % half_items
    )
    chosen_mask = (jnp.arange(total_items, dtype=jnp.int32)[None, :] == column[:, None]).astype(
        jnp.float32
    )
    row_peak = jnp.max(similarity_table, axis=1, keepdims=True)
    exp_terms = jnp.exp(similarity_table - row_peak)
    summed = jnp.sum(exp_terms, axis=1, keepdims=True)
    losses = (
        row_peak[:, 0] + jnp.log(summed[:, 0]) - jnp.sum(similarity_table * chosen_mask, axis=1)
    )
    similarity_derivative = loss_scale * (exp_terms / summed - chosen_mask)
    query_embedding_gradient = (
        jnp.dot(similarity_derivative, passage_list, precision=exact) / logit_divisor
    )
    doc_embed_grad = lax.psum_scatter(
        lax.dot_general(
            similarity_derivative, my_queries, (((0,), (0,)), ((), ())), precision=exact
        )
        / logit_divisor,
        ("tower", "rows"),
        scatter_dimension=0,
        tiled=True,
    )
    sendback = jnp.where(is_query, doc_embed_grad, query_embedding_gradient)
    received = from_partner(sendback, "tower", 0)
    embed_grad = jnp.where(
        is_query,
        jnp.concatenate([query_embedding_gradient, received], axis=0),
        jnp.concatenate([received, doc_embed_grad], axis=0),
    )
    inner_dot = jnp.sum(encoded_vector_list * embed_grad, axis=-1, keepdims=True)
    pooled_grad = inverse_pool * (embed_grad - encoded_vector_list * inner_dot)
    spread = member / counts
    three_grad = jnp.einsum(
        "ris,rid->rsd",
        spread,
        pooled_grad.reshape(row_count, ITEM_ROW, model_width),
        precision=exact,
    )
    three_grad = three_grad.reshape(token_count, model_width)
    final_gain_grad = jnp.sum(three_grad * unit_three, axis=0)
    final_grad = rms_back(three_grad * gain_three, unit_three, inverse_three)
    branch_two_grad = final_grad.astype(jnp.bfloat16)
    ffn_out_grad = contract_rows(hidden, branch_two_grad)
    inner_grad = (contract_cols(branch_two_grad, w_ffn_out) * gelu_slope(inner)).astype(
        jnp.bfloat16
    )
    ffn_in_grad = contract_rows(normed_two, inner_grad)
    two_grad = contract_cols(inner_grad, w_ffn_in)
    ffn_gain_grad = jnp.sum(two_grad * unit_two, axis=0)
    middle_grad = final_grad + rms_back(two_grad * gain_two, unit_two, inverse_two)
    branch_one_grad = middle_grad.astype(jnp.bfloat16)
    attn_out_grad = contract_rows(attended, branch_one_grad)
    attended_grad = contract_cols(branch_one_grad, w_attn_out).astype(jnp.bfloat16)

    def backward_row(bias_total, packed):
        row_query, row_key, row_value, row_seg, row_norm, row_grad = packed
        masked_scores = row_scores(row_query, row_key, row_seg)
        attn_probs = jnp.exp(masked_scores - row_norm[:, :, None])
        probs_grad = jnp.einsum(
            "shd,thd->hst", row_grad, row_value, preferred_element_type=jnp.float32
        )
        value_grad = jnp.einsum(
            "hst,shd->thd",
            attn_probs.astype(jnp.bfloat16),
            row_grad,
            preferred_element_type=jnp.float32,
        )
        score_part_grad = attn_probs * (
            probs_grad - jnp.sum(attn_probs * probs_grad, axis=-1, keepdims=True)
        )
        rounded = score_part_grad.astype(jnp.bfloat16)
        query_grad = jnp.einsum(
            "hst,thd->shd", rounded, row_key, preferred_element_type=jnp.float32
        )
        key_grad = jnp.einsum(
            "hst,shd->thd", rounded, row_query, preferred_element_type=jnp.float32
        )
        return (
            bias_total + score_part_grad,
            (
                query_grad.astype(jnp.bfloat16),
                key_grad.astype(jnp.bfloat16),
                value_grad.astype(jnp.bfloat16),
            ),
        )

    bias_total, head_grads = lax.scan(
        backward_row,
        jnp.zeros((head_count, seq_len, seq_len), jnp.float32),
        (
            split_heads(query_proj),
            split_heads(key_proj),
            split_heads(value_proj),
            segments,
            log_norms,
            split_heads(attended_grad),
        ),
    )
    query_grad = head_grads[0].reshape(token_count, model_width)
    key_grad = head_grads[1].reshape(token_count, model_width)
    value_grad = head_grads[2].reshape(token_count, model_width)
    table_local = jnp.einsum(
        "ib,hi->bh", onehot, diagonal_sums(bias_total, seq_len), precision=exact
    )
    query_w_grad = contract_rows(normed_one, query_grad)
    key_w_grad = contract_rows(normed_one, key_grad)
    value_w_grad = contract_rows(normed_one, value_grad)
    one_grad = (
        contract_cols(query_grad, w_query)
        + contract_cols(key_grad, w_key)
        + contract_cols(value_grad, w_value)
    )
    attn_gain_grad = jnp.sum(one_grad * unit_one, axis=0)
    input_grad = middle_grad + rms_back(one_grad * gain_one, unit_one, inverse_one)
    table_grad = lax.psum(table_local, ("tower", "rows"))
    shares = (
        lax.psum_scatter(attn_gain_grad, "rows", scatter_dimension=0, tiled=True),
        lax.psum_scatter(query_w_grad, "rows", scatter_dimension=0, tiled=True),
        lax.psum_scatter(key_w_grad, "rows", scatter_dimension=0, tiled=True),
        lax.psum_scatter(value_w_grad, "rows", scatter_dimension=0, tiled=True),
        lax.psum_scatter(attn_out_grad, "rows", scatter_dimension=0, tiled=True),
        lax.psum_scatter(ffn_gain_grad, "rows", scatter_dimension=0, tiled=True),
        lax.psum_scatter(ffn_in_grad, "rows", scatter_dimension=0, tiled=True),
        lax.psum_scatter(ffn_out_grad, "rows", scatter_dimension=0, tiled=True),
        lax.psum_scatter(final_gain_grad, "rows", scatter_dimension=0, tiled=True),
    )
    summed_grads = lax.psum(
        (
            shares[0],
            shares[1],
            shares[2],
            shares[3],
            shares[4],
            shares[5],
            shares[6],
            shares[7],
            shares[8],
        ),
        "tower",
    )
    return (
        encoded_vector_list[None],
        losses.reshape(1, 1, half_items),
        input_grad.reshape(hidden_in.shape),
        summed_grads[0],
        summed_grads[1],
        summed_grads[2],
        summed_grads[3],
        summed_grads[4],
        table_grad,
        summed_grads[5],
        summed_grads[6],
        summed_grads[7],
        summed_grads[8],
    )


def solution(mesh):
    in_specs = (
        P("tower", "rows", None, None),
        P("tower", "rows", None),
        P("rows"),
        P(),
        P(),
        P(),
        P(),
        P(),
        P(),
        P(),
        P(),
        P(),
        P(),
    )
    out_specs = (
        P("tower", "rows", None),
        P("rows", "tower", None),
        P("tower", "rows", None, None),
        P("rows"),
        P("rows", None),
        P("rows", None),
        P("rows", None),
        P("rows", None),
        P(),
        P("rows"),
        P("rows", None),
        P("rows", None),
        P("rows"),
    )
    axes = rows_axes(mesh)
    sized = mesh.shape["tower"] == 2 and tuple(ax.size for ax in axes) == STEPS_SIZES
    body = functools.partial(fused, axes) if sized else on_device
    return jax.shard_map(
        body, mesh=mesh, in_specs=in_specs, out_specs=out_specs, check_vma=False
    )
```

```python
import functools
import math

import jax
import jax.numpy as jnp
import numpy as np
from jax import lax
from jax.experimental import pallas as pl
from jax.experimental.pallas import tpu as pltpu
from jax.sharding import PartitionSpec as P

BUCKETS = 32
MAX_DIST = 128
ITEM_ROW = 8
BLOCK = 128

epsilon = 1e-06
logit_divisor = 0.01
loss_scale = 16.0
far_below = -1000000000.0
exact = lax.Precision.HIGHEST
gelu_cubic = 0.044715
gelu_factor = math.sqrt(2.0 / math.pi)
f32 = jnp.float32
bf16 = jnp.bfloat16
VMEM = pltpu.VMEM
VMEM_LIMIT = 62 * 2**20


def dot_nn(a, b, precision=None):
    return lax.dot_general(
        a, b, (((1,), (0,)), ((), ())), precision=precision, preferred_element_type=f32
    )


def dot_nt(a, b, precision=None):
    return lax.dot_general(
        a, b, (((1,), (1,)), ((), ())), precision=precision, preferred_element_type=f32
    )


def dot_tn(a, b, precision=None):
    return lax.dot_general(
        a, b, (((0,), (0,)), ((), ())), precision=precision, preferred_element_type=f32
    )


def bucket_of(relative, bucket_count, max_distance):
    half_count = bucket_count // 2
    exact_count = half_count // 2
    log_steps = half_count - exact_count
    bounds = []
    for section_index in range(1, log_steps):
        target = exact_count ** (log_steps - section_index) * max_distance**section_index
        lowest = exact_count
        while lowest**log_steps < target:
            lowest = lowest + 1
        bounds.append(lowest)
    distance = abs(relative)
    bucket = half_count if relative > 0 else 0
    if distance < exact_count:
        return bucket + distance
    return bucket + exact_count + len([b for b in bounds if distance >= b])


def lane_buckets():
    width = 4 * BLOCK
    onehot = np.zeros((BUCKETS, width), np.float32)
    for m in range(width):
        relative = (m if m < 3 * BLOCK else m - width) - BLOCK
        onehot[bucket_of(relative, BUCKETS, MAX_DIST), m] = 1.0
    return onehot


def row_of_gain(ref):
    return ref[...].astype(f32).reshape(1, ref.shape[0])


def rms_inverse(values):
    return lax.rsqrt(jnp.mean(values * values, axis=-1, keepdims=True) + epsilon)


def column_of(row):
    return jnp.broadcast_to(row, (8, row.shape[1])).T[:, 0:1]


def key_range(block, blocks):
    return max(block - 1, 0) * BLOCK, min(block + 2, blocks) * BLOCK


MESH_IDS = pl.DeviceIdType.MESH
OUT, IN, ATTN, VALUE, QUERY, KEY = range(6)
OWN, END, SEND = 3, 4, 5
SPAN = 384
INNER, TWO, ATTENDED, HEADS, NORMED, ONE, SMALL = range(7)


class Axis:

    def __init__(self, size, stride):
        self.size, self.stride = size, stride

    def place(self, row):
        return lax.rem(lax.div(row, self.stride), self.size)


UNIT = 128
SLOTS = 3
JOBS = (
    ((2, 0, 1), ((OUT, 0, 0), (OUT, 0, 1),)),
    ((0, 2, 1), ((OUT, 0, 2), (OUT, 0, 3),)),
    ((0, 2, 1), ((OUT, 1, 0), (OUT, 1, 1),)),
    ((0, 1, 2), ((OUT, 1, 2), (OUT, 1, 3),)),
    ((1, 2, 0), ((OUT, 2, 0), (OUT, 2, 1), (OUT, 2, 2), (OUT, 2, 3),)),
    ((1, 0, 2), ((IN, 0, 0), (IN, 1, 0), (IN, 2, 0), (IN, 3, 0),)),
    ((0, 1, 2), ((IN, 4, 0), (IN, 5, 0), (IN, 6, 0), (IN, 7, 0),)),
    ((2, 0, 1), ((IN, 8, 0), (IN, 9, 0), (IN, 10, 0), (IN, 11, 0),)),
    ((0, 1, 2), ((ATTN, 0, 0), (ATTN, 1, 0), (ATTN, 2, 0),)),
    ((1, 0, 2), ((VALUE, 0, 0), (QUERY, 0, 0), (KEY, 0, 0),)),
    ((0, 1, 2), ((VALUE, 1, 0), (QUERY, 1, 0), (KEY, 1, 0),)),
    ((1, 2, 0), ((VALUE, 2, 0),)),
    ((1, 2, 0), ((QUERY, 2, 0),)),
    ((0, 1, 2), ((KEY, 2, 0),)),
)
STEPS_SIZES = (2, 2, 4)
STEPS = (
    (0, SEND, 0), (2, SEND, 0), (0, OWN, 0), (0, 0, 0), (2, OWN, 0), (2, 0, 0), (4, SEND, 0), (1, SEND, 0),
    (3, SEND, 0), (4, OWN, 0), (4, 0, 0), (1, OWN, 0), (1, 0, 0), (3, OWN, 0), (3, 0, 0), (0, 0, 1),
    (-1, INNER, 0), (2, 0, 1), (2, 1, 0), (-1, INNER, 1), (-1, INNER, 2), (-1, INNER, 3), (0, 0, 2),
    (-1, INNER, 4), (-1, INNER, 5), (2, 1, 1), (5, SEND, 0), (1, 0, 1), (1, 1, 0), (6, SEND, 0), (0, 0, 3),
    (0, 1, 0), (2, 1, 2), (5, OWN, 0), (5, 0, 0), (7, SEND, 0), (4, 0, 1), (4, 1, 0), (1, 1, 1), (6, OWN, 0),
    (6, 0, 0), (3, 0, 1), (3, 1, 0), (7, OWN, 0), (7, 0, 0), (0, 1, 1), (0, 2, 0), (1, 1, 2), (2, 1, 3),
    (2, 2, 0), (-1, TWO, 0), (1, 1, 3), (1, 2, 0), (4, 1, 1), (8, SEND, 0), (-1, NORMED, 0),
    (-1, ATTENDED, 0), (-1, HEADS, 0), (5, 0, 1), (5, 1, 0), (8, OWN, 0), (8, 0, 0), (4, 1, 2), (3, 1, 1),
    (3, 2, 0), (-1, HEADS, 3), (1, 2, 1), (0, 2, 1), (6, 0, 1), (6, 1, 0), (2, 2, 1), (1, END, 0),
    (0, END, 0), (9, SEND, 0), (4, 1, 3), (4, 2, 0), (2, END, 0), (-1, HEADS, 1), (9, OWN, 0), (9, 0, 0),
    (5, 1, 1), (5, 2, 0), (7, 0, 1), (-1, HEADS, 4), (6, 1, 1), (6, 2, 0), (10, SEND, 0), (-1, HEADS, 2),
    (10, OWN, 0), (10, 0, 0), (-1, HEADS, 5), (3, 2, 1), (8, 0, 1), (8, 1, 0), (7, 0, 2), (11, SEND, 0),
    (4, 2, 1), (12, SEND, 0), (13, SEND, 0), (11, OWN, 0), (11, 0, 0), (9, 0, 1), (9, 1, 0), (12, OWN, 0),
    (12, 0, 0), (13, OWN, 0), (13, 0, 0), (5, 2, 1), (4, END, 0), (-1, ONE, 0), (3, 2, 2), (-1, SMALL, 0),
    (8, 1, 1), (8, 2, 0), (6, 2, 1), (-1, SMALL, 1), (5, 2, 2), (3, 2, 3), (7, 0, 3), (7, 1, 0), (3, END, 0),
    (10, 0, 1), (10, 1, 0), (11, 0, 1), (11, 1, 0), (6, 2, 2), (8, 2, 1), (5, 2, 3), (5, END, 0), (6, 2, 3),
    (8, 2, 2), (12, 0, 1), (12, 1, 0), (11, 1, 1), (6, END, 0), (9, 1, 1), (9, 2, 0), (8, 2, 3), (11, 1, 2),
    (12, 1, 1), (8, END, 0), (11, 1, 3), (11, 2, 0), (12, 1, 2), (13, 0, 1), (13, 1, 0), (12, 1, 3),
    (12, 2, 0), (9, 2, 1), (10, 1, 1), (10, 2, 0), (9, 2, 2), (13, 1, 1), (13, 2, 0), (-1, SMALL, 2),
    (9, 2, 3), (7, 1, 1), (7, 2, 0), (10, 2, 1), (11, 2, 1), (9, END, 0), (12, 2, 1), (11, END, 0),
    (12, END, 0), (13, 2, 1), (7, 2, 1), (10, 2, 2), (7, END, 0), (13, 2, 2), (10, 2, 3), (13, 2, 3),
    (10, END, 0), (-1, SMALL, 3), (13, END, 0),
)


def layer_kernel(axes, *refs):
    jobs = len(JOBS)
    (
        x_ref, seg_ref, pos_ref, g1_ref, g2_ref, g3_ref, table_ref, lanes_ref,
        wq_h, wk_h, wv_h, wo_h, w1_h, w2_h,
        emb_o, loss_o, small_o, gh_o, inner_o,
    ) = refs[:19]
    res, refs = refs[19 : 19 + jobs], refs[19 + jobs :]
    (
        all_e, gs, hid, ig, chunk, wslot, q, k, v, att, nrm, br2, br1, mid, fin, by_offset, d_all,
        sm, sm_core, sm_plane, sm_line, stg,
    ) = refs[:22]
    accs, landings, refs = refs[22 : 22 + jobs], refs[22 + jobs : 22 + 4 * jobs], refs[22 + 4 * jobs :]
    load_sem, ag_s, ag_r, sm_s, sm_r, tow_s, tow_r, end_s, end_r, end_l, line_s, line_r = refs

    t = lax.axis_index("tower")
    row = lax.axis_index("rows")
    place = [ax.place(row) for ax in axes]
    nx, ny, nz = (ax.size for ax in axes)
    sx, sy, sz = (ax.stride for ax in axes)
    plane_size = nx * ny
    plane = place[1] * nx + place[0]
    spot = plane * nz + place[2]

    def row_of(w, z):
        return lax.rem(w, nx) * sx + lax.div(w, nx) * sy + z * sz

    z_peers = [(t, row_of(plane, lax.rem(place[2] + m, nz))) for m in range(1, nz)]
    plane_peers = [(t, row_of(lax.rem(plane + m, plane_size), place[2])) for m in range(1, plane_size)]
    partner = (1 - t, row)

    barrier = pltpu.get_barrier_semaphore()
    for peer in z_peers + plane_peers + [partner]:
        pl.semaphore_signal(barrier, inc=1, device_id=peer, device_id_type=MESH_IDS)

    def load(i, src, dst):
        return pltpu.make_async_copy(src, dst, load_sem.at[i])

    def remote(src, dst, ss, rs, to):
        return pltpu.make_async_remote_copy(
            src_ref=src, dst_ref=dst, send_sem=ss, recv_sem=rs, device_id=to, device_id_type=MESH_IDS
        )

    seq, width = x_ref.shape
    heads = table_ref.shape[0]
    ff = hid.shape[1]
    piece = 512
    pieces = ff // piece
    blocks = seq // BLOCK
    tail = width - seq
    square_loads = [
        load(i, w, wslot.at[pl.ds(i * width, width)]) for i, w in enumerate((wq_h, wk_h, wv_h, wo_h))
    ]
    ahead_loads = [load(4, w1_h.at[pl.ds(0, seq)], ig)]
    tails = []
    for c in range(ff // width):
        held = (br2 if c < 2 else br1).at[pl.ds(c % 2 * tail, tail)]
        tails.append(held)
        ahead_loads.append(load(5 + c, w1_h.at[pl.ds(seq, tail), pl.ds(c * width, width)], held))
    w2_load = load(9, w2_h, wslot)
    back_loads = [
        load(10 + c, w1_h.at[:, pl.ds(c * width, width)], wslot.at[pl.ds(c * width, width)])
        for c in range(ff // width)
    ]
    gh_store = load(14, fin, gh_o)
    kept = [load(15 + c, chunk.at[c % 2], inner_o.at[:, pl.ds(c * piece, piece)]) for c in range(pieces - 2)]
    fetched = [load(15 + c, inner_o.at[:, pl.ds(c * piece, piece)], chunk.at[c % 2]) for c in range(pieces - 2)]
    for w in square_loads[:3]:
        w.start()

    def normed(values, gain_ref):
        return ((values * rms_inverse(values)) * row_of_gain(gain_ref)).astype(bf16)

    nrm[...] = normed(x_ref[...].astype(f32), g1_ref)
    square_loads[3].start()
    for w in ahead_loads:
        w.start()
    for i, out in enumerate((q, k, v)):
        square_loads[i].wait()
        out[...] = dot_nn(nrm[...], wslot[i * width : (i + 1) * width, :]).astype(bf16)

    seg_row = seg_ref[...].astype(f32)
    low_half = lax.broadcasted_iota(jnp.int32, (BLOCK, BLOCK), 1) < BLOCK // 2

    def bias_tile(h, first, last):
        n = h % 4 * BLOCK
        if h < 8:
            lane = h // 4 * 3 * BLOCK
            return fin[n : n + BLOCK, lane + first : lane + last]
        return chunk[0, n : n + BLOCK, first:last]

    def build_tiles():
        by_offset[0:heads, :] = dot_nn(table_ref[...], lanes_ref[...])
        for h in range(heads):
            spread = jnp.broadcast_to(by_offset[h : h + 1, :], (BLOCK, 4 * BLOCK))
            tile = pltpu.roll(spread, 0, 1, stride=1, stride_axis=0)[:, : 3 * BLOCK]
            n = h % 4 * BLOCK
            if h < 8:
                lane = h // 4 * 3 * BLOCK
                fin[n : n + BLOCK, lane : lane + 3 * BLOCK] = tile
            else:
                chunk[0, n : n + BLOCK, 0 : 3 * BLOCK] = tile
        seg_col = column_of(seg_row)
        for b in range(blocks):
            lo, hi = key_range(b, blocks)
            first = lo - (b - 1) * BLOCK
            same = seg_col[b * BLOCK : (b + 1) * BLOCK] == seg_row[:, lo:hi]
            chunk[1, b * BLOCK : (b + 1) * BLOCK, first : first + hi - lo] = jnp.where(same, 0.0, far_below)

    def two_heads(values):
        zero = jnp.zeros_like(values)
        return jnp.concatenate([jnp.where(low_half, values, zero), jnp.where(low_half, zero, values)], axis=0)

    def probabilities(pair, b, both, keys):
        lo, hi = key_range(b, blocks)
        first = lo - (b - 1) * BLOCK
        last = first + hi - lo
        mask = chunk[1, b * BLOCK : (b + 1) * BLOCK, first:last]
        s = dot_nt(both, keys)
        parts = []
        for e in range(2):
            part = s[e * BLOCK : (e + 1) * BLOCK] + bias_tile(2 * pair + e, first, last) + mask
            terms = jnp.exp(part - jnp.max(part, axis=-1, keepdims=True))
            parts.append(terms * (1.0 / jnp.sum(terms, axis=-1, keepdims=True)))
        return parts

    build_tiles()
    for pair in range(heads // 2):
        lanes = slice(pair * UNIT, (pair + 1) * UNIT)
        for b in range(blocks):
            lo, hi = key_range(b, blocks)
            mine = slice(b * BLOCK, (b + 1) * BLOCK)
            parts = probabilities(pair, b, two_heads(q[mine, lanes]), k[lo:hi, lanes])
            probs = jnp.concatenate([part.astype(bf16) for part in parts], axis=0)
            out = dot_nn(probs, v[lo:hi, lanes])
            att[mine, lanes] = jnp.where(low_half, out[:BLOCK], out[BLOCK:]).astype(bf16)

    square_loads[3].wait()
    middle = x_ref[...].astype(f32) + dot_nn(att[...], wslot[3 * width : 4 * width, :])
    w2_load.start()
    mid[...] = middle
    nrm[...] = normed(middle, g2_ref)
    for w in ahead_loads:
        w.wait()
    for c in range(pieces):
        low = c * piece
        inner = dot_nn(nrm[:, 0:seq], ig[:, low : low + piece])
        rest = []
        while low < (c + 1) * piece:
            n = low // width
            high = min((c + 1) * piece, (n + 1) * width)
            rest.append(dot_nn(nrm[:, seq:width], tails[n][:, low - n * width : high - n * width]))
            low = high
        inner = inner + (jnp.concatenate(rest, axis=1) if len(rest) > 1 else rest[0])
        if c >= 2:
            kept[c - 2].wait()
        chunk[c % 2] = inner
        if c < pieces - 2:
            kept[c].start()
        tangent = jnp.tanh(gelu_factor * (inner + gelu_cubic * (inner * inner * inner)))
        hid[:, c * piece : (c + 1) * piece] = (inner * (0.5 * (1.0 + tangent))).astype(bf16)
    w2_load.wait()
    final = mid[...] + dot_nn(hid[...], wslot[...])
    fin[...] = final
    member = (lax.broadcasted_iota(jnp.int32, (ITEM_ROW, seq), 0).astype(f32) == seg_row).astype(f32)
    counts = jnp.sum(member, axis=-1, keepdims=True)
    pooled = dot_nn(member, (final * rms_inverse(final)) * row_of_gain(g3_ref), exact) / counts

    inverse_pool = lax.rsqrt(jnp.sum(pooled * pooled, axis=-1, keepdims=True) + epsilon)
    own_e = pooled * inverse_pool
    emb_o[...] = own_e
    own_rows = pl.ds(pl.multiple_of(spot * ITEM_ROW, ITEM_ROW), ITEM_ROW)

    def bits(n):
        return n.bit_length() - 1

    p = pos_ref[...]
    of_row = p >> bits(ITEM_ROW)

    def along(ax):
        return (of_row >> bits(ax.stride)) & (ax.size - 1)

    p = ((along(axes[1]) * nx + along(axes[0])) * nz + along(axes[2])) * ITEM_ROW + (p & (ITEM_ROW - 1))
    i8 = lax.broadcasted_iota(jnp.int32, (ITEM_ROW, ITEM_ROW), 0)
    j8 = lax.broadcasted_iota(jnp.int32, (ITEM_ROW, ITEM_ROW), 1)
    diag = jnp.where(i8 == j8, jnp.broadcast_to(p.astype(f32), (ITEM_ROW, ITEM_ROW)), 0.0)
    pos_col = jnp.sum(diag, axis=-1, keepdims=True)
    all_e[t, own_rows, 0:width] = own_e
    all_e[t, own_rows, width : width + UNIT] = jnp.broadcast_to(pos_col, (ITEM_ROW, UNIT))

    pl.semaphore_wait(barrier, len(z_peers) + len(plane_peers) + 1)

    def column_rows(w):
        return pl.ds(pl.multiple_of(w * (nz * ITEM_ROW), ITEM_ROW), nz * ITEM_ROW)

    first = []
    for m, peer in enumerate(z_peers):
        block = all_e.at[t, own_rows]
        first.append(remote(block, block, ag_s.at[m], ag_r.at[m], peer))
        first[-1].start()
    inverse = rms_inverse(fin[...])
    sm[...] = jnp.zeros_like(sm)
    for c in first:
        c.wait_recv()
    n1 = len(z_peers)
    second = []
    mine = all_e.at[t, column_rows(plane)]
    for m, peer in enumerate(plane_peers):
        second.append(remote(mine, mine, ag_s.at[n1 + m], ag_r.at[n1 + m], peer))
        second[-1].start()
    n2 = n1 + len(plane_peers)
    third = [remote(mine, mine, ag_s.at[n2], ag_r.at[n2], partner)]
    third[0].start()
    for m in range(1, plane_size):
        second[m - 1].wait_recv()
        block = all_e.at[t, column_rows(lax.rem(plane + plane_size - m, plane_size))]
        third.append(remote(block, block, ag_s.at[n2 + m], ag_r.at[n2 + m], partner))
        third[-1].start()
    for c in third:
        c.wait_recv()
    sent = first + second + third

    queries, docs = all_e[0, :, 0:width], all_e[1, :, 0:width]
    items = queries.shape[0]
    scores = dot_nt(queries, docs, exact) / logit_divisor
    top = jnp.max(scores, axis=1, keepdims=True)
    terms = jnp.exp(scores - top)
    summed = jnp.sum(terms, axis=1, keepdims=True)
    chosen = (
        lax.broadcasted_iota(jnp.int32, (items, items), 1).astype(f32) == all_e[0, :, width : width + 1]
    ).astype(f32)
    slope = loss_scale * (terms / summed - chosen)

    @pl.when(t == 0)
    def _():
        gs[...] = slope

    @pl.when(t == 1)
    def _():
        gs[...] = slope.T

    embed_grad = dot_nn(gs[own_rows, :], all_e[1 - t, :, 0:width], exact) / logit_divisor
    inner_dot = jnp.sum(own_e * embed_grad, axis=-1, keepdims=True)
    pooled_grad = inverse_pool * (embed_grad - own_e * inner_dot)

    three_grad = dot_tn(member, pooled_grad / counts, exact)
    unit = fin[...] * inverse
    sm[0:1, 0:width] = jnp.sum(three_grad * unit, axis=0, keepdims=True)
    u = three_grad * row_of_gain(g3_ref)
    final_grad = inverse * (u - unit * jnp.mean(u * unit, axis=-1, keepdims=True))
    fin[...] = final_grad
    br2[...] = final_grad.astype(bf16)

    def write_losses():
        losses = top + jnp.log(summed) - jnp.sum(scores * chosen, axis=1, keepdims=True)
        loss_row = jnp.broadcast_to(losses, (items, UNIT)).T[0:8, :]
        pick = (
            lax.broadcasted_iota(jnp.int32, (items, UNIT), 0)
            == lax.broadcasted_iota(jnp.int32, (items, UNIT), 1) + spot * ITEM_ROW + t * (ITEM_ROW // 2)
        ).astype(f32)
        loss_o[...] = dot_nn(loss_row, pick, exact)

    chunk_rows = width // (nx * ny * nz)
    lefts = (hid, nrm, att, nrm, nrm, nrm)
    rights = (br2, ig, br1, v, q, k)
    in_slot = {}
    unwaited = []

    def spots(path):
        found = {}
        for r in range(nx * ny * nz):
            number = 0
            for a in path:
                number = number * axes[a].size + (r // axes[a].stride) % axes[a].size
            found[r] = number * chunk_rows
        return found

    def product(job, half, keep):
        path, parts = JOBS[job]
        lhs = lefts[parts[0][0]]
        stripes = list(dict.fromkeys((target, block) for target, block, _ in parts))
        subs = lhs.shape[1] // width
        group = SPAN // (subs * chunk_rows)
        where = spots(path)

        def step(i, carry):
            right = []
            for target, block in stripes:
                rhs = rights[target]
                lane = half * (rhs.shape[1] // 2) + block * UNIT
                right.append(rhs[:, pl.ds(pl.multiple_of(lane, UNIT), UNIT)])
            columns = pl.ds(pl.multiple_of(i * SPAN, UNIT), SPAN)
            value = dot_tn(lhs[:, columns], jnp.concatenate(right, axis=1) if len(right) > 1 else right[0])
            moved = sum(lax.rem(lax.div(i * group, ax.stride), ax.size) * where[ax.stride] for ax in axes)
            for r in range(group):
                at_row = pl.multiple_of(moved + where[r], 8)
                for n, (target, block, sub) in enumerate(parts):
                    low = (r * subs + sub) * chunk_rows
                    lane = stripes.index((target, block)) * UNIT
                    keep(n, pl.ds(at_row, chunk_rows), value[low : low + chunk_rows, lane : lane + UNIT])
            return carry

        lax.fori_loop(0, lhs.shape[1] // SPAN, step, 0, unroll=2 if subs > 1 else 1)

    def tower_copy(job, slot):
        units = len(JOBS[job][1])
        return remote(stg.at[slot, pl.ds(0, units)], accs[job], tow_s.at[job], tow_r.at[job], partner)

    def send_half(job):
        slot = len(in_slot) % SLOTS
        before = [n for n, s in in_slot.items() if s == slot]
        if before:
            tower_copy(before[-1], slot).wait_send()
            unwaited.remove(before[-1])

        def keep(n, rows, value):
            stg[slot, n, rows, :] = value

        product(job, 1 - t, keep)
        tower_copy(job, slot).start()
        in_slot[job] = slot
        unwaited.append(job)

    def take_own(job):
        acc = accs[job]
        tower_copy(job, 0).wait_recv()

        def keep(n, rows, value):
            acc[n, rows, :] = acc[n, rows, :] + value

        product(job, t, keep)

    def geometry(job, leg):
        path = JOBS[job][0]
        low, size = 0, width
        for a in path[:leg]:
            size = size // axes[a].size
            low = low + place[a] * size
        return low, size // axes[path[leg]].size, axes[path[leg]], place[path[leg]]

    def line_copy(job, leg, i, block):
        low, size, axis, _ = geometry(job, leg)
        n = axis.size
        if block > i:
            to, slot = (t, row + axis.stride), (0 if n == 2 else block)
        else:
            to, slot = (t, row - axis.stride), (0 if n == 2 else n if block == i - 1 else block)
        at_row = pl.multiple_of(low + block * size, 8)
        return remote(
            accs[job].at[:, pl.ds(at_row, size)], landings[3 * job + leg].at[slot],
            line_s.at[job, leg, block], line_r.at[job, leg, slot], to,
        )

    def take(job, leg, block, slot):
        low, size, axis, _ = geometry(job, leg)
        at_row = pl.multiple_of(low + block * size, 8)
        acc, landed = accs[job], landings[3 * job + leg]
        remote(
            landed.at[slot], landed.at[slot], line_s.at[job, leg, block], line_r.at[job, leg, slot], partner
        ).wait_recv()
        acc[:, pl.ds(at_row, size), :] = acc[:, pl.ds(at_row, size), :] + landed[slot]

    def line_step(job, leg, s):
        _, _, axis, my_place = geometry(job, leg)
        n = axis.size
        for i in range(n):
            from_left = s == i and i < n - 1
            from_right = s == n - 1 - i and i > 0
            last = s == n - 1
            if not (from_left or from_right or last):
                continue

            @pl.when(my_place == i)
            def _():
                if from_left:
                    for block in range(n - 1, i, -1):
                        if i > 0:
                            take(job, leg, block, block)
                        line_copy(job, leg, i, block).start()
                if from_right:
                    for block in range(i):
                        if i < n - 1:
                            take(job, leg, block, block)
                        line_copy(job, leg, i, block).start()
                if last:
                    if n == 2:
                        take(job, leg, i, 0)
                    else:
                        if i > 0:
                            take(job, leg, i, i)
                        if i < n - 1:
                            take(job, leg, i, n)

        if s == n - 1 and leg == 2:
            end_copy(job, True).start()
            end_copy(job, False).start()

    def line_drain(job, leg):
        _, _, axis, my_place = geometry(job, leg)
        for i in range(axis.size):

            @pl.when(my_place == i)
            def _():
                for block in range(axis.size):
                    if block != i:
                        line_copy(job, leg, i, block).wait_send()

    def end_copy(job, to_partner):
        low, size, _, my_place = geometry(job, 2)
        at_row = pl.multiple_of(low + my_place * size, 8)
        src, dst = accs[job].at[:, pl.ds(at_row, size)], res[job].at[t]
        if to_partner:
            return remote(src, dst, end_s.at[job], end_r.at[job], partner)
        return pltpu.make_async_copy(src, dst, end_l.at[job])

    def inner_step(n):
        c = (n + pieces - 2) % pieces
        if n >= 2:
            fetched[c].wait()
        v_in = chunk[c % 2]
        grad = dot_nt(br2[...], wslot[c * piece : (c + 1) * piece, :])
        tangent = jnp.tanh(gelu_factor * (v_in + gelu_cubic * (v_in * v_in * v_in)))
        ahead = 0.5 * (1.0 + tangent) + 0.5 * v_in * (1.0 - tangent * tangent) * gelu_factor * (
            1.0 + 3.0 * gelu_cubic * v_in * v_in
        )
        ig[:, c * piece : (c + 1) * piece] = (grad * ahead).astype(bf16)
        if n + 2 < pieces:
            fetched[n].start()
        if n == pieces - 1:
            for w in back_loads:
                w.start()

    def norm_back(grad, values, gain):
        inverse = rms_inverse(values)
        unit = values * inverse
        total = jnp.sum(grad * unit, axis=0, keepdims=True)
        w = grad * gain
        return inverse * (w - unit * jnp.mean(w * unit, axis=-1, keepdims=True)), total

    tokens = 256

    def two_step():
        for w in back_loads:
            w.wait()
        gain = row_of_gain(g2_ref)
        for low in range(0, seq, tokens):
            part = slice(low, low + tokens)
            grad = dot_nt(ig[part, 0:width], wslot[0:width, :])
            for c in range(1, ff // width):
                lanes = slice(c * width, (c + 1) * width)
                grad = grad + dot_nt(ig[part, lanes], wslot[lanes, :])
            back, total = norm_back(grad, mid[part, :], gain)
            sm[1:2, 0:width] = sm[1:2, 0:width] + total
            middle_grad = fin[part, :] + back
            mid[part, :] = middle_grad
            br1[part, :] = middle_grad.astype(bf16)
        for w in square_loads:
            w.start()
        build_tiles()

    def attended_step():
        for w in square_loads:
            w.wait()
        br2[...] = dot_nt(br1[...], wslot[3 * width : 4 * width, :]).astype(bf16)
        d_all[...] = jnp.zeros_like(d_all)

    turned = [lax.broadcasted_iota(jnp.int32, (BLOCK, BLOCK), n) for n in range(2)]
    upside = (turned[0] + turned[1] == BLOCK - 1).astype(bf16)

    def upside_down(values):
        high = values.astype(bf16)
        rest = values - high.astype(f32)
        middle_part = rest.astype(bf16)
        low_part = (rest - middle_part.astype(f32)).astype(bf16)
        return dot_nn(upside, high) + (dot_nn(upside, middle_part) + dot_nn(upside, low_part))

    def heads_step(pair):
        lanes = slice(pair * UNIT, (pair + 1) * UNIT)
        columns = [[None] * 3, [None] * 3]
        key_grads, value_grads = [None] * blocks, [None] * blocks

        def put(held, n, value):
            held[n] = value if held[n] is None else held[n] + value

        for b in range(blocks):
            lo, hi = key_range(b, blocks)
            mine = slice(b * BLOCK, (b + 1) * BLOCK)
            first = lo - (b - 1) * BLOCK
            keys = k[lo:hi, lanes]
            both_q, both_o = two_heads(q[mine, lanes]), two_heads(br2[mine, lanes])
            probs = probabilities(pair, b, both_q, keys)
            pg = dot_nt(both_o, v[lo:hi, lanes])
            grads = []
            for e in range(2):
                ds = pg[e * BLOCK : (e + 1) * BLOCK]
                ds = probs[e] * (ds - jnp.sum(probs[e] * ds, axis=-1, keepdims=True))
                for n in range((hi - lo) // BLOCK):
                    put(columns[e], first // BLOCK + n, ds[:, n * BLOCK : (n + 1) * BLOCK])
                grads.append(ds.astype(bf16))
            rounded = jnp.concatenate(grads, axis=0)
            dq = dot_nn(rounded, keys)
            dk = dot_tn(rounded, both_q)
            dv = dot_tn(jnp.concatenate([part.astype(bf16) for part in probs], axis=0), both_o)
            for n in range((hi - lo) // BLOCK):
                rows = slice(n * BLOCK, (n + 1) * BLOCK)
                put(key_grads, lo // BLOCK + n, dk[rows])
                put(value_grads, lo // BLOCK + n, dv[rows])
            q[mine, lanes] = jnp.where(low_half, dq[:BLOCK], dq[BLOCK:]).astype(bf16)
        for b in range(blocks):
            mine = slice(b * BLOCK, (b + 1) * BLOCK)
            k[mine, lanes] = key_grads[b].astype(bf16)
            v[mine, lanes] = value_grads[b].astype(bf16)
        for e in range(2):
            wide = jnp.concatenate(columns[e] + [jnp.zeros((BLOCK, BLOCK), f32)], axis=1)
            skewed = pltpu.roll(upside_down(wide), 3 * BLOCK + 1, 1, stride=1, stride_axis=0)
            d_all[2 * pair + e : 2 * pair + e + 1, :] = jnp.sum(skewed, axis=0, keepdims=True)

    def normed_step():
        nrm[...] = normed(x_ref[...].astype(f32), g1_ref)

    def one_step():
        gain = row_of_gain(g1_ref)
        for low in range(0, seq, tokens):
            part = slice(low, low + tokens)
            grad = dot_nt(q[part, :], wslot[0:width, :])
            grad = grad + dot_nt(k[part, :], wslot[width : 2 * width, :])
            grad = grad + dot_nt(v[part, :], wslot[2 * width : 3 * width, :])
            back, total = norm_back(grad, x_ref[part, :].astype(f32), gain)
            sm[2:3, 0:width] = sm[2:3, 0:width] + total
            fin[part, :] = mid[part, :] + back
        gh_store.start()
        write_losses()

    small_first = remote(sm, sm_core, sm_s.at[0], sm_r.at[0], partner)
    base = 1 + len(plane_peers)
    own_plane, own_line = sm_plane.at[plane], sm_line.at[place[2]]
    small_second = [
        remote(own_plane, own_plane, sm_s.at[1 + m], sm_r.at[1 + m], peer) for m, peer in enumerate(plane_peers)
    ]
    small_third = [
        remote(own_line, own_line, sm_s.at[base + m], sm_r.at[base + m], peer) for m, peer in enumerate(z_peers)
    ]

    def small_step(s):
        if s == 0:
            table_grad = dot_nt(d_all[...], lanes_ref[...].astype(f32), exact)
            for n in range(2):
                sm[:, width + n * UNIT : width + n * UNIT + BUCKETS] = table_grad[8 * n : 8 * n + 8, :]
            small_first.start()
        elif s == 1:
            small_first.wait()
            sm_plane[plane] = sm[...] + sm_core[...]
            for c in small_second:
                c.start()
        elif s == 2:
            for c in small_second:
                c.wait()
            total = sm_plane[0]
            for w in range(1, plane_size):
                total = total + sm_plane[w]
            sm_line[place[2]] = total
            for c in small_third:
                c.start()
        else:
            for c in small_third:
                c.wait()
            total = sm_line[0]
            for w in range(1, nz):
                total = total + sm_line[w]
            small_o[...] = total

    layer_steps = {
        INNER: inner_step, TWO: lambda n: two_step(), ATTENDED: lambda n: attended_step(), HEADS: heads_step,
        NORMED: lambda n: normed_step(), ONE: lambda n: one_step(), SMALL: small_step,
    }
    for job, leg, s in STEPS:
        if job < 0:
            layer_steps[leg](s)
        elif leg == SEND:
            send_half(job)
        elif leg == OWN:
            take_own(job)
        elif leg == END:
            end_copy(job, True).wait_recv()
            end_copy(job, False).wait()
        else:
            line_step(job, leg, s)
    for c in sent:
        c.wait_send()
    for job in unwaited:
        tower_copy(job, in_slot[job]).wait_send()
    for job in range(jobs):
        for leg in range(3):
            line_drain(job, leg)
        end_copy(job, True).wait_send()
    gh_store.wait()


def layer_call(axes, args):
    seq, width = args[0].shape
    ff = args[12].shape[1]
    nx, ny, nz = (ax.size for ax in axes)
    rows = nx * ny * nz
    chunk_rows = width // rows
    s = jax.ShapeDtypeStruct
    vm, hbm = pl.BlockSpec(memory_space=VMEM), pl.BlockSpec(memory_space=pl.ANY)
    small = (8, width + 2 * UNIT)
    most_units = max(len(parts) for _, parts in JOBS)
    outs = [
        s((ITEM_ROW, width), f32), s((8, UNIT), f32), s(small, f32), s((seq, width), f32), s((seq, ff), f32),
    ]
    outs += [s((2, len(parts), chunk_rows, UNIT), f32) for _, parts in JOBS]
    scratch = [
        VMEM((2, rows * ITEM_ROW, width + UNIT), f32), VMEM((rows * ITEM_ROW, rows * ITEM_ROW), f32),
        VMEM((seq, ff), bf16), VMEM((seq, ff), bf16), VMEM((2, seq, 512), f32), VMEM((ff, width), bf16),
    ]
    scratch += [VMEM((seq, width), bf16)] * 7 + [VMEM((seq, width), f32)] * 2
    scratch += [
        VMEM((16, 4 * BLOCK), f32), VMEM((16, 4 * BLOCK), f32),
        VMEM(small, f32), VMEM(small, f32), VMEM((nx * ny, *small), f32), VMEM((nz, *small), f32),
        VMEM((SLOTS, most_units, width, UNIT), f32),
    ]
    scratch += [VMEM((len(parts), width, UNIT), f32) for _, parts in JOBS]
    for path, parts in JOBS:
        size = width
        for a in path:
            n = axes[a].size
            size = size // n
            scratch.append(VMEM((1 if n == 2 else n + 1, len(parts), size, UNIT), f32))
    dma = pltpu.SemaphoreType.DMA
    jobs, most = len(JOBS), max(nx, ny, nz)
    gathers = nz - 1 + nx * ny - 1 + nx * ny
    smalls = nz + nx * ny - 1
    scratch += [
        dma((19,)), dma((gathers,)), dma((gathers,)), dma((smalls,)), dma((smalls,)),
        dma((jobs,)), dma((jobs,)), dma((jobs,)), dma((jobs,)), dma((jobs,)),
        dma((jobs, 3, most)), dma((jobs, 3, most + 1)),
    ]
    return pl.pallas_call(
        functools.partial(layer_kernel, axes),
        name="layer",
        out_shape=outs,
        in_specs=[vm] * 8 + [hbm] * 6,
        out_specs=[vm] * 3 + [hbm] * (2 + jobs),
        scratch_shapes=scratch,
        compiler_params=pltpu.CompilerParams(
            collective_id=0, has_side_effects=True, vmem_limit_bytes=VMEM_LIMIT
        ),
    )(*args)


def place_kernel(emb, loss, small, gh, *refs):
    res = refs[: len(JOBS)]
    (
        emb_o, loss_o, gh_o, attn_gain_o, query_o, key_o, value_o, attn_o, table_o, ffn_gain_o, in_o, out_o, final_gain_o,
    ) = refs[len(JOBS) :]
    row = lax.axis_index("rows")
    targets = (out_o, in_o, attn_o, value_o, query_o, key_o)
    emb_o[0] = emb[...]
    gh_o[0, 0] = gh[...]
    for job, (_, parts) in enumerate(JOBS):
        for n, (target, block, sub) in enumerate(parts):
            out, height = targets[target], res[job].shape[2]
            for t in range(2):
                low = t * (out.shape[1] // 2) + block * UNIT
                out[sub * height : (sub + 1) * height, low : low + UNIT] = res[job][t, n]
    loss_o[0] = loss[0:1, 0 : loss_o.shape[2]]
    width = gh.shape[1]
    share = attn_gain_o.shape[0]
    pick = (
        lax.broadcasted_iota(jnp.int32, (width, UNIT), 0)
        == lax.broadcasted_iota(jnp.int32, (width, UNIT), 1) + row * share
    ).astype(f32)
    gains = dot_nn(small[:, 0:width], pick, exact)
    for n, out in enumerate((final_gain_o, ffn_gain_o, attn_gain_o)):
        out[...] = gains[n, 0:share]
    heads = table_o.shape[0]
    for low in range(0, heads, 8):
        lane = width + low // 8 * UNIT
        high = min(low + 8, heads)
        table_o[low:high, :] = small[0 : high - low, lane : lane + BUCKETS]


def place_call(axes, heads, emb, loss, small, gh, res):
    seq, width = gh.shape
    ff = 4 * width
    rows = math.prod(a.size for a in axes)
    share = width // rows
    s = jax.ShapeDtypeStruct
    vm = pl.BlockSpec(memory_space=VMEM)
    weight = s((share, width), f32)
    outs = [
        s((1, *emb.shape), f32), s((1, 1, ITEM_ROW // 2), f32), s((1, 1, seq, width), f32), s((share,), f32),
        weight, weight, weight, weight, s((heads, BUCKETS), f32), s((share,), f32),
        s((share, ff), f32), s((ff // rows, width), f32), s((share,), f32),
    ]
    return pl.pallas_call(
        place_kernel,
        name="place",
        out_shape=outs,
        in_specs=[vm] * (4 + len(JOBS)),
        out_specs=[vm] * len(outs),
        compiler_params=pltpu.CompilerParams(vmem_limit_bytes=VMEM_LIMIT),
    )(emb, loss, small, gh, *res)


def rows_axes(mesh):
    rows = mesh.shape["rows"]
    line = mesh.devices.reshape(-1, rows)[0]
    places = [tuple(getattr(d, "coords", (i % 2, i // 2 % 2, i // 4))) for i, d in enumerate(line)]
    axes = []
    for n in range(3):
        values = sorted({p[n] for p in places})
        stride = next((i for i, p in enumerate(places) if p[n] != places[0][n]), 1)
        axes.append(Axis(len(values), stride))
    return tuple(axes)


def fused(
    axes, hidden_in, segment_ids, positives, attn_gain, w_query, w_key, w_value, w_attn_out, rel_table,
    ffn_gain, w_ffn_in, w_ffn_out, final_gain,
):
    seq, width = hidden_in.shape[2:]
    lanes = jnp.asarray(lane_buckets(), bf16)
    emb, loss, small, gh, _, *res = layer_call(
        axes,
        (
            hidden_in.reshape(seq, width), segment_ids.reshape(1, seq), positives.reshape(1, -1),
            attn_gain, ffn_gain, final_gain, rel_table.T, lanes,
            w_query, w_key, w_value, w_attn_out, w_ffn_in, w_ffn_out,
        ),
    )
    outs = list(place_call(axes, rel_table.shape[1], emb, loss, small, gh, res))
    outs[8] = outs[8].T
    return tuple(outs)


def from_partner(block, axis, bit):
    count = lax.axis_size(axis)
    route = []
    for low in range(count):
        high = low | 1 << bit
        if high != low and high < count:
            route += [(low, high), (high, low)]
    return lax.ppermute(block, axis, route)


def bucket_onehot(seq_len, bucket_count, max_distance):
    half_count = bucket_count // 2
    exact_count = half_count // 2
    log_steps = half_count - exact_count
    bounds = []
    for section_index in range(1, log_steps):
        target = exact_count ** (log_steps - section_index) * max_distance**section_index
        lowest = exact_count
        while lowest**log_steps < target:
            lowest = lowest + 1
        bounds.append(lowest)
    onehot = np.zeros((2 * seq_len - 1, bucket_count), np.float32)
    for offset in range(2 * seq_len - 1):
        relative = offset - (seq_len - 1)
        distance = abs(relative)
        bucket = half_count if relative > 0 else 0
        if distance < exact_count:
            bucket = bucket + distance
        else:
            bucket = (
                bucket
                + exact_count
                + len([boundary for boundary in bounds if distance >= boundary])
            )
        onehot[offset, bucket] = 1.0
    return onehot


def matmul(left_side, right_side):
    return jnp.dot(left_side, right_side, preferred_element_type=jnp.float32)


def contract_rows(left_side, right_side):
    return lax.dot_general(
        left_side, right_side, (((0,), (0,)), ((), ())), preferred_element_type=jnp.float32
    )


def contract_cols(left_side, right_side):
    return lax.dot_general(
        left_side, right_side, (((1,), (1,)), ((), ())), preferred_element_type=jnp.float32
    )


def gelu_slope(values):
    factor = math.sqrt(2.0 / math.pi)
    tangent = jnp.tanh(factor * (values + gelu_cubic * values * values * values))
    return 0.5 * (1.0 + tangent) + 0.5 * values * (1.0 - tangent * tangent) * factor * (
        1.0 + 3.0 * gelu_cubic * values * values
    )


def rms_parts(values):
    inverse = lax.rsqrt(jnp.mean(values * values, axis=-1, keepdims=True) + epsilon)
    return (values * inverse, inverse)


def rms_back(unit_grad, unit_values, inverse):
    return inverse * (
        unit_grad - unit_values * jnp.mean(unit_grad * unit_values, axis=-1, keepdims=True)
    )


def position_bias(rel_table, onehot, seq_len):
    head_count = rel_table.shape[1]
    by_offset = lax.dot_general(
        rel_table.astype(jnp.float32), onehot, (((0,), (1,)), ((), ())), precision=exact
    )
    rolled = jnp.concatenate([by_offset[:, seq_len - 1 :], by_offset[:, : seq_len - 1]], axis=1)
    repeated = jnp.tile(rolled, (1, seq_len))[:, : seq_len * (2 * seq_len - 2)]
    return repeated.reshape(head_count, seq_len, 2 * seq_len - 2)[:, :, :seq_len]


def diagonal_sums(matrix, seq_len):
    head_count = matrix.shape[0]
    flipped = matrix[:, :, ::-1]
    padded = jnp.pad(flipped, ((0, 0), (0, 0), (0, seq_len)))
    skewed = padded.reshape(head_count, 2 * seq_len * seq_len)[:, : seq_len * (2 * seq_len - 1)]
    skewed = skewed.reshape(head_count, seq_len, 2 * seq_len - 1)
    return jnp.sum(skewed, axis=1)[:, ::-1]


def on_device(
    hidden_in,
    segment_ids,
    positives,
    attn_gain,
    w_query,
    w_key,
    w_value,
    w_attn_out,
    rel_table,
    ffn_gain,
    w_ffn_in,
    w_ffn_out,
    final_gain,
):
    row_count = hidden_in.shape[1]
    seq_len = hidden_in.shape[2]
    model_width = hidden_in.shape[3]
    head_count = rel_table.shape[1]
    head_width = model_width // head_count
    token_count = row_count * seq_len
    tokens = hidden_in.reshape(token_count, model_width).astype(jnp.float32)
    segments = segment_ids.reshape(row_count, seq_len)
    gain_one = attn_gain.astype(jnp.float32)
    gain_two = ffn_gain.astype(jnp.float32)
    gain_three = final_gain.astype(jnp.float32)
    onehot = jnp.asarray(bucket_onehot(seq_len, BUCKETS, MAX_DIST))
    unit_one, inverse_one = rms_parts(tokens)
    normed_one = (unit_one * gain_one).astype(jnp.bfloat16)
    query_proj = matmul(normed_one, w_query).astype(jnp.bfloat16)
    key_proj = matmul(normed_one, w_key).astype(jnp.bfloat16)
    value_proj = matmul(normed_one, w_value).astype(jnp.bfloat16)
    bias_full = position_bias(rel_table, onehot, seq_len)

    def split_heads(values):
        return values.reshape(row_count, seq_len, head_count, head_width)

    def row_scores(row_query, row_key, row_seg):
        same_item = row_seg[:, None] == row_seg[None, :]
        similarity_table = jnp.einsum(
            "shd,thd->hst", row_query, row_key, preferred_element_type=jnp.float32
        )
        return jnp.where(same_item[None], similarity_table + bias_full, far_below)

    def forward_row(packed):
        row_query, row_key, row_value, row_seg = packed
        masked_scores = row_scores(row_query, row_key, row_seg)
        row_peak = jnp.max(masked_scores, axis=-1, keepdims=True)
        exp_terms = jnp.exp(masked_scores - row_peak)
        summed = jnp.sum(exp_terms, axis=-1, keepdims=True)
        attn_probs = (exp_terms / summed).astype(jnp.bfloat16)
        combined_attention_output = jnp.einsum(
            "hst,thd->shd", attn_probs, row_value, preferred_element_type=jnp.float32
        )
        return (
            combined_attention_output.astype(jnp.bfloat16),
            (row_peak + jnp.log(summed))[:, :, 0],
        )

    attended, log_norms = lax.map(
        forward_row,
        (split_heads(query_proj), split_heads(key_proj), split_heads(value_proj), segments),
    )
    attended = attended.reshape(token_count, model_width)
    middle = tokens + matmul(attended, w_attn_out)
    unit_two, inverse_two = rms_parts(middle)
    normed_two = (unit_two * gain_two).astype(jnp.bfloat16)
    inner = matmul(normed_two, w_ffn_in)
    hidden = jax.nn.gelu(inner, approximate=True).astype(jnp.bfloat16)
    final_sum = middle + matmul(hidden, w_ffn_out)
    unit_three, inverse_three = rms_parts(final_sum)
    normed_three = unit_three * gain_three
    member = (segments[:, None, :] == jnp.arange(ITEM_ROW, dtype=jnp.int32)[None, :, None]).astype(
        jnp.float32
    )
    counts = jnp.sum(member, axis=-1, keepdims=True)
    pooled = (
        jnp.einsum(
            "ris,rsd->rid",
            member,
            normed_three.reshape(row_count, seq_len, model_width),
            precision=exact,
        )
        / counts
    )
    item_count = row_count * ITEM_ROW
    pooled = pooled.reshape(item_count, model_width)
    inverse_pool = lax.rsqrt(jnp.sum(pooled * pooled, axis=-1, keepdims=True) + epsilon)
    encoded_vector_list = pooled * inverse_pool
    half_items = item_count // 2
    tower_index = lax.axis_index("tower")
    rows_size = lax.axis_size("rows")
    is_query = tower_index == 0
    first_half = encoded_vector_list[:half_items]
    second_half = encoded_vector_list[half_items:]
    outgoing = jnp.where(is_query, second_half, first_half)
    incoming = from_partner(outgoing, "tower", 0)
    my_queries = jnp.where(is_query, first_half, incoming)
    local_passages = jnp.where(is_query, incoming, second_half)
    passage_list = lax.all_gather(local_passages, ("tower", "rows"), axis=0, tiled=True)
    total_items = passage_list.shape[0]
    similarity_table = (
        lax.dot_general(
            my_queries, passage_list, (((1,), (1,)), ((), ())), precision=exact
        )
        / logit_divisor
    )
    my_positive = lax.dynamic_slice_in_dim(positives, tower_index * half_items, half_items)
    column = (
        my_positive // half_items % 2 * (rows_size * half_items)
        + my_positive // item_count * half_items
        + my_positive % half_items
    )
    chosen_mask = (jnp.arange(total_items, dtype=jnp.int32)[None, :] == column[:, None]).astype(
        jnp.float32
    )
    row_peak = jnp.max(similarity_table, axis=1, keepdims=True)
    exp_terms = jnp.exp(similarity_table - row_peak)
    summed = jnp.sum(exp_terms, axis=1, keepdims=True)
    losses = (
        row_peak[:, 0] + jnp.log(summed[:, 0]) - jnp.sum(similarity_table * chosen_mask, axis=1)
    )
    similarity_derivative = loss_scale * (exp_terms / summed - chosen_mask)
    query_embedding_gradient = (
        jnp.dot(similarity_derivative, passage_list, precision=exact) / logit_divisor
    )
    doc_embed_grad = lax.psum_scatter(
        lax.dot_general(
            similarity_derivative, my_queries, (((0,), (0,)), ((), ())), precision=exact
        )
        / logit_divisor,
        ("tower", "rows"),
        scatter_dimension=0,
        tiled=True,
    )
    sendback = jnp.where(is_query, doc_embed_grad, query_embedding_gradient)
    received = from_partner(sendback, "tower", 0)
    embed_grad = jnp.where(
        is_query,
        jnp.concatenate([query_embedding_gradient, received], axis=0),
        jnp.concatenate([received, doc_embed_grad], axis=0),
    )
    inner_dot = jnp.sum(encoded_vector_list * embed_grad, axis=-1, keepdims=True)
    pooled_grad = inverse_pool * (embed_grad - encoded_vector_list * inner_dot)
    spread = member / counts
    three_grad = jnp.einsum(
        "ris,rid->rsd",
        spread,
        pooled_grad.reshape(row_count, ITEM_ROW, model_width),
        precision=exact,
    )
    three_grad = three_grad.reshape(token_count, model_width)
    final_gain_grad = jnp.sum(three_grad * unit_three, axis=0)
    final_grad = rms_back(three_grad * gain_three, unit_three, inverse_three)
    branch_two_grad = final_grad.astype(jnp.bfloat16)
    ffn_out_grad = contract_rows(hidden, branch_two_grad)
    inner_grad = (contract_cols(branch_two_grad, w_ffn_out) * gelu_slope(inner)).astype(
        jnp.bfloat16
    )
    ffn_in_grad = contract_rows(normed_two, inner_grad)
    two_grad = contract_cols(inner_grad, w_ffn_in)
    ffn_gain_grad = jnp.sum(two_grad * unit_two, axis=0)
    middle_grad = final_grad + rms_back(two_grad * gain_two, unit_two, inverse_two)
    branch_one_grad = middle_grad.astype(jnp.bfloat16)
    attn_out_grad = contract_rows(attended, branch_one_grad)
    attended_grad = contract_cols(branch_one_grad, w_attn_out).astype(jnp.bfloat16)

    def backward_row(bias_total, packed):
        row_query, row_key, row_value, row_seg, row_norm, row_grad = packed
        masked_scores = row_scores(row_query, row_key, row_seg)
        attn_probs = jnp.exp(masked_scores - row_norm[:, :, None])
        probs_grad = jnp.einsum(
            "shd,thd->hst", row_grad, row_value, preferred_element_type=jnp.float32
        )
        value_grad = jnp.einsum(
            "hst,shd->thd",
            attn_probs.astype(jnp.bfloat16),
            row_grad,
            preferred_element_type=jnp.float32,
        )
        score_part_grad = attn_probs * (
            probs_grad - jnp.sum(attn_probs * probs_grad, axis=-1, keepdims=True)
        )
        rounded = score_part_grad.astype(jnp.bfloat16)
        query_grad = jnp.einsum(
            "hst,thd->shd", rounded, row_key, preferred_element_type=jnp.float32
        )
        key_grad = jnp.einsum(
            "hst,shd->thd", rounded, row_query, preferred_element_type=jnp.float32
        )
        return (
            bias_total + score_part_grad,
            (
                query_grad.astype(jnp.bfloat16),
                key_grad.astype(jnp.bfloat16),
                value_grad.astype(jnp.bfloat16),
            ),
        )

    bias_total, head_grads = lax.scan(
        backward_row,
        jnp.zeros((head_count, seq_len, seq_len), jnp.float32),
        (
            split_heads(query_proj),
            split_heads(key_proj),
            split_heads(value_proj),
            segments,
            log_norms,
            split_heads(attended_grad),
        ),
    )
    query_grad = head_grads[0].reshape(token_count, model_width)
    key_grad = head_grads[1].reshape(token_count, model_width)
    value_grad = head_grads[2].reshape(token_count, model_width)
    table_local = jnp.einsum(
        "ib,hi->bh", onehot, diagonal_sums(bias_total, seq_len), precision=exact
    )
    query_w_grad = contract_rows(normed_one, query_grad)
    key_w_grad = contract_rows(normed_one, key_grad)
    value_w_grad = contract_rows(normed_one, value_grad)
    one_grad = (
        contract_cols(query_grad, w_query)
        + contract_cols(key_grad, w_key)
        + contract_cols(value_grad, w_value)
    )
    attn_gain_grad = jnp.sum(one_grad * unit_one, axis=0)
    input_grad = middle_grad + rms_back(one_grad * gain_one, unit_one, inverse_one)
    table_grad = lax.psum(table_local, ("tower", "rows"))
    shares = (
        lax.psum_scatter(attn_gain_grad, "rows", scatter_dimension=0, tiled=True),
        lax.psum_scatter(query_w_grad, "rows", scatter_dimension=0, tiled=True),
        lax.psum_scatter(key_w_grad, "rows", scatter_dimension=0, tiled=True),
        lax.psum_scatter(value_w_grad, "rows", scatter_dimension=0, tiled=True),
        lax.psum_scatter(attn_out_grad, "rows", scatter_dimension=0, tiled=True),
        lax.psum_scatter(ffn_gain_grad, "rows", scatter_dimension=0, tiled=True),
        lax.psum_scatter(ffn_in_grad, "rows", scatter_dimension=0, tiled=True),
        lax.psum_scatter(ffn_out_grad, "rows", scatter_dimension=0, tiled=True),
        lax.psum_scatter(final_gain_grad, "rows", scatter_dimension=0, tiled=True),
    )
    summed_grads = lax.psum(
        (
            shares[0],
            shares[1],
            shares[2],
            shares[3],
            shares[4],
            shares[5],
            shares[6],
            shares[7],
            shares[8],
        ),
        "tower",
    )
    return (
        encoded_vector_list[None],
        losses.reshape(1, 1, half_items),
        input_grad.reshape(hidden_in.shape),
        summed_grads[0],
        summed_grads[1],
        summed_grads[2],
        summed_grads[3],
        summed_grads[4],
        table_grad,
        summed_grads[5],
        summed_grads[6],
        summed_grads[7],
        summed_grads[8],
    )


def solution(mesh):
    in_specs = (
        P("tower", "rows", None, None),
        P("tower", "rows", None),
        P("rows"),
        P(),
        P(),
        P(),
        P(),
        P(),
        P(),
        P(),
        P(),
        P(),
        P(),
    )
    out_specs = (
        P("tower", "rows", None),
        P("rows", "tower", None),
        P("tower", "rows", None, None),
        P("rows"),
        P("rows", None),
        P("rows", None),
        P("rows", None),
        P("rows", None),
        P(),
        P("rows"),
        P("rows", None),
        P("rows", None),
        P("rows"),
    )
    axes = rows_axes(mesh)
    sized = mesh.shape["tower"] == 2 and tuple(ax.size for ax in axes) == STEPS_SIZES
    body = functools.partial(fused, axes) if sized else on_device
    return jax.shard_map(
        body, mesh=mesh, in_specs=in_specs, out_specs=out_specs, check_vma=False
    )
```

```python
import functools
import math

import jax
import jax.numpy as jnp
import numpy as np
from jax import lax
from jax.experimental import pallas as pl
from jax.experimental.pallas import tpu as pltpu
from jax.sharding import PartitionSpec as P

BUCKETS = 32
MAX_DIST = 128
ITEM_ROW = 8
BLOCK = 128

epsilon = 1e-06
logit_divisor = 0.01
loss_scale = 16.0
far_below = -1000000000.0
exact = lax.Precision.HIGHEST
gelu_cubic = 0.044715
gelu_factor = math.sqrt(2.0 / math.pi)
f32 = jnp.float32
bf16 = jnp.bfloat16
VMEM = pltpu.VMEM
VMEM_LIMIT = 62 * 2**20


def dot_nn(a, b, precision=None):
    return lax.dot_general(
        a, b, (((1,), (0,)), ((), ())), precision=precision, preferred_element_type=f32
    )


def dot_nt(a, b, precision=None):
    return lax.dot_general(
        a, b, (((1,), (1,)), ((), ())), precision=precision, preferred_element_type=f32
    )


def dot_tn(a, b, precision=None):
    return lax.dot_general(
        a, b, (((0,), (0,)), ((), ())), precision=precision, preferred_element_type=f32
    )


def bucket_of(relative, bucket_count, max_distance):
    half_count = bucket_count // 2
    exact_count = half_count // 2
    log_steps = half_count - exact_count
    bounds = []
    for section_index in range(1, log_steps):
        target = exact_count ** (log_steps - section_index) * max_distance**section_index
        lowest = exact_count
        while lowest**log_steps < target:
            lowest = lowest + 1
        bounds.append(lowest)
    distance = abs(relative)
    bucket = half_count if relative > 0 else 0
    if distance < exact_count:
        return bucket + distance
    return bucket + exact_count + len([b for b in bounds if distance >= b])


def lane_buckets():
    width = 4 * BLOCK
    onehot = np.zeros((BUCKETS, width), np.float32)
    for m in range(width):
        relative = (m if m < 3 * BLOCK else m - width) - BLOCK
        onehot[bucket_of(relative, BUCKETS, MAX_DIST), m] = 1.0
    return onehot


def row_of_gain(ref):
    return ref[...].astype(f32).reshape(1, ref.shape[0])


def rms_inverse(values):
    return lax.rsqrt(jnp.mean(values * values, axis=-1, keepdims=True) + epsilon)


def column_of(row):
    return jnp.broadcast_to(row, (8, row.shape[1])).T[:, 0:1]


def three_terms(values):
    high = values.astype(bf16)
    rest = values - high.astype(f32)
    middle = rest.astype(bf16)
    return high, middle, (rest - middle.astype(f32)).astype(bf16)


def key_range(block, blocks):
    return max(block - 1, 0) * BLOCK, min(block + 2, blocks) * BLOCK


MESH_IDS = pl.DeviceIdType.MESH
OUT, IN, ATTN, VALUE, QUERY, KEY = range(6)
OWN, END, SEND = 3, 4, 5
SPAN = 384
INNER, TWO, ATTENDED, HEADS, NORMED, ONE, SMALL = range(7)


class Axis:

    def __init__(self, size, stride):
        self.size, self.stride = size, stride

    def place(self, row):
        return lax.rem(lax.div(row, self.stride), self.size)


UNIT = 128
SLOTS = 3
JOBS = (
    ((2, 0, 1), ((OUT, 0, 0), (OUT, 0, 1),)),
    ((0, 2, 1), ((OUT, 0, 2), (OUT, 0, 3),)),
    ((0, 2, 1), ((OUT, 1, 0), (OUT, 1, 1),)),
    ((0, 1, 2), ((OUT, 1, 2), (OUT, 1, 3),)),
    ((1, 2, 0), ((OUT, 2, 0), (OUT, 2, 1), (OUT, 2, 2), (OUT, 2, 3),)),
    ((1, 0, 2), ((IN, 0, 0), (IN, 1, 0), (IN, 2, 0), (IN, 3, 0),)),
    ((0, 1, 2), ((IN, 4, 0), (IN, 5, 0), (IN, 6, 0), (IN, 7, 0),)),
    ((2, 0, 1), ((IN, 8, 0), (IN, 9, 0), (IN, 10, 0), (IN, 11, 0),)),
    ((0, 1, 2), ((ATTN, 0, 0), (ATTN, 1, 0), (ATTN, 2, 0),)),
    ((1, 0, 2), ((VALUE, 0, 0), (QUERY, 0, 0), (KEY, 0, 0),)),
    ((0, 1, 2), ((VALUE, 1, 0), (QUERY, 1, 0), (KEY, 1, 0),)),
    ((1, 2, 0), ((VALUE, 2, 0),)),
    ((1, 2, 0), ((QUERY, 2, 0),)),
    ((0, 1, 2), ((KEY, 2, 0),)),
)
STEPS_SIZES = (2, 2, 4)
STEPS = (
    (0, SEND, 0), (2, SEND, 0), (0, OWN, 0), (0, 0, 0), (2, OWN, 0), (2, 0, 0), (4, SEND, 0), (1, SEND, 0),
    (3, SEND, 0), (4, OWN, 0), (4, 0, 0), (1, OWN, 0), (1, 0, 0), (3, OWN, 0), (3, 0, 0), (0, 0, 1),
    (-1, INNER, 0), (2, 0, 1), (2, 1, 0), (-1, INNER, 1), (-1, INNER, 2), (-1, INNER, 3), (0, 0, 2),
    (-1, INNER, 4), (-1, INNER, 5), (2, 1, 1), (5, SEND, 0), (1, 0, 1), (1, 1, 0), (6, SEND, 0), (0, 0, 3),
    (0, 1, 0), (2, 1, 2), (5, OWN, 0), (5, 0, 0), (7, SEND, 0), (4, 0, 1), (4, 1, 0), (1, 1, 1), (6, OWN, 0),
    (6, 0, 0), (3, 0, 1), (3, 1, 0), (7, OWN, 0), (7, 0, 0), (0, 1, 1), (0, 2, 0), (1, 1, 2), (2, 1, 3),
    (2, 2, 0), (-1, TWO, 0), (1, 1, 3), (1, 2, 0), (4, 1, 1), (8, SEND, 0), (-1, NORMED, 0),
    (-1, ATTENDED, 0), (-1, HEADS, 0), (5, 0, 1), (5, 1, 0), (8, OWN, 0), (8, 0, 0), (4, 1, 2), (3, 1, 1),
    (3, 2, 0), (-1, HEADS, 3), (1, 2, 1), (0, 2, 1), (6, 0, 1), (6, 1, 0), (2, 2, 1), (1, END, 0),
    (0, END, 0), (9, SEND, 0), (4, 1, 3), (4, 2, 0), (2, END, 0), (-1, HEADS, 1), (9, OWN, 0), (9, 0, 0),
    (5, 1, 1), (5, 2, 0), (7, 0, 1), (-1, HEADS, 4), (6, 1, 1), (6, 2, 0), (10, SEND, 0), (-1, HEADS, 2),
    (10, OWN, 0), (10, 0, 0), (-1, HEADS, 5), (3, 2, 1), (8, 0, 1), (8, 1, 0), (7, 0, 2), (11, SEND, 0),
    (4, 2, 1), (12, SEND, 0), (13, SEND, 0), (11, OWN, 0), (11, 0, 0), (9, 0, 1), (9, 1, 0), (12, OWN, 0),
    (12, 0, 0), (13, OWN, 0), (13, 0, 0), (5, 2, 1), (4, END, 0), (-1, ONE, 0), (3, 2, 2), (-1, SMALL, 0),
    (8, 1, 1), (8, 2, 0), (6, 2, 1), (-1, SMALL, 1), (5, 2, 2), (3, 2, 3), (7, 0, 3), (7, 1, 0), (3, END, 0),
    (10, 0, 1), (10, 1, 0), (11, 0, 1), (11, 1, 0), (6, 2, 2), (8, 2, 1), (5, 2, 3), (5, END, 0), (6, 2, 3),
    (8, 2, 2), (12, 0, 1), (12, 1, 0), (11, 1, 1), (6, END, 0), (9, 1, 1), (9, 2, 0), (8, 2, 3), (11, 1, 2),
    (12, 1, 1), (8, END, 0), (11, 1, 3), (11, 2, 0), (12, 1, 2), (13, 0, 1), (13, 1, 0), (12, 1, 3),
    (12, 2, 0), (9, 2, 1), (10, 1, 1), (10, 2, 0), (9, 2, 2), (13, 1, 1), (13, 2, 0), (-1, SMALL, 2),
    (9, 2, 3), (7, 1, 1), (7, 2, 0), (10, 2, 1), (11, 2, 1), (9, END, 0), (12, 2, 1), (11, END, 0),
    (12, END, 0), (13, 2, 1), (7, 2, 1), (10, 2, 2), (7, END, 0), (13, 2, 2), (10, 2, 3), (13, 2, 3),
    (10, END, 0), (-1, SMALL, 3), (13, END, 0),
)


def layer_kernel(axes, *refs):
    jobs = len(JOBS)
    (
        x_ref, seg_ref, pos_ref, g1_ref, g2_ref, g3_ref, table_ref, lanes_ref,
        wq_h, wk_h, wv_h, wo_h, w1_h, w2_h,
        emb_o, loss_o, small_o, gh_o, inner_o,
    ) = refs[:19]
    res, refs = refs[19 : 19 + jobs], refs[19 + jobs :]
    (
        all_e, gs, hid, ig, chunk, wslot, q, k, v, att, nrm, br2, br1, mid, fin, by_offset, d_all,
        sm, sm_core, sm_plane, sm_line, stg,
    ) = refs[:22]
    accs, landings, refs = refs[22 : 22 + jobs], refs[22 + jobs : 22 + 4 * jobs], refs[22 + 4 * jobs :]
    load_sem, ag_s, ag_r, sm_s, sm_r, tow_s, tow_r, end_s, end_r, end_l, line_s, line_r = refs

    t = lax.axis_index("tower")
    row = lax.axis_index("rows")
    place = [ax.place(row) for ax in axes]
    nx, ny, nz = (ax.size for ax in axes)
    sx, sy, sz = (ax.stride for ax in axes)
    plane_size = nx * ny
    plane = place[1] * nx + place[0]
    spot = plane * nz + place[2]

    def row_of(w, z):
        return lax.rem(w, nx) * sx + lax.div(w, nx) * sy + z * sz

    z_peers = [(t, row_of(plane, lax.rem(place[2] + m, nz))) for m in range(1, nz)]
    plane_peers = [(t, row_of(lax.rem(plane + m, plane_size), place[2])) for m in range(1, plane_size)]
    partner = (1 - t, row)

    barrier = pltpu.get_barrier_semaphore()
    for peer in z_peers + plane_peers + [partner]:
        pl.semaphore_signal(barrier, inc=1, device_id=peer, device_id_type=MESH_IDS)

    def load(i, src, dst):
        return pltpu.make_async_copy(src, dst, load_sem.at[i])

    def remote(src, dst, ss, rs, to):
        return pltpu.make_async_remote_copy(
            src_ref=src, dst_ref=dst, send_sem=ss, recv_sem=rs, device_id=to, device_id_type=MESH_IDS
        )

    seq, width = x_ref.shape
    heads = table_ref.shape[0]
    ff = hid.shape[1]
    piece = 512
    pieces = ff // piece
    blocks = seq // BLOCK
    tail = width - seq
    square_loads = [
        load(i, w, wslot.at[pl.ds(i * width, width)]) for i, w in enumerate((wq_h, wk_h, wv_h, wo_h))
    ]
    ahead_loads = [load(4, w1_h.at[pl.ds(0, seq)], ig)]
    tails = []
    for c in range(ff // width):
        held = (br2 if c < 2 else br1).at[pl.ds(c % 2 * tail, tail)]
        tails.append(held)
        ahead_loads.append(load(5 + c, w1_h.at[pl.ds(seq, tail), pl.ds(c * width, width)], held))
    w2_load = load(9, w2_h, wslot)
    back_loads = [
        load(10 + c, w1_h.at[:, pl.ds(c * width, width)], wslot.at[pl.ds(c * width, width)])
        for c in range(ff // width)
    ]
    gh_store = load(14, fin, gh_o)
    kept = [load(15 + c, chunk.at[c % 2], inner_o.at[:, pl.ds(c * piece, piece)]) for c in range(pieces - 2)]
    fetched = [load(15 + c, inner_o.at[:, pl.ds(c * piece, piece)], chunk.at[c % 2]) for c in range(pieces - 2)]
    for w in square_loads[:3]:
        w.start()

    def normed(values, gain_ref):
        return ((values * rms_inverse(values)) * row_of_gain(gain_ref)).astype(bf16)

    nrm[...] = normed(x_ref[...].astype(f32), g1_ref)
    square_loads[3].start()
    for w in ahead_loads:
        w.start()
    for i, out in enumerate((q, k, v)):
        square_loads[i].wait()
        out[...] = dot_nn(nrm[...], wslot[i * width : (i + 1) * width, :]).astype(bf16)

    seg_row = seg_ref[...].astype(f32)
    low_half = lax.broadcasted_iota(jnp.int32, (BLOCK, BLOCK), 1) < BLOCK // 2

    def bias_tile(h, first, last):
        n = h % 4 * BLOCK
        if h < 8:
            lane = h // 4 * 3 * BLOCK
            return fin[n : n + BLOCK, lane + first : lane + last]
        return chunk[0, n : n + BLOCK, first:last]

    def build_tiles():
        by_offset[0:heads, :] = dot_nn(table_ref[...], lanes_ref[...])
        for h in range(heads):
            spread = jnp.broadcast_to(by_offset[h : h + 1, :], (BLOCK, 4 * BLOCK))
            tile = pltpu.roll(spread, 0, 1, stride=1, stride_axis=0)[:, : 3 * BLOCK]
            n = h % 4 * BLOCK
            if h < 8:
                lane = h // 4 * 3 * BLOCK
                fin[n : n + BLOCK, lane : lane + 3 * BLOCK] = tile
            else:
                chunk[0, n : n + BLOCK, 0 : 3 * BLOCK] = tile
        seg_col = column_of(seg_row)
        for b in range(blocks):
            lo, hi = key_range(b, blocks)
            first = lo - (b - 1) * BLOCK
            same = seg_col[b * BLOCK : (b + 1) * BLOCK] == seg_row[:, lo:hi]
            chunk[1, b * BLOCK : (b + 1) * BLOCK, first : first + hi - lo] = jnp.where(same, 0.0, far_below)

    def two_heads(values):
        zero = jnp.zeros_like(values)
        return jnp.concatenate([jnp.where(low_half, values, zero), jnp.where(low_half, zero, values)], axis=0)

    def probabilities(pair, b, both, keys):
        lo, hi = key_range(b, blocks)
        first = lo - (b - 1) * BLOCK
        last = first + hi - lo
        mask = chunk[1, b * BLOCK : (b + 1) * BLOCK, first:last]
        s = dot_nt(both, keys)
        parts = []
        for e in range(2):
            part = s[e * BLOCK : (e + 1) * BLOCK] + bias_tile(2 * pair + e, first, last) + mask
            terms = jnp.exp(part - jnp.max(part, axis=-1, keepdims=True))
            parts.append(terms * (1.0 / jnp.sum(terms, axis=-1, keepdims=True)))
        return parts

    build_tiles()
    for pair in range(heads // 2):
        lanes = slice(pair * UNIT, (pair + 1) * UNIT)
        for b in range(blocks):
            lo, hi = key_range(b, blocks)
            mine = slice(b * BLOCK, (b + 1) * BLOCK)
            parts = probabilities(pair, b, two_heads(q[mine, lanes]), k[lo:hi, lanes])
            probs = jnp.concatenate([part.astype(bf16) for part in parts], axis=0)
            out = dot_nn(probs, v[lo:hi, lanes])
            att[mine, lanes] = jnp.where(low_half, out[:BLOCK], out[BLOCK:]).astype(bf16)

    square_loads[3].wait()
    middle = x_ref[...].astype(f32) + dot_nn(att[...], wslot[3 * width : 4 * width, :])
    w2_load.start()
    mid[...] = middle
    nrm[...] = normed(middle, g2_ref)
    for w in ahead_loads:
        w.wait()
    for c in range(pieces):
        low = c * piece
        inner = dot_nn(nrm[:, 0:seq], ig[:, low : low + piece])
        rest = []
        while low < (c + 1) * piece:
            n = low // width
            high = min((c + 1) * piece, (n + 1) * width)
            rest.append(dot_nn(nrm[:, seq:width], tails[n][:, low - n * width : high - n * width]))
            low = high
        inner = inner + (jnp.concatenate(rest, axis=1) if len(rest) > 1 else rest[0])
        if c >= 2:
            kept[c - 2].wait()
        chunk[c % 2] = inner
        if c < pieces - 2:
            kept[c].start()
        tangent = jnp.tanh(gelu_factor * (inner + gelu_cubic * (inner * inner * inner)))
        hid[:, c * piece : (c + 1) * piece] = (inner * (0.5 * (1.0 + tangent))).astype(bf16)
    w2_load.wait()
    final = mid[...] + dot_nn(hid[...], wslot[...])
    fin[...] = final
    member = (lax.broadcasted_iota(jnp.int32, (ITEM_ROW, seq), 0).astype(f32) == seg_row).astype(f32)
    counts = jnp.sum(member, axis=-1, keepdims=True)
    ones = member.astype(bf16)
    high, middle_part, low_part = three_terms((final * rms_inverse(final)) * row_of_gain(g3_ref))
    pooled = (dot_nn(ones, high) + (dot_nn(ones, middle_part) + dot_nn(ones, low_part))) / counts

    inverse_pool = lax.rsqrt(jnp.sum(pooled * pooled, axis=-1, keepdims=True) + epsilon)
    own_e = pooled * inverse_pool
    emb_o[...] = own_e
    own_rows = pl.ds(pl.multiple_of(spot * ITEM_ROW, ITEM_ROW), ITEM_ROW)

    def bits(n):
        return n.bit_length() - 1

    p = pos_ref[...]
    of_row = p >> bits(ITEM_ROW)

    def along(ax):
        return (of_row >> bits(ax.stride)) & (ax.size - 1)

    p = ((along(axes[1]) * nx + along(axes[0])) * nz + along(axes[2])) * ITEM_ROW + (p & (ITEM_ROW - 1))
    i8 = lax.broadcasted_iota(jnp.int32, (ITEM_ROW, ITEM_ROW), 0)
    j8 = lax.broadcasted_iota(jnp.int32, (ITEM_ROW, ITEM_ROW), 1)
    diag = jnp.where(i8 == j8, jnp.broadcast_to(p.astype(f32), (ITEM_ROW, ITEM_ROW)), 0.0)
    pos_col = jnp.sum(diag, axis=-1, keepdims=True)
    all_e[t, own_rows, 0:width] = own_e
    all_e[t, own_rows, width : width + UNIT] = jnp.broadcast_to(pos_col, (ITEM_ROW, UNIT))

    pl.semaphore_wait(barrier, len(z_peers) + len(plane_peers) + 1)

    def column_rows(w):
        return pl.ds(pl.multiple_of(w * (nz * ITEM_ROW), ITEM_ROW), nz * ITEM_ROW)

    def item_rows(w, z):
        return pl.ds(pl.multiple_of((w * nz + z) * ITEM_ROW, ITEM_ROW), ITEM_ROW)

    sent = []

    def spread(index, rows, peer):
        block = all_e.at[t, rows]
        sent.append(remote(block, block, ag_s.at[index], ag_r.at[index], peer))
        sent[-1].start()
        return sent[-1]

    along_z = [spread(m, own_rows, peer) for m, peer in enumerate(z_peers)]
    count = len(z_peers)

    def over_plane(m):
        rows = item_rows(plane, lax.rem(place[2] + nz - m, nz))
        first = count + m * len(plane_peers)
        return [spread(first + j, rows, peer) for j, peer in enumerate(plane_peers)]

    in_plane = [over_plane(0)]
    inverse = rms_inverse(fin[...])
    fin[...] = fin[...] * inverse
    sm[...] = jnp.zeros_like(sm)
    for m in range(1, nz):
        along_z[m - 1].wait_recv()
        in_plane.append(over_plane(m))
    count += nz * len(plane_peers)
    to_tower = [spread(count, column_rows(plane), partner)]
    for j in range(1, plane_size):
        for m in range(nz):
            in_plane[m][j - 1].wait_recv()
        rows = column_rows(lax.rem(plane + plane_size - j, plane_size))
        to_tower.append(spread(count + j, rows, partner))
    for c in to_tower:
        c.wait_recv()

    queries, docs = all_e[0, :, 0:width], all_e[1, :, 0:width]
    items = queries.shape[0]
    scores = dot_nt(queries, docs, exact) / logit_divisor
    top = jnp.max(scores, axis=1, keepdims=True)
    terms = jnp.exp(scores - top)
    summed = jnp.sum(terms, axis=1, keepdims=True)
    chosen = (
        lax.broadcasted_iota(jnp.int32, (items, items), 1).astype(f32) == all_e[0, :, width : width + 1]
    ).astype(f32)
    slope = loss_scale * (terms / summed - chosen)

    @pl.when(t == 0)
    def _():
        gs[...] = slope

    @pl.when(t == 1)
    def _():
        gs[...] = slope.T

    embed_grad = dot_nn(gs[own_rows, :], all_e[1 - t, :, 0:width], exact) / logit_divisor
    inner_dot = jnp.sum(own_e * embed_grad, axis=-1, keepdims=True)
    pooled_grad = inverse_pool * (embed_grad - own_e * inner_dot)

    terms_of_grad = jnp.concatenate([part.astype(f32) for part in three_terms(pooled_grad / counts)], axis=0)
    three_grad = dot_tn(jnp.concatenate([member] * 3, axis=0).astype(bf16), terms_of_grad.astype(bf16))
    unit = fin[...]
    sm[0:1, 0:width] = jnp.sum(three_grad * unit, axis=0, keepdims=True)
    u = three_grad * row_of_gain(g3_ref)
    final_grad = inverse * (u - unit * jnp.mean(u * unit, axis=-1, keepdims=True))
    fin[...] = final_grad
    br2[...] = final_grad.astype(bf16)

    def write_losses():
        losses = top + jnp.log(summed) - jnp.sum(scores * chosen, axis=1, keepdims=True)
        loss_row = jnp.broadcast_to(losses, (items, UNIT)).T[0:8, :]
        pick = (
            lax.broadcasted_iota(jnp.int32, (items, UNIT), 0)
            == lax.broadcasted_iota(jnp.int32, (items, UNIT), 1) + spot * ITEM_ROW + t * (ITEM_ROW // 2)
        ).astype(f32)
        loss_o[...] = dot_nn(loss_row, pick, exact)

    chunk_rows = width // (nx * ny * nz)
    lefts = (hid, nrm, att, nrm, nrm, nrm)
    rights = (br2, ig, br1, v, q, k)
    in_slot = {}
    unwaited = []

    def spots(path):
        found = {}
        for r in range(nx * ny * nz):
            number = 0
            for a in path:
                number = number * axes[a].size + (r // axes[a].stride) % axes[a].size
            found[r] = number * chunk_rows
        return found

    def product(job, half, keep):
        path, parts = JOBS[job]
        lhs = lefts[parts[0][0]]
        stripes = list(dict.fromkeys((target, block) for target, block, _ in parts))
        subs = lhs.shape[1] // width
        group = SPAN // (subs * chunk_rows)
        where = spots(path)

        def step(i, carry):
            right = []
            for target, block in stripes:
                rhs = rights[target]
                lane = half * (rhs.shape[1] // 2) + block * UNIT
                right.append(rhs[:, pl.ds(pl.multiple_of(lane, UNIT), UNIT)])
            columns = pl.ds(pl.multiple_of(i * SPAN, UNIT), SPAN)
            value = dot_tn(lhs[:, columns], jnp.concatenate(right, axis=1) if len(right) > 1 else right[0])
            moved = sum(lax.rem(lax.div(i * group, ax.stride), ax.size) * where[ax.stride] for ax in axes)
            for r in range(group):
                at_row = pl.multiple_of(moved + where[r], 8)
                for n, (target, block, sub) in enumerate(parts):
                    low = (r * subs + sub) * chunk_rows
                    lane = stripes.index((target, block)) * UNIT
                    keep(n, pl.ds(at_row, chunk_rows), value[low : low + chunk_rows, lane : lane + UNIT])
            return carry

        lax.fori_loop(0, lhs.shape[1] // SPAN, step, 0, unroll=2 if subs > 1 else 1)

    def tower_copy(job, slot):
        units = len(JOBS[job][1])
        return remote(stg.at[slot, pl.ds(0, units)], accs[job], tow_s.at[job], tow_r.at[job], partner)

    def send_half(job):
        slot = len(in_slot) % SLOTS
        before = [n for n, s in in_slot.items() if s == slot]
        if before:
            tower_copy(before[-1], slot).wait_send()
            unwaited.remove(before[-1])

        def keep(n, rows, value):
            stg[slot, n, rows, :] = value

        product(job, 1 - t, keep)
        tower_copy(job, slot).start()
        in_slot[job] = slot
        unwaited.append(job)

    def take_own(job):
        acc = accs[job]
        tower_copy(job, 0).wait_recv()

        def keep(n, rows, value):
            acc[n, rows, :] = acc[n, rows, :] + value

        product(job, t, keep)

    def geometry(job, leg):
        path = JOBS[job][0]
        low, size = 0, width
        for a in path[:leg]:
            size = size // axes[a].size
            low = low + place[a] * size
        return low, size // axes[path[leg]].size, axes[path[leg]], place[path[leg]]

    def line_copy(job, leg, i, block):
        low, size, axis, _ = geometry(job, leg)
        n = axis.size
        if block > i:
            to, slot = (t, row + axis.stride), (0 if n == 2 else block)
        else:
            to, slot = (t, row - axis.stride), (0 if n == 2 else n if block == i - 1 else block)
        at_row = pl.multiple_of(low + block * size, 8)
        return remote(
            accs[job].at[:, pl.ds(at_row, size)], landings[3 * job + leg].at[slot],
            line_s.at[job, leg, block], line_r.at[job, leg, slot], to,
        )

    def take(job, leg, block, slot):
        low, size, axis, _ = geometry(job, leg)
        at_row = pl.multiple_of(low + block * size, 8)
        acc, landed = accs[job], landings[3 * job + leg]
        remote(
            landed.at[slot], landed.at[slot], line_s.at[job, leg, block], line_r.at[job, leg, slot], partner
        ).wait_recv()
        acc[:, pl.ds(at_row, size), :] = acc[:, pl.ds(at_row, size), :] + landed[slot]

    def line_step(job, leg, s):
        _, _, axis, my_place = geometry(job, leg)
        n = axis.size
        for i in range(n):
            from_left = s == i and i < n - 1
            from_right = s == n - 1 - i and i > 0
            last = s == n - 1
            if not (from_left or from_right or last):
                continue

            @pl.when(my_place == i)
            def _():
                if from_left:
                    for block in range(n - 1, i, -1):
                        if i > 0:
                            take(job, leg, block, block)
                        line_copy(job, leg, i, block).start()
                if from_right:
                    for block in range(i):
                        if i < n - 1:
                            take(job, leg, block, block)
                        line_copy(job, leg, i, block).start()
                if last:
                    if n == 2:
                        take(job, leg, i, 0)
                    else:
                        if i > 0:
                            take(job, leg, i, i)
                        if i < n - 1:
                            take(job, leg, i, n)

        if s == n - 1 and leg == 2:
            end_copy(job, True).start()
            end_copy(job, False).start()

    def line_drain(job, leg):
        _, _, axis, my_place = geometry(job, leg)
        for i in range(axis.size):

            @pl.when(my_place == i)
            def _():
                for block in range(axis.size):
                    if block != i:
                        line_copy(job, leg, i, block).wait_send()

    def end_copy(job, to_partner):
        low, size, _, my_place = geometry(job, 2)
        at_row = pl.multiple_of(low + my_place * size, 8)
        src, dst = accs[job].at[:, pl.ds(at_row, size)], res[job].at[t]
        if to_partner:
            return remote(src, dst, end_s.at[job], end_r.at[job], partner)
        return pltpu.make_async_copy(src, dst, end_l.at[job])

    def inner_step(n):
        c = (n + pieces - 2) % pieces
        if n >= 2:
            fetched[c].wait()
        v_in = chunk[c % 2]
        grad = dot_nt(br2[...], wslot[c * piece : (c + 1) * piece, :])
        tangent = jnp.tanh(gelu_factor * (v_in + gelu_cubic * (v_in * v_in * v_in)))
        ahead = 0.5 * (1.0 + tangent) + 0.5 * v_in * (1.0 - tangent * tangent) * gelu_factor * (
            1.0 + 3.0 * gelu_cubic * v_in * v_in
        )
        ig[:, c * piece : (c + 1) * piece] = (grad * ahead).astype(bf16)
        if n + 2 < pieces:
            fetched[n].start()
        if n == pieces - 1:
            for w in back_loads:
                w.start()

    def norm_back(grad, values, gain):
        inverse = rms_inverse(values)
        unit = values * inverse
        total = jnp.sum(grad * unit, axis=0, keepdims=True)
        w = grad * gain
        return inverse * (w - unit * jnp.mean(w * unit, axis=-1, keepdims=True)), total

    tokens = 256

    def two_step():
        for w in back_loads:
            w.wait()
        gain = row_of_gain(g2_ref)
        for low in range(0, seq, tokens):
            part = slice(low, low + tokens)
            grad = dot_nt(ig[part, 0:width], wslot[0:width, :])
            for c in range(1, ff // width):
                lanes = slice(c * width, (c + 1) * width)
                grad = grad + dot_nt(ig[part, lanes], wslot[lanes, :])
            back, total = norm_back(grad, mid[part, :], gain)
            sm[1:2, 0:width] = sm[1:2, 0:width] + total
            middle_grad = fin[part, :] + back
            mid[part, :] = middle_grad
            br1[part, :] = middle_grad.astype(bf16)
        for w in square_loads:
            w.start()
        build_tiles()

    def attended_step():
        for w in square_loads:
            w.wait()
        br2[...] = dot_nt(br1[...], wslot[3 * width : 4 * width, :]).astype(bf16)
        d_all[...] = jnp.zeros_like(d_all)

    turned = [lax.broadcasted_iota(jnp.int32, (BLOCK, BLOCK), n) for n in range(2)]
    upside = (turned[0] + turned[1] == BLOCK - 1).astype(bf16)

    def upside_down(values):
        high, middle_part, low_part = three_terms(values)
        return dot_nn(upside, high) + (dot_nn(upside, middle_part) + dot_nn(upside, low_part))

    def heads_step(pair):
        lanes = slice(pair * UNIT, (pair + 1) * UNIT)
        columns = [[None] * 3, [None] * 3]
        key_grads, value_grads = [None] * blocks, [None] * blocks

        def put(held, n, value):
            held[n] = value if held[n] is None else held[n] + value

        for b in range(blocks):
            lo, hi = key_range(b, blocks)
            mine = slice(b * BLOCK, (b + 1) * BLOCK)
            first = lo - (b - 1) * BLOCK
            keys = k[lo:hi, lanes]
            both_q, both_o = two_heads(q[mine, lanes]), two_heads(br2[mine, lanes])
            probs = probabilities(pair, b, both_q, keys)
            pg = dot_nt(both_o, v[lo:hi, lanes])
            grads = []
            for e in range(2):
                ds = pg[e * BLOCK : (e + 1) * BLOCK]
                ds = probs[e] * (ds - jnp.sum(probs[e] * ds, axis=-1, keepdims=True))
                for n in range((hi - lo) // BLOCK):
                    put(columns[e], first // BLOCK + n, ds[:, n * BLOCK : (n + 1) * BLOCK])
                grads.append(ds.astype(bf16))
            rounded = jnp.concatenate(grads, axis=0)
            dq = dot_nn(rounded, keys)
            dk = dot_tn(rounded, both_q)
            dv = dot_tn(jnp.concatenate([part.astype(bf16) for part in probs], axis=0), both_o)
            for n in range((hi - lo) // BLOCK):
                rows = slice(n * BLOCK, (n + 1) * BLOCK)
                put(key_grads, lo // BLOCK + n, dk[rows])
                put(value_grads, lo // BLOCK + n, dv[rows])
            q[mine, lanes] = jnp.where(low_half, dq[:BLOCK], dq[BLOCK:]).astype(bf16)
        for b in range(blocks):
            mine = slice(b * BLOCK, (b + 1) * BLOCK)
            k[mine, lanes] = key_grads[b].astype(bf16)
            v[mine, lanes] = value_grads[b].astype(bf16)
        for e in range(2):
            wide = jnp.concatenate(columns[e] + [jnp.zeros((BLOCK, BLOCK), f32)], axis=1)
            skewed = pltpu.roll(upside_down(wide), 3 * BLOCK + 1, 1, stride=1, stride_axis=0)
            d_all[2 * pair + e : 2 * pair + e + 1, :] = jnp.sum(skewed, axis=0, keepdims=True)

    def normed_step():
        nrm[...] = normed(x_ref[...].astype(f32), g1_ref)

    def one_step():
        gain = row_of_gain(g1_ref)
        for low in range(0, seq, tokens):
            part = slice(low, low + tokens)
            grad = dot_nt(q[part, :], wslot[0:width, :])
            grad = grad + dot_nt(k[part, :], wslot[width : 2 * width, :])
            grad = grad + dot_nt(v[part, :], wslot[2 * width : 3 * width, :])
            back, total = norm_back(grad, x_ref[part, :].astype(f32), gain)
            sm[2:3, 0:width] = sm[2:3, 0:width] + total
            fin[part, :] = mid[part, :] + back
        gh_store.start()
        write_losses()

    small_first = remote(sm, sm_core, sm_s.at[0], sm_r.at[0], partner)
    base = 1 + len(plane_peers)
    own_plane, own_line = sm_plane.at[plane], sm_line.at[place[2]]
    small_second = [
        remote(own_plane, own_plane, sm_s.at[1 + m], sm_r.at[1 + m], peer) for m, peer in enumerate(plane_peers)
    ]
    small_third = [
        remote(own_line, own_line, sm_s.at[base + m], sm_r.at[base + m], peer) for m, peer in enumerate(z_peers)
    ]

    def small_step(s):
        if s == 0:
            table_grad = dot_nt(d_all[...], lanes_ref[...].astype(f32), exact)
            for n in range(2):
                sm[:, width + n * UNIT : width + n * UNIT + BUCKETS] = table_grad[8 * n : 8 * n + 8, :]
            small_first.start()
        elif s == 1:
            small_first.wait()
            sm_plane[plane] = sm[...] + sm_core[...]
            for c in small_second:
                c.start()
        elif s == 2:
            for c in small_second:
                c.wait()
            total = sm_plane[0]
            for w in range(1, plane_size):
                total = total + sm_plane[w]
            sm_line[place[2]] = total
            for c in small_third:
                c.start()
        else:
            for c in small_third:
                c.wait()
            total = sm_line[0]
            for w in range(1, nz):
                total = total + sm_line[w]
            small_o[...] = total

    layer_steps = {
        INNER: inner_step, TWO: lambda n: two_step(), ATTENDED: lambda n: attended_step(), HEADS: heads_step,
        NORMED: lambda n: normed_step(), ONE: lambda n: one_step(), SMALL: small_step,
    }
    for job, leg, s in STEPS:
        if job < 0:
            layer_steps[leg](s)
        elif leg == SEND:
            send_half(job)
        elif leg == OWN:
            take_own(job)
        elif leg == END:
            end_copy(job, True).wait_recv()
            end_copy(job, False).wait()
        else:
            line_step(job, leg, s)
    for c in sent:
        c.wait_send()
    for job in unwaited:
        tower_copy(job, in_slot[job]).wait_send()
    for job in range(jobs):
        for leg in range(3):
            line_drain(job, leg)
        end_copy(job, True).wait_send()
    gh_store.wait()


def layer_call(axes, args):
    seq, width = args[0].shape
    ff = args[12].shape[1]
    nx, ny, nz = (ax.size for ax in axes)
    rows = nx * ny * nz
    chunk_rows = width // rows
    s = jax.ShapeDtypeStruct
    vm, hbm = pl.BlockSpec(memory_space=VMEM), pl.BlockSpec(memory_space=pl.ANY)
    small = (8, width + 2 * UNIT)
    most_units = max(len(parts) for _, parts in JOBS)
    outs = [
        s((ITEM_ROW, width), f32), s((8, UNIT), f32), s(small, f32), s((seq, width), f32), s((seq, ff), f32),
    ]
    outs += [s((2, len(parts), chunk_rows, UNIT), f32) for _, parts in JOBS]
    scratch = [
        VMEM((2, rows * ITEM_ROW, width + UNIT), f32), VMEM((rows * ITEM_ROW, rows * ITEM_ROW), f32),
        VMEM((seq, ff), bf16), VMEM((seq, ff), bf16), VMEM((2, seq, 512), f32), VMEM((ff, width), bf16),
    ]
    scratch += [VMEM((seq, width), bf16)] * 7 + [VMEM((seq, width), f32)] * 2
    scratch += [
        VMEM((16, 4 * BLOCK), f32), VMEM((16, 4 * BLOCK), f32),
        VMEM(small, f32), VMEM(small, f32), VMEM((nx * ny, *small), f32), VMEM((nz, *small), f32),
        VMEM((SLOTS, most_units, width, UNIT), f32),
    ]
    scratch += [VMEM((len(parts), width, UNIT), f32) for _, parts in JOBS]
    for path, parts in JOBS:
        size = width
        for a in path:
            n = axes[a].size
            size = size // n
            scratch.append(VMEM((1 if n == 2 else n + 1, len(parts), size, UNIT), f32))
    dma = pltpu.SemaphoreType.DMA
    jobs, most = len(JOBS), max(nx, ny, nz)
    gathers = nz - 1 + nz * (nx * ny - 1) + nx * ny
    smalls = nz + nx * ny - 1
    scratch += [
        dma((19,)), dma((gathers,)), dma((gathers,)), dma((smalls,)), dma((smalls,)),
        dma((jobs,)), dma((jobs,)), dma((jobs,)), dma((jobs,)), dma((jobs,)),
        dma((jobs, 3, most)), dma((jobs, 3, most + 1)),
    ]
    return pl.pallas_call(
        functools.partial(layer_kernel, axes),
        name="layer",
        out_shape=outs,
        in_specs=[vm] * 8 + [hbm] * 6,
        out_specs=[vm] * 3 + [hbm] * (2 + jobs),
        scratch_shapes=scratch,
        compiler_params=pltpu.CompilerParams(
            collective_id=0, has_side_effects=True, vmem_limit_bytes=VMEM_LIMIT
        ),
    )(*args)


def place_kernel(emb, loss, small, gh, *refs):
    res = refs[: len(JOBS)]
    (
        emb_o, loss_o, gh_o, attn_gain_o, query_o, key_o, value_o, attn_o, table_o, ffn_gain_o, in_o, out_o, final_gain_o,
    ) = refs[len(JOBS) :]
    row = lax.axis_index("rows")
    targets = (out_o, in_o, attn_o, value_o, query_o, key_o)
    emb_o[0] = emb[...]
    gh_o[0, 0] = gh[...]
    for job, (_, parts) in enumerate(JOBS):
        for n, (target, block, sub) in enumerate(parts):
            out, height = targets[target], res[job].shape[2]
            for t in range(2):
                low = t * (out.shape[1] // 2) + block * UNIT
                out[sub * height : (sub + 1) * height, low : low + UNIT] = res[job][t, n]
    loss_o[0] = loss[0:1, 0 : loss_o.shape[2]]
    width = gh.shape[1]
    share = attn_gain_o.shape[0]
    pick = (
        lax.broadcasted_iota(jnp.int32, (width, UNIT), 0)
        == lax.broadcasted_iota(jnp.int32, (width, UNIT), 1) + row * share
    ).astype(f32)
    gains = dot_nn(small[:, 0:width], pick, exact)
    for n, out in enumerate((final_gain_o, ffn_gain_o, attn_gain_o)):
        out[...] = gains[n, 0:share]
    heads = table_o.shape[0]
    for low in range(0, heads, 8):
        lane = width + low // 8 * UNIT
        high = min(low + 8, heads)
        table_o[low:high, :] = small[0 : high - low, lane : lane + BUCKETS]


def place_call(axes, heads, emb, loss, small, gh, res):
    seq, width = gh.shape
    ff = 4 * width
    rows = math.prod(a.size for a in axes)
    share = width // rows
    s = jax.ShapeDtypeStruct
    vm = pl.BlockSpec(memory_space=VMEM)
    weight = s((share, width), f32)
    outs = [
        s((1, *emb.shape), f32), s((1, 1, ITEM_ROW // 2), f32), s((1, 1, seq, width), f32), s((share,), f32),
        weight, weight, weight, weight, s((heads, BUCKETS), f32), s((share,), f32),
        s((share, ff), f32), s((ff // rows, width), f32), s((share,), f32),
    ]
    return pl.pallas_call(
        place_kernel,
        name="place",
        out_shape=outs,
        in_specs=[vm] * (4 + len(JOBS)),
        out_specs=[vm] * len(outs),
        compiler_params=pltpu.CompilerParams(vmem_limit_bytes=VMEM_LIMIT),
    )(emb, loss, small, gh, *res)


def rows_axes(mesh):
    rows = mesh.shape["rows"]
    line = mesh.devices.reshape(-1, rows)[0]
    places = [tuple(getattr(d, "coords", (i % 2, i // 2 % 2, i // 4))) for i, d in enumerate(line)]
    axes = []
    for n in range(3):
        values = sorted({p[n] for p in places})
        stride = next((i for i, p in enumerate(places) if p[n] != places[0][n]), 1)
        axes.append(Axis(len(values), stride))
    return tuple(axes)


def fused(
    axes, hidden_in, segment_ids, positives, attn_gain, w_query, w_key, w_value, w_attn_out, rel_table,
    ffn_gain, w_ffn_in, w_ffn_out, final_gain,
):
    seq, width = hidden_in.shape[2:]
    lanes = jnp.asarray(lane_buckets(), bf16)
    emb, loss, small, gh, _, *res = layer_call(
        axes,
        (
            hidden_in.reshape(seq, width), segment_ids.reshape(1, seq), positives.reshape(1, -1),
            attn_gain, ffn_gain, final_gain, rel_table.T, lanes,
            w_query, w_key, w_value, w_attn_out, w_ffn_in, w_ffn_out,
        ),
    )
    outs = list(place_call(axes, rel_table.shape[1], emb, loss, small, gh, res))
    outs[8] = outs[8].T
    return tuple(outs)


def from_partner(block, axis, bit):
    count = lax.axis_size(axis)
    route = []
    for low in range(count):
        high = low | 1 << bit
        if high != low and high < count:
            route += [(low, high), (high, low)]
    return lax.ppermute(block, axis, route)


def bucket_onehot(seq_len, bucket_count, max_distance):
    half_count = bucket_count // 2
    exact_count = half_count // 2
    log_steps = half_count - exact_count
    bounds = []
    for section_index in range(1, log_steps):
        target = exact_count ** (log_steps - section_index) * max_distance**section_index
        lowest = exact_count
        while lowest**log_steps < target:
            lowest = lowest + 1
        bounds.append(lowest)
    onehot = np.zeros((2 * seq_len - 1, bucket_count), np.float32)
    for offset in range(2 * seq_len - 1):
        relative = offset - (seq_len - 1)
        distance = abs(relative)
        bucket = half_count if relative > 0 else 0
        if distance < exact_count:
            bucket = bucket + distance
        else:
            bucket = (
                bucket
                + exact_count
                + len([boundary for boundary in bounds if distance >= boundary])
            )
        onehot[offset, bucket] = 1.0
    return onehot


def matmul(left_side, right_side):
    return jnp.dot(left_side, right_side, preferred_element_type=jnp.float32)


def contract_rows(left_side, right_side):
    return lax.dot_general(
        left_side, right_side, (((0,), (0,)), ((), ())), preferred_element_type=jnp.float32
    )


def contract_cols(left_side, right_side):
    return lax.dot_general(
        left_side, right_side, (((1,), (1,)), ((), ())), preferred_element_type=jnp.float32
    )


def gelu_slope(values):
    factor = math.sqrt(2.0 / math.pi)
    tangent = jnp.tanh(factor * (values + gelu_cubic * values * values * values))
    return 0.5 * (1.0 + tangent) + 0.5 * values * (1.0 - tangent * tangent) * factor * (
        1.0 + 3.0 * gelu_cubic * values * values
    )


def rms_parts(values):
    inverse = lax.rsqrt(jnp.mean(values * values, axis=-1, keepdims=True) + epsilon)
    return (values * inverse, inverse)


def rms_back(unit_grad, unit_values, inverse):
    return inverse * (
        unit_grad - unit_values * jnp.mean(unit_grad * unit_values, axis=-1, keepdims=True)
    )


def position_bias(rel_table, onehot, seq_len):
    head_count = rel_table.shape[1]
    by_offset = lax.dot_general(
        rel_table.astype(jnp.float32), onehot, (((0,), (1,)), ((), ())), precision=exact
    )
    rolled = jnp.concatenate([by_offset[:, seq_len - 1 :], by_offset[:, : seq_len - 1]], axis=1)
    repeated = jnp.tile(rolled, (1, seq_len))[:, : seq_len * (2 * seq_len - 2)]
    return repeated.reshape(head_count, seq_len, 2 * seq_len - 2)[:, :, :seq_len]


def diagonal_sums(matrix, seq_len):
    head_count = matrix.shape[0]
    flipped = matrix[:, :, ::-1]
    padded = jnp.pad(flipped, ((0, 0), (0, 0), (0, seq_len)))
    skewed = padded.reshape(head_count, 2 * seq_len * seq_len)[:, : seq_len * (2 * seq_len - 1)]
    skewed = skewed.reshape(head_count, seq_len, 2 * seq_len - 1)
    return jnp.sum(skewed, axis=1)[:, ::-1]


def on_device(
    hidden_in,
    segment_ids,
    positives,
    attn_gain,
    w_query,
    w_key,
    w_value,
    w_attn_out,
    rel_table,
    ffn_gain,
    w_ffn_in,
    w_ffn_out,
    final_gain,
):
    row_count = hidden_in.shape[1]
    seq_len = hidden_in.shape[2]
    model_width = hidden_in.shape[3]
    head_count = rel_table.shape[1]
    head_width = model_width // head_count
    token_count = row_count * seq_len
    tokens = hidden_in.reshape(token_count, model_width).astype(jnp.float32)
    segments = segment_ids.reshape(row_count, seq_len)
    gain_one = attn_gain.astype(jnp.float32)
    gain_two = ffn_gain.astype(jnp.float32)
    gain_three = final_gain.astype(jnp.float32)
    onehot = jnp.asarray(bucket_onehot(seq_len, BUCKETS, MAX_DIST))
    unit_one, inverse_one = rms_parts(tokens)
    normed_one = (unit_one * gain_one).astype(jnp.bfloat16)
    query_proj = matmul(normed_one, w_query).astype(jnp.bfloat16)
    key_proj = matmul(normed_one, w_key).astype(jnp.bfloat16)
    value_proj = matmul(normed_one, w_value).astype(jnp.bfloat16)
    bias_full = position_bias(rel_table, onehot, seq_len)

    def split_heads(values):
        return values.reshape(row_count, seq_len, head_count, head_width)

    def row_scores(row_query, row_key, row_seg):
        same_item = row_seg[:, None] == row_seg[None, :]
        similarity_table = jnp.einsum(
            "shd,thd->hst", row_query, row_key, preferred_element_type=jnp.float32
        )
        return jnp.where(same_item[None], similarity_table + bias_full, far_below)

    def forward_row(packed):
        row_query, row_key, row_value, row_seg = packed
        masked_scores = row_scores(row_query, row_key, row_seg)
        row_peak = jnp.max(masked_scores, axis=-1, keepdims=True)
        exp_terms = jnp.exp(masked_scores - row_peak)
        summed = jnp.sum(exp_terms, axis=-1, keepdims=True)
        attn_probs = (exp_terms / summed).astype(jnp.bfloat16)
        combined_attention_output = jnp.einsum(
            "hst,thd->shd", attn_probs, row_value, preferred_element_type=jnp.float32
        )
        return (
            combined_attention_output.astype(jnp.bfloat16),
            (row_peak + jnp.log(summed))[:, :, 0],
        )

    attended, log_norms = lax.map(
        forward_row,
        (split_heads(query_proj), split_heads(key_proj), split_heads(value_proj), segments),
    )
    attended = attended.reshape(token_count, model_width)
    middle = tokens + matmul(attended, w_attn_out)
    unit_two, inverse_two = rms_parts(middle)
    normed_two = (unit_two * gain_two).astype(jnp.bfloat16)
    inner = matmul(normed_two, w_ffn_in)
    hidden = jax.nn.gelu(inner, approximate=True).astype(jnp.bfloat16)
    final_sum = middle + matmul(hidden, w_ffn_out)
    unit_three, inverse_three = rms_parts(final_sum)
    normed_three = unit_three * gain_three
    member = (segments[:, None, :] == jnp.arange(ITEM_ROW, dtype=jnp.int32)[None, :, None]).astype(
        jnp.float32
    )
    counts = jnp.sum(member, axis=-1, keepdims=True)
    pooled = (
        jnp.einsum(
            "ris,rsd->rid",
            member,
            normed_three.reshape(row_count, seq_len, model_width),
            precision=exact,
        )
        / counts
    )
    item_count = row_count * ITEM_ROW
    pooled = pooled.reshape(item_count, model_width)
    inverse_pool = lax.rsqrt(jnp.sum(pooled * pooled, axis=-1, keepdims=True) + epsilon)
    encoded_vector_list = pooled * inverse_pool
    half_items = item_count // 2
    tower_index = lax.axis_index("tower")
    rows_size = lax.axis_size("rows")
    is_query = tower_index == 0
    first_half = encoded_vector_list[:half_items]
    second_half = encoded_vector_list[half_items:]
    outgoing = jnp.where(is_query, second_half, first_half)
    incoming = from_partner(outgoing, "tower", 0)
    my_queries = jnp.where(is_query, first_half, incoming)
    local_passages = jnp.where(is_query, incoming, second_half)
    passage_list = lax.all_gather(local_passages, ("tower", "rows"), axis=0, tiled=True)
    total_items = passage_list.shape[0]
    similarity_table = (
        lax.dot_general(
            my_queries, passage_list, (((1,), (1,)), ((), ())), precision=exact
        )
        / logit_divisor
    )
    my_positive = lax.dynamic_slice_in_dim(positives, tower_index * half_items, half_items)
    column = (
        my_positive // half_items % 2 * (rows_size * half_items)
        + my_positive // item_count * half_items
        + my_positive % half_items
    )
    chosen_mask = (jnp.arange(total_items, dtype=jnp.int32)[None, :] == column[:, None]).astype(
        jnp.float32
    )
    row_peak = jnp.max(similarity_table, axis=1, keepdims=True)
    exp_terms = jnp.exp(similarity_table - row_peak)
    summed = jnp.sum(exp_terms, axis=1, keepdims=True)
    losses = (
        row_peak[:, 0] + jnp.log(summed[:, 0]) - jnp.sum(similarity_table * chosen_mask, axis=1)
    )
    similarity_derivative = loss_scale * (exp_terms / summed - chosen_mask)
    query_embedding_gradient = (
        jnp.dot(similarity_derivative, passage_list, precision=exact) / logit_divisor
    )
    doc_embed_grad = lax.psum_scatter(
        lax.dot_general(
            similarity_derivative, my_queries, (((0,), (0,)), ((), ())), precision=exact
        )
        / logit_divisor,
        ("tower", "rows"),
        scatter_dimension=0,
        tiled=True,
    )
    sendback = jnp.where(is_query, doc_embed_grad, query_embedding_gradient)
    received = from_partner(sendback, "tower", 0)
    embed_grad = jnp.where(
        is_query,
        jnp.concatenate([query_embedding_gradient, received], axis=0),
        jnp.concatenate([received, doc_embed_grad], axis=0),
    )
    inner_dot = jnp.sum(encoded_vector_list * embed_grad, axis=-1, keepdims=True)
    pooled_grad = inverse_pool * (embed_grad - encoded_vector_list * inner_dot)
    spread = member / counts
    three_grad = jnp.einsum(
        "ris,rid->rsd",
        spread,
        pooled_grad.reshape(row_count, ITEM_ROW, model_width),
        precision=exact,
    )
    three_grad = three_grad.reshape(token_count, model_width)
    final_gain_grad = jnp.sum(three_grad * unit_three, axis=0)
    final_grad = rms_back(three_grad * gain_three, unit_three, inverse_three)
    branch_two_grad = final_grad.astype(jnp.bfloat16)
    ffn_out_grad = contract_rows(hidden, branch_two_grad)
    inner_grad = (contract_cols(branch_two_grad, w_ffn_out) * gelu_slope(inner)).astype(
        jnp.bfloat16
    )
    ffn_in_grad = contract_rows(normed_two, inner_grad)
    two_grad = contract_cols(inner_grad, w_ffn_in)
    ffn_gain_grad = jnp.sum(two_grad * unit_two, axis=0)
    middle_grad = final_grad + rms_back(two_grad * gain_two, unit_two, inverse_two)
    branch_one_grad = middle_grad.astype(jnp.bfloat16)
    attn_out_grad = contract_rows(attended, branch_one_grad)
    attended_grad = contract_cols(branch_one_grad, w_attn_out).astype(jnp.bfloat16)

    def backward_row(bias_total, packed):
        row_query, row_key, row_value, row_seg, row_norm, row_grad = packed
        masked_scores = row_scores(row_query, row_key, row_seg)
        attn_probs = jnp.exp(masked_scores - row_norm[:, :, None])
        probs_grad = jnp.einsum(
            "shd,thd->hst", row_grad, row_value, preferred_element_type=jnp.float32
        )
        value_grad = jnp.einsum(
            "hst,shd->thd",
            attn_probs.astype(jnp.bfloat16),
            row_grad,
            preferred_element_type=jnp.float32,
        )
        score_part_grad = attn_probs * (
            probs_grad - jnp.sum(attn_probs * probs_grad, axis=-1, keepdims=True)
        )
        rounded = score_part_grad.astype(jnp.bfloat16)
        query_grad = jnp.einsum(
            "hst,thd->shd", rounded, row_key, preferred_element_type=jnp.float32
        )
        key_grad = jnp.einsum(
            "hst,shd->thd", rounded, row_query, preferred_element_type=jnp.float32
        )
        return (
            bias_total + score_part_grad,
            (
                query_grad.astype(jnp.bfloat16),
                key_grad.astype(jnp.bfloat16),
                value_grad.astype(jnp.bfloat16),
            ),
        )

    bias_total, head_grads = lax.scan(
        backward_row,
        jnp.zeros((head_count, seq_len, seq_len), jnp.float32),
        (
            split_heads(query_proj),
            split_heads(key_proj),
            split_heads(value_proj),
            segments,
            log_norms,
            split_heads(attended_grad),
        ),
    )
    query_grad = head_grads[0].reshape(token_count, model_width)
    key_grad = head_grads[1].reshape(token_count, model_width)
    value_grad = head_grads[2].reshape(token_count, model_width)
    table_local = jnp.einsum(
        "ib,hi->bh", onehot, diagonal_sums(bias_total, seq_len), precision=exact
    )
    query_w_grad = contract_rows(normed_one, query_grad)
    key_w_grad = contract_rows(normed_one, key_grad)
    value_w_grad = contract_rows(normed_one, value_grad)
    one_grad = (
        contract_cols(query_grad, w_query)
        + contract_cols(key_grad, w_key)
        + contract_cols(value_grad, w_value)
    )
    attn_gain_grad = jnp.sum(one_grad * unit_one, axis=0)
    input_grad = middle_grad + rms_back(one_grad * gain_one, unit_one, inverse_one)
    table_grad = lax.psum(table_local, ("tower", "rows"))
    shares = (
        lax.psum_scatter(attn_gain_grad, "rows", scatter_dimension=0, tiled=True),
        lax.psum_scatter(query_w_grad, "rows", scatter_dimension=0, tiled=True),
        lax.psum_scatter(key_w_grad, "rows", scatter_dimension=0, tiled=True),
        lax.psum_scatter(value_w_grad, "rows", scatter_dimension=0, tiled=True),
        lax.psum_scatter(attn_out_grad, "rows", scatter_dimension=0, tiled=True),
        lax.psum_scatter(ffn_gain_grad, "rows", scatter_dimension=0, tiled=True),
        lax.psum_scatter(ffn_in_grad, "rows", scatter_dimension=0, tiled=True),
        lax.psum_scatter(ffn_out_grad, "rows", scatter_dimension=0, tiled=True),
        lax.psum_scatter(final_gain_grad, "rows", scatter_dimension=0, tiled=True),
    )
    summed_grads = lax.psum(
        (
            shares[0],
            shares[1],
            shares[2],
            shares[3],
            shares[4],
            shares[5],
            shares[6],
            shares[7],
            shares[8],
        ),
        "tower",
    )
    return (
        encoded_vector_list[None],
        losses.reshape(1, 1, half_items),
        input_grad.reshape(hidden_in.shape),
        summed_grads[0],
        summed_grads[1],
        summed_grads[2],
        summed_grads[3],
        summed_grads[4],
        table_grad,
        summed_grads[5],
        summed_grads[6],
        summed_grads[7],
        summed_grads[8],
    )


def solution(mesh):
    in_specs = (
        P("tower", "rows", None, None),
        P("tower", "rows", None),
        P("rows"),
        P(),
        P(),
        P(),
        P(),
        P(),
        P(),
        P(),
        P(),
        P(),
        P(),
    )
    out_specs = (
        P("tower", "rows", None),
        P("rows", "tower", None),
        P("tower", "rows", None, None),
        P("rows"),
        P("rows", None),
        P("rows", None),
        P("rows", None),
        P("rows", None),
        P(),
        P("rows"),
        P("rows", None),
        P("rows", None),
        P("rows"),
    )
    axes = rows_axes(mesh)
    sized = mesh.shape["tower"] == 2 and tuple(ax.size for ax in axes) == STEPS_SIZES
    body = functools.partial(fused, axes) if sized else on_device
    return jax.shard_map(
        body, mesh=mesh, in_specs=in_specs, out_specs=out_specs, check_vma=False
    )
```

```python
import functools
import math

import jax
import jax.numpy as jnp
import numpy as np
from jax import lax
from jax.experimental import pallas as pl
from jax.experimental.pallas import tpu as pltpu
from jax.sharding import PartitionSpec as P

BUCKETS = 32
MAX_DIST = 128
ITEM_ROW = 8
BLOCK = 128

epsilon = 1e-06
logit_divisor = 0.01
loss_scale = 16.0
far_below = -1000000000.0
exact = lax.Precision.HIGHEST
gelu_cubic = 0.044715
gelu_factor = math.sqrt(2.0 / math.pi)
f32 = jnp.float32
bf16 = jnp.bfloat16
VMEM = pltpu.VMEM
VMEM_LIMIT = 62 * 2**20


def dot_nn(a, b, precision=None):
    return lax.dot_general(
        a, b, (((1,), (0,)), ((), ())), precision=precision, preferred_element_type=f32
    )


def dot_nt(a, b, precision=None):
    return lax.dot_general(
        a, b, (((1,), (1,)), ((), ())), precision=precision, preferred_element_type=f32
    )


def dot_tn(a, b, precision=None):
    return lax.dot_general(
        a, b, (((0,), (0,)), ((), ())), precision=precision, preferred_element_type=f32
    )


def bucket_of(relative, bucket_count, max_distance):
    half_count = bucket_count // 2
    exact_count = half_count // 2
    log_steps = half_count - exact_count
    bounds = []
    for section_index in range(1, log_steps):
        target = exact_count ** (log_steps - section_index) * max_distance**section_index
        lowest = exact_count
        while lowest**log_steps < target:
            lowest = lowest + 1
        bounds.append(lowest)
    distance = abs(relative)
    bucket = half_count if relative > 0 else 0
    if distance < exact_count:
        return bucket + distance
    return bucket + exact_count + len([b for b in bounds if distance >= b])


def lane_buckets():
    width = 4 * BLOCK
    onehot = np.zeros((BUCKETS, width), np.float32)
    for m in range(width):
        relative = (m if m < 3 * BLOCK else m - width) - BLOCK
        onehot[bucket_of(relative, BUCKETS, MAX_DIST), m] = 1.0
    return onehot


def row_of_gain(ref):
    return ref[...].astype(f32).reshape(1, ref.shape[0])


def rms_inverse(values):
    return lax.rsqrt(jnp.mean(values * values, axis=-1, keepdims=True) + epsilon)


def column_of(row):
    return jnp.broadcast_to(row, (8, row.shape[1])).T[:, 0:1]


def three_terms(values):
    high = values.astype(bf16)
    rest = values - high.astype(f32)
    middle = rest.astype(bf16)
    return high, middle, (rest - middle.astype(f32)).astype(bf16)


def key_range(block, blocks):
    return max(block - 1, 0) * BLOCK, min(block + 2, blocks) * BLOCK


MESH_IDS = pl.DeviceIdType.MESH
OUT, IN, ATTN, VALUE, QUERY, KEY = range(6)
OWN, END, SEND = 3, 4, 5
SPAN = 384
INNER, TWO, ATTENDED, HEADS, NORMED, ONE, SMALL = range(7)


class Axis:

    def __init__(self, size, stride):
        self.size, self.stride = size, stride

    def place(self, row):
        return lax.rem(lax.div(row, self.stride), self.size)


UNIT = 128
SLOTS = 3
JOBS = (
    ((0, 2, 1), ((OUT, 0, 0), (OUT, 0, 1),)),
    ((0, 1, 2), ((OUT, 0, 2), (OUT, 0, 3),)),
    ((2, 1, 0), ((OUT, 1, 0), (OUT, 1, 1),)),
    ((0, 2, 1), ((OUT, 1, 2), (OUT, 1, 3),)),
    ((1, 2, 0), ((OUT, 2, 0), (OUT, 2, 1), (OUT, 2, 2), (OUT, 2, 3),)),
    ((1, 0, 2), ((IN, 0, 0), (IN, 1, 0), (IN, 2, 0), (IN, 3, 0),)),
    ((0, 2, 1), ((IN, 4, 0), (IN, 5, 0), (IN, 6, 0), (IN, 7, 0),)),
    ((1, 2, 0), ((IN, 8, 0), (IN, 9, 0), (IN, 10, 0), (IN, 11, 0),)),
    ((0, 2, 1), ((ATTN, 0, 0), (ATTN, 1, 0), (ATTN, 2, 0),)),
    ((1, 0, 2), ((VALUE, 0, 0), (QUERY, 0, 0), (KEY, 0, 0),)),
    ((0, 1, 2), ((VALUE, 1, 0), (QUERY, 1, 0),)),
    ((1, 0, 2), ((KEY, 1, 0),)),
    ((0, 1, 2), ((VALUE, 2, 0),)),
    ((1, 0, 2), ((QUERY, 2, 0),)),
    ((0, 1, 2), ((KEY, 2, 0),)),
)
STEPS_SIZES = (2, 2, 4)
STEPS = (
    (0, SEND, 0), (2, SEND, 0), (4, SEND, 0), (0, OWN, 0), (0, 0, 0), (2, OWN, 0), (2, 0, 0), (4, OWN, 0),
    (4, 0, 0), (1, SEND, 0), (3, SEND, 0), (-1, INNER, 0), (1, OWN, 0), (1, 0, 0), (0, 0, 1), (0, 1, 0),
    (3, OWN, 0), (3, 0, 0), (2, 0, 1), (-1, INNER, 1), (-1, INNER, 2), (-1, INNER, 3), (-1, INNER, 4),
    (-1, INNER, 5), (2, 0, 2), (5, SEND, 0), (0, 1, 1), (1, 0, 1), (1, 1, 0), (6, SEND, 0), (4, 0, 1),
    (4, 1, 0), (7, SEND, 0), (5, OWN, 0), (5, 0, 0), (0, 1, 2), (2, 0, 3), (2, 1, 0), (6, OWN, 0), (6, 0, 0),
    (3, 0, 1), (3, 1, 0), (0, 1, 3), (0, 2, 0), (7, OWN, 0), (7, 0, 0), (1, 1, 1), (1, 2, 0), (-1, TWO, 0),
    (4, 1, 1), (8, SEND, 0), (-1, NORMED, 0), (-1, ATTENDED, 0), (3, 1, 1), (-1, HEADS, 0), (8, OWN, 0),
    (8, 0, 0), (5, 0, 1), (5, 1, 0), (1, 2, 1), (6, 0, 1), (6, 1, 0), (4, 1, 2), (0, 2, 1), (2, 1, 1),
    (2, 2, 0), (-1, HEADS, 3), (3, 1, 2), (0, END, 0), (9, SEND, 0), (-1, HEADS, 1), (3, 1, 3), (3, 2, 0),
    (9, OWN, 0), (9, 0, 0), (6, 1, 1), (1, 2, 2), (4, 1, 3), (4, 2, 0), (-1, HEADS, 4), (8, 0, 1), (8, 1, 0),
    (1, 2, 3), (10, SEND, 0), (6, 1, 2), (1, END, 0), (11, SEND, 0), (-1, HEADS, 2), (3, 2, 1), (10, OWN, 0),
    (10, 0, 0), (11, OWN, 0), (11, 0, 0), (6, 1, 3), (6, 2, 0), (5, 1, 1), (5, 2, 0), (2, 2, 1), (7, 0, 1),
    (7, 1, 0), (8, 1, 1), (3, END, 0), (2, END, 0), (-1, HEADS, 5), (4, 2, 1), (12, SEND, 0), (8, 1, 2),
    (5, 2, 1), (4, END, 0), (13, SEND, 0), (12, OWN, 0), (12, 0, 0), (14, SEND, 0), (-1, ONE, 0), (9, 0, 1),
    (9, 1, 0), (10, 0, 1), (10, 1, 0), (13, OWN, 0), (13, 0, 0), (14, OWN, 0), (14, 0, 0), (5, 2, 2),
    (11, 0, 1), (11, 1, 0), (8, 1, 3), (8, 2, 0), (-1, SMALL, 0), (12, 0, 1), (12, 1, 0), (6, 2, 1),
    (7, 1, 1), (-1, SMALL, 1), (5, 2, 3), (6, END, 0), (5, END, 0), (10, 1, 1), (10, 2, 0), (7, 1, 2),
    (9, 1, 1), (9, 2, 0), (10, 2, 1), (13, 0, 1), (13, 1, 0), (14, 0, 1), (14, 1, 0), (8, 2, 1), (7, 1, 3),
    (7, 2, 0), (10, 2, 2), (8, END, 0), (9, 2, 1), (11, 1, 1), (11, 2, 0), (12, 1, 1), (12, 2, 0), (10, 2, 3),
    (9, 2, 2), (11, 2, 1), (10, END, 0), (12, 2, 1), (13, 1, 1), (13, 2, 0), (14, 1, 1), (14, 2, 0),
    (-1, SMALL, 2), (11, 2, 2), (9, 2, 3), (13, 2, 1), (12, 2, 2), (7, 2, 1), (9, END, 0), (14, 2, 1),
    (7, END, 0), (11, 2, 3), (13, 2, 2), (12, 2, 3), (11, END, 0), (14, 2, 2), (12, END, 0), (13, 2, 3),
    (14, 2, 3), (-1, SMALL, 3), (13, END, 0), (14, END, 0),
)


def layer_kernel(axes, *refs):
    jobs = len(JOBS)
    (
        x_ref, seg_ref, pos_ref, g1_ref, g2_ref, g3_ref, table_ref, lanes_ref,
        wq_h, wk_h, wv_h, wo_h, w1_h, w2_h,
        emb_o, loss_o, small_o, gh_o, inner_o,
    ) = refs[:19]
    res, refs = refs[19 : 19 + jobs], refs[19 + jobs :]
    (
        all_e, gs, hid, ig, chunk, wslot, q, k, v, att, nrm, br2, br1, mid, fin, by_offset, d_all,
        sm, sm_core, sm_plane, sm_line, stg,
    ) = refs[:22]
    accs, landings, refs = refs[22 : 22 + jobs], refs[22 + jobs : 22 + 4 * jobs], refs[22 + 4 * jobs :]
    load_sem, ag_s, ag_r, sm_s, sm_r, tow_s, tow_r, end_s, end_r, end_l, line_s, line_r = refs

    t = lax.axis_index("tower")
    row = lax.axis_index("rows")
    place = [ax.place(row) for ax in axes]
    nx, ny, nz = (ax.size for ax in axes)
    sx, sy, sz = (ax.stride for ax in axes)
    plane_size = nx * ny
    plane = place[1] * nx + place[0]
    spot = plane * nz + place[2]

    def row_of(w, z):
        return lax.rem(w, nx) * sx + lax.div(w, nx) * sy + z * sz

    z_peers = [(t, row_of(plane, lax.rem(place[2] + m, nz))) for m in range(1, nz)]
    plane_peers = [(t, row_of(lax.rem(plane + m, plane_size), place[2])) for m in range(1, plane_size)]
    partner = (1 - t, row)

    barrier = pltpu.get_barrier_semaphore()
    for peer in z_peers + plane_peers + [partner]:
        pl.semaphore_signal(barrier, inc=1, device_id=peer, device_id_type=MESH_IDS)

    def load(i, src, dst):
        return pltpu.make_async_copy(src, dst, load_sem.at[i])

    def remote(src, dst, ss, rs, to):
        return pltpu.make_async_remote_copy(
            src_ref=src, dst_ref=dst, send_sem=ss, recv_sem=rs, device_id=to, device_id_type=MESH_IDS
        )

    seq, width = x_ref.shape
    heads = table_ref.shape[0]
    ff = hid.shape[1]
    piece = 512
    pieces = ff // piece
    blocks = seq // BLOCK
    tail = width - seq
    square_loads = [
        load(i, w, wslot.at[pl.ds(i * width, width)]) for i, w in enumerate((wq_h, wk_h, wv_h, wo_h))
    ]
    ahead_loads = [load(4, w1_h.at[pl.ds(0, seq)], ig)]
    tails = []
    for c in range(ff // width):
        held = (br2 if c < 2 else br1).at[pl.ds(c % 2 * tail, tail)]
        tails.append(held)
        ahead_loads.append(load(5 + c, w1_h.at[pl.ds(seq, tail), pl.ds(c * width, width)], held))
    w2_load = load(9, w2_h, wslot)
    back_loads = [
        load(10 + c, w1_h.at[:, pl.ds(c * width, width)], wslot.at[pl.ds(c * width, width)])
        for c in range(ff // width)
    ]
    gh_store = load(14, fin, gh_o)
    kept = [load(15 + c, chunk.at[c % 2], inner_o.at[:, pl.ds(c * piece, piece)]) for c in range(pieces - 2)]
    fetched = [load(15 + c, inner_o.at[:, pl.ds(c * piece, piece)], chunk.at[c % 2]) for c in range(pieces - 2)]
    for w in square_loads[:3]:
        w.start()

    def normed(values, gain_ref):
        return ((values * rms_inverse(values)) * row_of_gain(gain_ref)).astype(bf16)

    nrm[...] = normed(x_ref[...].astype(f32), g1_ref)
    square_loads[3].start()
    for w in ahead_loads:
        w.start()
    for i, out in enumerate((q, k, v)):
        square_loads[i].wait()
        out[...] = dot_nn(nrm[...], wslot[i * width : (i + 1) * width, :]).astype(bf16)

    seg_row = seg_ref[...].astype(f32)
    low_half = lax.broadcasted_iota(jnp.int32, (BLOCK, BLOCK), 1) < BLOCK // 2

    def bias_tile(h, first, last):
        n = h % 4 * BLOCK
        if h < 8:
            lane = h // 4 * 3 * BLOCK
            return fin[n : n + BLOCK, lane + first : lane + last]
        return chunk[0, n : n + BLOCK, first:last]

    def build_tiles():
        by_offset[0:heads, :] = dot_nn(table_ref[...], lanes_ref[...])
        for h in range(heads):
            spread = jnp.broadcast_to(by_offset[h : h + 1, :], (BLOCK, 4 * BLOCK))
            tile = pltpu.roll(spread, 0, 1, stride=1, stride_axis=0)[:, : 3 * BLOCK]
            n = h % 4 * BLOCK
            if h < 8:
                lane = h // 4 * 3 * BLOCK
                fin[n : n + BLOCK, lane : lane + 3 * BLOCK] = tile
            else:
                chunk[0, n : n + BLOCK, 0 : 3 * BLOCK] = tile
        seg_col = column_of(seg_row)
        for b in range(blocks):
            lo, hi = key_range(b, blocks)
            first = lo - (b - 1) * BLOCK
            same = seg_col[b * BLOCK : (b + 1) * BLOCK] == seg_row[:, lo:hi]
            chunk[1, b * BLOCK : (b + 1) * BLOCK, first : first + hi - lo] = jnp.where(same, 0.0, far_below)

    def two_heads(values):
        zero = jnp.zeros_like(values)
        return jnp.concatenate([jnp.where(low_half, values, zero), jnp.where(low_half, zero, values)], axis=0)

    def probabilities(pair, b, both, keys):
        lo, hi = key_range(b, blocks)
        first = lo - (b - 1) * BLOCK
        last = first + hi - lo
        mask = chunk[1, b * BLOCK : (b + 1) * BLOCK, first:last]
        s = dot_nt(both, keys)
        parts = []
        for e in range(2):
            part = s[e * BLOCK : (e + 1) * BLOCK] + bias_tile(2 * pair + e, first, last) + mask
            terms = jnp.exp(part - jnp.max(part, axis=-1, keepdims=True))
            parts.append(terms * (1.0 / jnp.sum(terms, axis=-1, keepdims=True)))
        return parts

    build_tiles()
    for pair in range(heads // 2):
        lanes = slice(pair * UNIT, (pair + 1) * UNIT)
        for b in range(blocks):
            lo, hi = key_range(b, blocks)
            mine = slice(b * BLOCK, (b + 1) * BLOCK)
            parts = probabilities(pair, b, two_heads(q[mine, lanes]), k[lo:hi, lanes])
            probs = jnp.concatenate([part.astype(bf16) for part in parts], axis=0)
            out = dot_nn(probs, v[lo:hi, lanes])
            att[mine, lanes] = jnp.where(low_half, out[:BLOCK], out[BLOCK:]).astype(bf16)

    square_loads[3].wait()
    middle = x_ref[...].astype(f32) + dot_nn(att[...], wslot[3 * width : 4 * width, :])
    w2_load.start()
    mid[...] = middle
    nrm[...] = normed(middle, g2_ref)
    for w in ahead_loads:
        w.wait()
    for c in range(pieces):
        low = c * piece
        inner = dot_nn(nrm[:, 0:seq], ig[:, low : low + piece])
        rest = []
        while low < (c + 1) * piece:
            n = low // width
            high = min((c + 1) * piece, (n + 1) * width)
            rest.append(dot_nn(nrm[:, seq:width], tails[n][:, low - n * width : high - n * width]))
            low = high
        inner = inner + (jnp.concatenate(rest, axis=1) if len(rest) > 1 else rest[0])
        if c >= 2:
            kept[c - 2].wait()
        chunk[c % 2] = inner
        if c < pieces - 2:
            kept[c].start()
        tangent = jnp.tanh(gelu_factor * (inner + gelu_cubic * (inner * inner * inner)))
        hid[:, c * piece : (c + 1) * piece] = (inner * (0.5 * (1.0 + tangent))).astype(bf16)
    w2_load.wait()
    final = mid[...] + dot_nn(hid[...], wslot[...])
    fin[...] = final
    member = (lax.broadcasted_iota(jnp.int32, (ITEM_ROW, seq), 0).astype(f32) == seg_row).astype(f32)
    counts = jnp.sum(member, axis=-1, keepdims=True)
    ones = member.astype(bf16)
    high, middle_part, low_part = three_terms((final * rms_inverse(final)) * row_of_gain(g3_ref))
    pooled = (dot_nn(ones, high) + (dot_nn(ones, middle_part) + dot_nn(ones, low_part))) / counts

    inverse_pool = lax.rsqrt(jnp.sum(pooled * pooled, axis=-1, keepdims=True) + epsilon)
    own_e = pooled * inverse_pool
    emb_o[...] = own_e
    own_rows = pl.ds(pl.multiple_of(spot * ITEM_ROW, ITEM_ROW), ITEM_ROW)

    def bits(n):
        return n.bit_length() - 1

    p = pos_ref[...]
    of_row = p >> bits(ITEM_ROW)

    def along(ax):
        return (of_row >> bits(ax.stride)) & (ax.size - 1)

    p = ((along(axes[1]) * nx + along(axes[0])) * nz + along(axes[2])) * ITEM_ROW + (p & (ITEM_ROW - 1))
    i8 = lax.broadcasted_iota(jnp.int32, (ITEM_ROW, ITEM_ROW), 0)
    j8 = lax.broadcasted_iota(jnp.int32, (ITEM_ROW, ITEM_ROW), 1)
    diag = jnp.where(i8 == j8, jnp.broadcast_to(p.astype(f32), (ITEM_ROW, ITEM_ROW)), 0.0)
    pos_col = jnp.sum(diag, axis=-1, keepdims=True)
    all_e[t, own_rows, 0:width] = own_e
    all_e[t, own_rows, width : width + UNIT] = jnp.broadcast_to(pos_col, (ITEM_ROW, UNIT))

    pl.semaphore_wait(barrier, len(z_peers) + len(plane_peers) + 1)

    def column_rows(w):
        return pl.ds(pl.multiple_of(w * (nz * ITEM_ROW), ITEM_ROW), nz * ITEM_ROW)

    def item_rows(w, z):
        return pl.ds(pl.multiple_of((w * nz + z) * ITEM_ROW, ITEM_ROW), ITEM_ROW)

    sent = []

    def spread(index, rows, peer):
        block = all_e.at[t, rows]
        sent.append(remote(block, block, ag_s.at[index], ag_r.at[index], peer))
        sent[-1].start()
        return sent[-1]

    along_z = [spread(m, own_rows, peer) for m, peer in enumerate(z_peers)]
    count = len(z_peers)

    def over_plane(m):
        rows = item_rows(plane, lax.rem(place[2] + nz - m, nz))
        first = count + m * len(plane_peers)
        return [spread(first + j, rows, peer) for j, peer in enumerate(plane_peers)]

    in_plane = [over_plane(0)]
    inverse = rms_inverse(fin[...])
    fin[...] = fin[...] * inverse
    sm[...] = jnp.zeros_like(sm)
    for m in range(1, nz):
        along_z[m - 1].wait_recv()
        in_plane.append(over_plane(m))
    count += nz * len(plane_peers)
    to_tower = [spread(count, column_rows(plane), partner)]
    for j in range(1, plane_size):
        for m in range(nz):
            in_plane[m][j - 1].wait_recv()
        rows = column_rows(lax.rem(plane + plane_size - j, plane_size))
        to_tower.append(spread(count + j, rows, partner))
    for c in to_tower:
        c.wait_recv()

    queries, docs = all_e[0, :, 0:width], all_e[1, :, 0:width]
    items = queries.shape[0]
    scores = dot_nt(queries, docs, exact) / logit_divisor
    top = jnp.max(scores, axis=1, keepdims=True)
    terms = jnp.exp(scores - top)
    summed = jnp.sum(terms, axis=1, keepdims=True)
    chosen = (
        lax.broadcasted_iota(jnp.int32, (items, items), 1).astype(f32) == all_e[0, :, width : width + 1]
    ).astype(f32)
    slope = loss_scale * (terms / summed - chosen)

    @pl.when(t == 0)
    def _():
        gs[...] = slope

    @pl.when(t == 1)
    def _():
        gs[...] = slope.T

    embed_grad = dot_nn(gs[own_rows, :], all_e[1 - t, :, 0:width], exact) / logit_divisor
    inner_dot = jnp.sum(own_e * embed_grad, axis=-1, keepdims=True)
    pooled_grad = inverse_pool * (embed_grad - own_e * inner_dot)

    terms_of_grad = jnp.concatenate([part.astype(f32) for part in three_terms(pooled_grad / counts)], axis=0)
    three_grad = dot_tn(jnp.concatenate([member] * 3, axis=0).astype(bf16), terms_of_grad.astype(bf16))
    unit = fin[...]
    sm[0:1, 0:width] = jnp.sum(three_grad * unit, axis=0, keepdims=True)
    u = three_grad * row_of_gain(g3_ref)
    final_grad = inverse * (u - unit * jnp.mean(u * unit, axis=-1, keepdims=True))
    fin[...] = final_grad
    br2[...] = final_grad.astype(bf16)

    def write_losses():
        losses = top + jnp.log(summed) - jnp.sum(scores * chosen, axis=1, keepdims=True)
        loss_row = jnp.broadcast_to(losses, (items, UNIT)).T[0:8, :]
        pick = (
            lax.broadcasted_iota(jnp.int32, (items, UNIT), 0)
            == lax.broadcasted_iota(jnp.int32, (items, UNIT), 1) + spot * ITEM_ROW + t * (ITEM_ROW // 2)
        ).astype(f32)
        loss_o[...] = dot_nn(loss_row, pick, exact)

    chunk_rows = width // (nx * ny * nz)
    lefts = (hid, nrm, att, nrm, nrm, nrm)
    rights = (br2, ig, br1, v, q, k)
    in_slot = {}
    unwaited = []

    def spots(path):
        found = {}
        for r in range(nx * ny * nz):
            number = 0
            for a in path:
                number = number * axes[a].size + (r // axes[a].stride) % axes[a].size
            found[r] = number * chunk_rows
        return found

    def product(job, half, keep):
        path, parts = JOBS[job]
        lhs = lefts[parts[0][0]]
        stripes = list(dict.fromkeys((target, block) for target, block, _ in parts))
        subs = lhs.shape[1] // width
        group = SPAN // (subs * chunk_rows)
        where = spots(path)

        def step(i, carry):
            right = []
            for target, block in stripes:
                rhs = rights[target]
                lane = half * (rhs.shape[1] // 2) + block * UNIT
                right.append(rhs[:, pl.ds(pl.multiple_of(lane, UNIT), UNIT)])
            columns = pl.ds(pl.multiple_of(i * SPAN, UNIT), SPAN)
            value = dot_tn(lhs[:, columns], jnp.concatenate(right, axis=1) if len(right) > 1 else right[0])
            moved = sum(lax.rem(lax.div(i * group, ax.stride), ax.size) * where[ax.stride] for ax in axes)
            for r in range(group):
                at_row = pl.multiple_of(moved + where[r], 8)
                for n, (target, block, sub) in enumerate(parts):
                    low = (r * subs + sub) * chunk_rows
                    lane = stripes.index((target, block)) * UNIT
                    keep(n, pl.ds(at_row, chunk_rows), value[low : low + chunk_rows, lane : lane + UNIT])
            return carry

        lax.fori_loop(0, lhs.shape[1] // SPAN, step, 0, unroll=2 if subs > 1 else 1)

    def tower_copy(job, slot):
        units = len(JOBS[job][1])
        return remote(stg.at[slot, pl.ds(0, units)], accs[job], tow_s.at[job], tow_r.at[job], partner)

    def send_half(job):
        slot = len(in_slot) % SLOTS
        before = [n for n, s in in_slot.items() if s == slot]
        if before:
            tower_copy(before[-1], slot).wait_send()
            unwaited.remove(before[-1])

        def keep(n, rows, value):
            stg[slot, n, rows, :] = value

        product(job, 1 - t, keep)
        tower_copy(job, slot).start()
        in_slot[job] = slot
        unwaited.append(job)

    def take_own(job):
        acc = accs[job]
        tower_copy(job, 0).wait_recv()

        def keep(n, rows, value):
            acc[n, rows, :] = acc[n, rows, :] + value

        product(job, t, keep)

    def geometry(job, leg):
        path = JOBS[job][0]
        low, size = 0, width
        for a in path[:leg]:
            size = size // axes[a].size
            low = low + place[a] * size
        return low, size // axes[path[leg]].size, axes[path[leg]], place[path[leg]]

    def line_copy(job, leg, i, block):
        low, size, axis, _ = geometry(job, leg)
        n = axis.size
        if block > i:
            to, slot = (t, row + axis.stride), (0 if n == 2 else block)
        else:
            to, slot = (t, row - axis.stride), (0 if n == 2 else n if block == i - 1 else block)
        at_row = pl.multiple_of(low + block * size, 8)
        return remote(
            accs[job].at[:, pl.ds(at_row, size)], landings[3 * job + leg].at[slot],
            line_s.at[job, leg, block], line_r.at[job, leg, slot], to,
        )

    def take(job, leg, block, slot):
        low, size, axis, _ = geometry(job, leg)
        at_row = pl.multiple_of(low + block * size, 8)
        acc, landed = accs[job], landings[3 * job + leg]
        remote(
            landed.at[slot], landed.at[slot], line_s.at[job, leg, block], line_r.at[job, leg, slot], partner
        ).wait_recv()
        acc[:, pl.ds(at_row, size), :] = acc[:, pl.ds(at_row, size), :] + landed[slot]

    def line_step(job, leg, s):
        _, _, axis, my_place = geometry(job, leg)
        n = axis.size
        for i in range(n):
            from_left = s == i and i < n - 1
            from_right = s == n - 1 - i and i > 0
            last = s == n - 1
            if not (from_left or from_right or last):
                continue

            @pl.when(my_place == i)
            def _():
                if from_left:
                    for block in range(n - 1, i, -1):
                        if i > 0:
                            take(job, leg, block, block)
                        line_copy(job, leg, i, block).start()
                if from_right:
                    for block in range(i):
                        if i < n - 1:
                            take(job, leg, block, block)
                        line_copy(job, leg, i, block).start()
                if last:
                    if n == 2:
                        take(job, leg, i, 0)
                    else:
                        if i > 0:
                            take(job, leg, i, i)
                        if i < n - 1:
                            take(job, leg, i, n)

        if s == n - 1 and leg == 2:
            end_copy(job, True).start()
            end_copy(job, False).start()

    def line_drain(job, leg):
        _, _, axis, my_place = geometry(job, leg)
        for i in range(axis.size):

            @pl.when(my_place == i)
            def _():
                for block in range(axis.size):
                    if block != i:
                        line_copy(job, leg, i, block).wait_send()

    def end_copy(job, to_partner):
        low, size, _, my_place = geometry(job, 2)
        at_row = pl.multiple_of(low + my_place * size, 8)
        src, dst = accs[job].at[:, pl.ds(at_row, size)], res[job].at[t]
        if to_partner:
            return remote(src, dst, end_s.at[job], end_r.at[job], partner)
        return pltpu.make_async_copy(src, dst, end_l.at[job])

    def inner_step(n):
        c = (n + pieces - 2) % pieces
        if n >= 2:
            fetched[c].wait()
        v_in = chunk[c % 2]
        grad = dot_nt(br2[...], wslot[c * piece : (c + 1) * piece, :])
        tangent = jnp.tanh(gelu_factor * (v_in + gelu_cubic * (v_in * v_in * v_in)))
        ahead = 0.5 * (1.0 + tangent) + 0.5 * v_in * (1.0 - tangent * tangent) * gelu_factor * (
            1.0 + 3.0 * gelu_cubic * v_in * v_in
        )
        ig[:, c * piece : (c + 1) * piece] = (grad * ahead).astype(bf16)
        if n + 2 < pieces:
            fetched[n].start()
        if n == pieces - 1:
            for w in back_loads:
                w.start()

    def norm_back(grad, values, gain):
        inverse = rms_inverse(values)
        unit = values * inverse
        total = jnp.sum(grad * unit, axis=0, keepdims=True)
        w = grad * gain
        return inverse * (w - unit * jnp.mean(w * unit, axis=-1, keepdims=True)), total

    tokens = 256

    def two_step():
        for w in back_loads:
            w.wait()
        gain = row_of_gain(g2_ref)
        for low in range(0, seq, tokens):
            part = slice(low, low + tokens)
            grad = dot_nt(ig[part, 0:width], wslot[0:width, :])
            for c in range(1, ff // width):
                lanes = slice(c * width, (c + 1) * width)
                grad = grad + dot_nt(ig[part, lanes], wslot[lanes, :])
            back, total = norm_back(grad, mid[part, :], gain)
            sm[1:2, 0:width] = sm[1:2, 0:width] + total
            middle_grad = fin[part, :] + back
            mid[part, :] = middle_grad
            br1[part, :] = middle_grad.astype(bf16)
        for w in square_loads:
            w.start()
        build_tiles()

    def attended_step():
        for w in square_loads:
            w.wait()
        br2[...] = dot_nt(br1[...], wslot[3 * width : 4 * width, :]).astype(bf16)
        d_all[...] = jnp.zeros_like(d_all)

    turned = [lax.broadcasted_iota(jnp.int32, (BLOCK, BLOCK), n) for n in range(2)]
    upside = (turned[0] + turned[1] == BLOCK - 1).astype(bf16)

    def upside_down(values):
        high, middle_part, low_part = three_terms(values)
        return dot_nn(upside, high) + (dot_nn(upside, middle_part) + dot_nn(upside, low_part))

    def heads_step(pair):
        lanes = slice(pair * UNIT, (pair + 1) * UNIT)
        columns = [[None] * 3, [None] * 3]
        key_grads, value_grads = [None] * blocks, [None] * blocks

        def put(held, n, value):
            held[n] = value if held[n] is None else held[n] + value

        for b in range(blocks):
            lo, hi = key_range(b, blocks)
            mine = slice(b * BLOCK, (b + 1) * BLOCK)
            first = lo - (b - 1) * BLOCK
            keys = k[lo:hi, lanes]
            both_q, both_o = two_heads(q[mine, lanes]), two_heads(br2[mine, lanes])
            probs = probabilities(pair, b, both_q, keys)
            pg = dot_nt(both_o, v[lo:hi, lanes])
            grads = []
            for e in range(2):
                ds = pg[e * BLOCK : (e + 1) * BLOCK]
                ds = probs[e] * (ds - jnp.sum(probs[e] * ds, axis=-1, keepdims=True))
                for n in range((hi - lo) // BLOCK):
                    put(columns[e], first // BLOCK + n, ds[:, n * BLOCK : (n + 1) * BLOCK])
                grads.append(ds.astype(bf16))
            rounded = jnp.concatenate(grads, axis=0)
            dq = dot_nn(rounded, keys)
            dk = dot_tn(rounded, both_q)
            dv = dot_tn(jnp.concatenate([part.astype(bf16) for part in probs], axis=0), both_o)
            for n in range((hi - lo) // BLOCK):
                rows = slice(n * BLOCK, (n + 1) * BLOCK)
                put(key_grads, lo // BLOCK + n, dk[rows])
                put(value_grads, lo // BLOCK + n, dv[rows])
            q[mine, lanes] = jnp.where(low_half, dq[:BLOCK], dq[BLOCK:]).astype(bf16)
        for b in range(blocks):
            mine = slice(b * BLOCK, (b + 1) * BLOCK)
            k[mine, lanes] = key_grads[b].astype(bf16)
            v[mine, lanes] = value_grads[b].astype(bf16)
        for e in range(2):
            wide = jnp.concatenate(columns[e] + [jnp.zeros((BLOCK, BLOCK), f32)], axis=1)
            skewed = pltpu.roll(upside_down(wide), 3 * BLOCK + 1, 1, stride=1, stride_axis=0)
            d_all[2 * pair + e : 2 * pair + e + 1, :] = jnp.sum(skewed, axis=0, keepdims=True)

    def normed_step():
        nrm[...] = normed(x_ref[...].astype(f32), g1_ref)

    def one_step():
        gain = row_of_gain(g1_ref)
        for low in range(0, seq, tokens):
            part = slice(low, low + tokens)
            grad = dot_nt(q[part, :], wslot[0:width, :])
            grad = grad + dot_nt(k[part, :], wslot[width : 2 * width, :])
            grad = grad + dot_nt(v[part, :], wslot[2 * width : 3 * width, :])
            back, total = norm_back(grad, x_ref[part, :].astype(f32), gain)
            sm[2:3, 0:width] = sm[2:3, 0:width] + total
            fin[part, :] = mid[part, :] + back
        gh_store.start()
        write_losses()

    small_first = remote(sm, sm_core, sm_s.at[0], sm_r.at[0], partner)
    base = 1 + len(plane_peers)
    own_plane, own_line = sm_plane.at[plane], sm_line.at[place[2]]
    small_second = [
        remote(own_plane, own_plane, sm_s.at[1 + m], sm_r.at[1 + m], peer) for m, peer in enumerate(plane_peers)
    ]
    small_third = [
        remote(own_line, own_line, sm_s.at[base + m], sm_r.at[base + m], peer) for m, peer in enumerate(z_peers)
    ]

    def small_step(s):
        if s == 0:
            table_grad = dot_nt(d_all[...], lanes_ref[...].astype(f32), exact)
            for n in range(2):
                sm[:, width + n * UNIT : width + n * UNIT + BUCKETS] = table_grad[8 * n : 8 * n + 8, :]
            small_first.start()
        elif s == 1:
            small_first.wait()
            sm_plane[plane] = sm[...] + sm_core[...]
            for c in small_second:
                c.start()
        elif s == 2:
            for c in small_second:
                c.wait()
            total = sm_plane[0]
            for w in range(1, plane_size):
                total = total + sm_plane[w]
            sm_line[place[2]] = total
            for c in small_third:
                c.start()
        else:
            for c in small_third:
                c.wait()
            total = sm_line[0]
            for w in range(1, nz):
                total = total + sm_line[w]
            small_o[...] = total

    layer_steps = {
        INNER: inner_step, TWO: lambda n: two_step(), ATTENDED: lambda n: attended_step(), HEADS: heads_step,
        NORMED: lambda n: normed_step(), ONE: lambda n: one_step(), SMALL: small_step,
    }
    for job, leg, s in STEPS:
        if job < 0:
            layer_steps[leg](s)
        elif leg == SEND:
            send_half(job)
        elif leg == OWN:
            take_own(job)
        elif leg == END:
            end_copy(job, True).wait_recv()
            end_copy(job, False).wait()
        else:
            line_step(job, leg, s)
    for c in sent:
        c.wait_send()
    for job in unwaited:
        tower_copy(job, in_slot[job]).wait_send()
    for job in range(jobs):
        for leg in range(3):
            line_drain(job, leg)
        end_copy(job, True).wait_send()
    gh_store.wait()


def layer_call(axes, args):
    seq, width = args[0].shape
    ff = args[12].shape[1]
    nx, ny, nz = (ax.size for ax in axes)
    rows = nx * ny * nz
    chunk_rows = width // rows
    s = jax.ShapeDtypeStruct
    vm, hbm = pl.BlockSpec(memory_space=VMEM), pl.BlockSpec(memory_space=pl.ANY)
    small = (8, width + 2 * UNIT)
    most_units = max(len(parts) for _, parts in JOBS)
    outs = [
        s((ITEM_ROW, width), f32), s((8, UNIT), f32), s(small, f32), s((seq, width), f32), s((seq, ff), f32),
    ]
    outs += [s((2, len(parts), chunk_rows, UNIT), f32) for _, parts in JOBS]
    scratch = [
        VMEM((2, rows * ITEM_ROW, width + UNIT), f32), VMEM((rows * ITEM_ROW, rows * ITEM_ROW), f32),
        VMEM((seq, ff), bf16), VMEM((seq, ff), bf16), VMEM((2, seq, 512), f32), VMEM((ff, width), bf16),
    ]
    scratch += [VMEM((seq, width), bf16)] * 7 + [VMEM((seq, width), f32)] * 2
    scratch += [
        VMEM((16, 4 * BLOCK), f32), VMEM((16, 4 * BLOCK), f32),
        VMEM(small, f32), VMEM(small, f32), VMEM((nx * ny, *small), f32), VMEM((nz, *small), f32),
        VMEM((SLOTS, most_units, width, UNIT), f32),
    ]
    scratch += [VMEM((len(parts), width, UNIT), f32) for _, parts in JOBS]
    for path, parts in JOBS:
        size = width
        for a in path:
            n = axes[a].size
            size = size // n
            scratch.append(VMEM((1 if n == 2 else n + 1, len(parts), size, UNIT), f32))
    dma = pltpu.SemaphoreType.DMA
    jobs, most = len(JOBS), max(nx, ny, nz)
    gathers = nz - 1 + nz * (nx * ny - 1) + nx * ny
    smalls = nz + nx * ny - 1
    scratch += [
        dma((19,)), dma((gathers,)), dma((gathers,)), dma((smalls,)), dma((smalls,)),
        dma((jobs,)), dma((jobs,)), dma((jobs,)), dma((jobs,)), dma((jobs,)),
        dma((jobs, 3, most)), dma((jobs, 3, most + 1)),
    ]
    return pl.pallas_call(
        functools.partial(layer_kernel, axes),
        name="layer",
        out_shape=outs,
        in_specs=[vm] * 8 + [hbm] * 6,
        out_specs=[vm] * 3 + [hbm] * (2 + jobs),
        scratch_shapes=scratch,
        compiler_params=pltpu.CompilerParams(
            collective_id=0, has_side_effects=True, vmem_limit_bytes=VMEM_LIMIT
        ),
    )(*args)


def place_kernel(emb, loss, small, gh, *refs):
    res = refs[: len(JOBS)]
    (
        emb_o, loss_o, gh_o, attn_gain_o, query_o, key_o, value_o, attn_o, table_o, ffn_gain_o, in_o, out_o, final_gain_o,
    ) = refs[len(JOBS) :]
    row = lax.axis_index("rows")
    targets = (out_o, in_o, attn_o, value_o, query_o, key_o)
    emb_o[0] = emb[...]
    gh_o[0, 0] = gh[...]
    for job, (_, parts) in enumerate(JOBS):
        for n, (target, block, sub) in enumerate(parts):
            out, height = targets[target], res[job].shape[2]
            for t in range(2):
                low = t * (out.shape[1] // 2) + block * UNIT
                out[sub * height : (sub + 1) * height, low : low + UNIT] = res[job][t, n]
    loss_o[0] = loss[0:1, 0 : loss_o.shape[2]]
    width = gh.shape[1]
    share = attn_gain_o.shape[0]
    pick = (
        lax.broadcasted_iota(jnp.int32, (width, UNIT), 0)
        == lax.broadcasted_iota(jnp.int32, (width, UNIT), 1) + row * share
    ).astype(f32)
    gains = dot_nn(small[:, 0:width], pick, exact)
    for n, out in enumerate((final_gain_o, ffn_gain_o, attn_gain_o)):
        out[...] = gains[n, 0:share]
    heads = table_o.shape[0]
    for low in range(0, heads, 8):
        lane = width + low // 8 * UNIT
        high = min(low + 8, heads)
        table_o[low:high, :] = small[0 : high - low, lane : lane + BUCKETS]


def place_call(axes, heads, emb, loss, small, gh, res):
    seq, width = gh.shape
    ff = 4 * width
    rows = math.prod(a.size for a in axes)
    share = width // rows
    s = jax.ShapeDtypeStruct
    vm = pl.BlockSpec(memory_space=VMEM)
    weight = s((share, width), f32)
    outs = [
        s((1, *emb.shape), f32), s((1, 1, ITEM_ROW // 2), f32), s((1, 1, seq, width), f32), s((share,), f32),
        weight, weight, weight, weight, s((heads, BUCKETS), f32), s((share,), f32),
        s((share, ff), f32), s((ff // rows, width), f32), s((share,), f32),
    ]
    return pl.pallas_call(
        place_kernel,
        name="place",
        out_shape=outs,
        in_specs=[vm] * (4 + len(JOBS)),
        out_specs=[vm] * len(outs),
        compiler_params=pltpu.CompilerParams(vmem_limit_bytes=VMEM_LIMIT),
    )(emb, loss, small, gh, *res)


def rows_axes(mesh):
    rows = mesh.shape["rows"]
    line = mesh.devices.reshape(-1, rows)[0]
    places = [tuple(getattr(d, "coords", (i % 2, i // 2 % 2, i // 4))) for i, d in enumerate(line)]
    axes = []
    for n in range(3):
        values = sorted({p[n] for p in places})
        stride = next((i for i, p in enumerate(places) if p[n] != places[0][n]), 1)
        axes.append(Axis(len(values), stride))
    return tuple(axes)


def fused(
    axes, hidden_in, segment_ids, positives, attn_gain, w_query, w_key, w_value, w_attn_out, rel_table,
    ffn_gain, w_ffn_in, w_ffn_out, final_gain,
):
    seq, width = hidden_in.shape[2:]
    lanes = jnp.asarray(lane_buckets(), bf16)
    emb, loss, small, gh, _, *res = layer_call(
        axes,
        (
            hidden_in.reshape(seq, width), segment_ids.reshape(1, seq), positives.reshape(1, -1),
            attn_gain, ffn_gain, final_gain, rel_table.T, lanes,
            w_query, w_key, w_value, w_attn_out, w_ffn_in, w_ffn_out,
        ),
    )
    outs = list(place_call(axes, rel_table.shape[1], emb, loss, small, gh, res))
    outs[8] = outs[8].T
    return tuple(outs)


def from_partner(block, axis, bit):
    count = lax.axis_size(axis)
    route = []
    for low in range(count):
        high = low | 1 << bit
        if high != low and high < count:
            route += [(low, high), (high, low)]
    return lax.ppermute(block, axis, route)


def bucket_onehot(seq_len, bucket_count, max_distance):
    half_count = bucket_count // 2
    exact_count = half_count // 2
    log_steps = half_count - exact_count
    bounds = []
    for section_index in range(1, log_steps):
        target = exact_count ** (log_steps - section_index) * max_distance**section_index
        lowest = exact_count
        while lowest**log_steps < target:
            lowest = lowest + 1
        bounds.append(lowest)
    onehot = np.zeros((2 * seq_len - 1, bucket_count), np.float32)
    for offset in range(2 * seq_len - 1):
        relative = offset - (seq_len - 1)
        distance = abs(relative)
        bucket = half_count if relative > 0 else 0
        if distance < exact_count:
            bucket = bucket + distance
        else:
            bucket = (
                bucket
                + exact_count
                + len([boundary for boundary in bounds if distance >= boundary])
            )
        onehot[offset, bucket] = 1.0
    return onehot


def matmul(left_side, right_side):
    return jnp.dot(left_side, right_side, preferred_element_type=jnp.float32)


def contract_rows(left_side, right_side):
    return lax.dot_general(
        left_side, right_side, (((0,), (0,)), ((), ())), preferred_element_type=jnp.float32
    )


def contract_cols(left_side, right_side):
    return lax.dot_general(
        left_side, right_side, (((1,), (1,)), ((), ())), preferred_element_type=jnp.float32
    )


def gelu_slope(values):
    factor = math.sqrt(2.0 / math.pi)
    tangent = jnp.tanh(factor * (values + gelu_cubic * values * values * values))
    return 0.5 * (1.0 + tangent) + 0.5 * values * (1.0 - tangent * tangent) * factor * (
        1.0 + 3.0 * gelu_cubic * values * values
    )


def rms_parts(values):
    inverse = lax.rsqrt(jnp.mean(values * values, axis=-1, keepdims=True) + epsilon)
    return (values * inverse, inverse)


def rms_back(unit_grad, unit_values, inverse):
    return inverse * (
        unit_grad - unit_values * jnp.mean(unit_grad * unit_values, axis=-1, keepdims=True)
    )


def position_bias(rel_table, onehot, seq_len):
    head_count = rel_table.shape[1]
    by_offset = lax.dot_general(
        rel_table.astype(jnp.float32), onehot, (((0,), (1,)), ((), ())), precision=exact
    )
    rolled = jnp.concatenate([by_offset[:, seq_len - 1 :], by_offset[:, : seq_len - 1]], axis=1)
    repeated = jnp.tile(rolled, (1, seq_len))[:, : seq_len * (2 * seq_len - 2)]
    return repeated.reshape(head_count, seq_len, 2 * seq_len - 2)[:, :, :seq_len]


def diagonal_sums(matrix, seq_len):
    head_count = matrix.shape[0]
    flipped = matrix[:, :, ::-1]
    padded = jnp.pad(flipped, ((0, 0), (0, 0), (0, seq_len)))
    skewed = padded.reshape(head_count, 2 * seq_len * seq_len)[:, : seq_len * (2 * seq_len - 1)]
    skewed = skewed.reshape(head_count, seq_len, 2 * seq_len - 1)
    return jnp.sum(skewed, axis=1)[:, ::-1]


def on_device(
    hidden_in,
    segment_ids,
    positives,
    attn_gain,
    w_query,
    w_key,
    w_value,
    w_attn_out,
    rel_table,
    ffn_gain,
    w_ffn_in,
    w_ffn_out,
    final_gain,
):
    row_count = hidden_in.shape[1]
    seq_len = hidden_in.shape[2]
    model_width = hidden_in.shape[3]
    head_count = rel_table.shape[1]
    head_width = model_width // head_count
    token_count = row_count * seq_len
    tokens = hidden_in.reshape(token_count, model_width).astype(jnp.float32)
    segments = segment_ids.reshape(row_count, seq_len)
    gain_one = attn_gain.astype(jnp.float32)
    gain_two = ffn_gain.astype(jnp.float32)
    gain_three = final_gain.astype(jnp.float32)
    onehot = jnp.asarray(bucket_onehot(seq_len, BUCKETS, MAX_DIST))
    unit_one, inverse_one = rms_parts(tokens)
    normed_one = (unit_one * gain_one).astype(jnp.bfloat16)
    query_proj = matmul(normed_one, w_query).astype(jnp.bfloat16)
    key_proj = matmul(normed_one, w_key).astype(jnp.bfloat16)
    value_proj = matmul(normed_one, w_value).astype(jnp.bfloat16)
    bias_full = position_bias(rel_table, onehot, seq_len)

    def split_heads(values):
        return values.reshape(row_count, seq_len, head_count, head_width)

    def row_scores(row_query, row_key, row_seg):
        same_item = row_seg[:, None] == row_seg[None, :]
        similarity_table = jnp.einsum(
            "shd,thd->hst", row_query, row_key, preferred_element_type=jnp.float32
        )
        return jnp.where(same_item[None], similarity_table + bias_full, far_below)

    def forward_row(packed):
        row_query, row_key, row_value, row_seg = packed
        masked_scores = row_scores(row_query, row_key, row_seg)
        row_peak = jnp.max(masked_scores, axis=-1, keepdims=True)
        exp_terms = jnp.exp(masked_scores - row_peak)
        summed = jnp.sum(exp_terms, axis=-1, keepdims=True)
        attn_probs = (exp_terms / summed).astype(jnp.bfloat16)
        combined_attention_output = jnp.einsum(
            "hst,thd->shd", attn_probs, row_value, preferred_element_type=jnp.float32
        )
        return (
            combined_attention_output.astype(jnp.bfloat16),
            (row_peak + jnp.log(summed))[:, :, 0],
        )

    attended, log_norms = lax.map(
        forward_row,
        (split_heads(query_proj), split_heads(key_proj), split_heads(value_proj), segments),
    )
    attended = attended.reshape(token_count, model_width)
    middle = tokens + matmul(attended, w_attn_out)
    unit_two, inverse_two = rms_parts(middle)
    normed_two = (unit_two * gain_two).astype(jnp.bfloat16)
    inner = matmul(normed_two, w_ffn_in)
    hidden = jax.nn.gelu(inner, approximate=True).astype(jnp.bfloat16)
    final_sum = middle + matmul(hidden, w_ffn_out)
    unit_three, inverse_three = rms_parts(final_sum)
    normed_three = unit_three * gain_three
    member = (segments[:, None, :] == jnp.arange(ITEM_ROW, dtype=jnp.int32)[None, :, None]).astype(
        jnp.float32
    )
    counts = jnp.sum(member, axis=-1, keepdims=True)
    pooled = (
        jnp.einsum(
            "ris,rsd->rid",
            member,
            normed_three.reshape(row_count, seq_len, model_width),
            precision=exact,
        )
        / counts
    )
    item_count = row_count * ITEM_ROW
    pooled = pooled.reshape(item_count, model_width)
    inverse_pool = lax.rsqrt(jnp.sum(pooled * pooled, axis=-1, keepdims=True) + epsilon)
    encoded_vector_list = pooled * inverse_pool
    half_items = item_count // 2
    tower_index = lax.axis_index("tower")
    rows_size = lax.axis_size("rows")
    is_query = tower_index == 0
    first_half = encoded_vector_list[:half_items]
    second_half = encoded_vector_list[half_items:]
    outgoing = jnp.where(is_query, second_half, first_half)
    incoming = from_partner(outgoing, "tower", 0)
    my_queries = jnp.where(is_query, first_half, incoming)
    local_passages = jnp.where(is_query, incoming, second_half)
    passage_list = lax.all_gather(local_passages, ("tower", "rows"), axis=0, tiled=True)
    total_items = passage_list.shape[0]
    similarity_table = (
        lax.dot_general(
            my_queries, passage_list, (((1,), (1,)), ((), ())), precision=exact
        )
        / logit_divisor
    )
    my_positive = lax.dynamic_slice_in_dim(positives, tower_index * half_items, half_items)
    column = (
        my_positive // half_items % 2 * (rows_size * half_items)
        + my_positive // item_count * half_items
        + my_positive % half_items
    )
    chosen_mask = (jnp.arange(total_items, dtype=jnp.int32)[None, :] == column[:, None]).astype(
        jnp.float32
    )
    row_peak = jnp.max(similarity_table, axis=1, keepdims=True)
    exp_terms = jnp.exp(similarity_table - row_peak)
    summed = jnp.sum(exp_terms, axis=1, keepdims=True)
    losses = (
        row_peak[:, 0] + jnp.log(summed[:, 0]) - jnp.sum(similarity_table * chosen_mask, axis=1)
    )
    similarity_derivative = loss_scale * (exp_terms / summed - chosen_mask)
    query_embedding_gradient = (
        jnp.dot(similarity_derivative, passage_list, precision=exact) / logit_divisor
    )
    doc_embed_grad = lax.psum_scatter(
        lax.dot_general(
            similarity_derivative, my_queries, (((0,), (0,)), ((), ())), precision=exact
        )
        / logit_divisor,
        ("tower", "rows"),
        scatter_dimension=0,
        tiled=True,
    )
    sendback = jnp.where(is_query, doc_embed_grad, query_embedding_gradient)
    received = from_partner(sendback, "tower", 0)
    embed_grad = jnp.where(
        is_query,
        jnp.concatenate([query_embedding_gradient, received], axis=0),
        jnp.concatenate([received, doc_embed_grad], axis=0),
    )
    inner_dot = jnp.sum(encoded_vector_list * embed_grad, axis=-1, keepdims=True)
    pooled_grad = inverse_pool * (embed_grad - encoded_vector_list * inner_dot)
    spread = member / counts
    three_grad = jnp.einsum(
        "ris,rid->rsd",
        spread,
        pooled_grad.reshape(row_count, ITEM_ROW, model_width),
        precision=exact,
    )
    three_grad = three_grad.reshape(token_count, model_width)
    final_gain_grad = jnp.sum(three_grad * unit_three, axis=0)
    final_grad = rms_back(three_grad * gain_three, unit_three, inverse_three)
    branch_two_grad = final_grad.astype(jnp.bfloat16)
    ffn_out_grad = contract_rows(hidden, branch_two_grad)
    inner_grad = (contract_cols(branch_two_grad, w_ffn_out) * gelu_slope(inner)).astype(
        jnp.bfloat16
    )
    ffn_in_grad = contract_rows(normed_two, inner_grad)
    two_grad = contract_cols(inner_grad, w_ffn_in)
    ffn_gain_grad = jnp.sum(two_grad * unit_two, axis=0)
    middle_grad = final_grad + rms_back(two_grad * gain_two, unit_two, inverse_two)
    branch_one_grad = middle_grad.astype(jnp.bfloat16)
    attn_out_grad = contract_rows(attended, branch_one_grad)
    attended_grad = contract_cols(branch_one_grad, w_attn_out).astype(jnp.bfloat16)

    def backward_row(bias_total, packed):
        row_query, row_key, row_value, row_seg, row_norm, row_grad = packed
        masked_scores = row_scores(row_query, row_key, row_seg)
        attn_probs = jnp.exp(masked_scores - row_norm[:, :, None])
        probs_grad = jnp.einsum(
            "shd,thd->hst", row_grad, row_value, preferred_element_type=jnp.float32
        )
        value_grad = jnp.einsum(
            "hst,shd->thd",
            attn_probs.astype(jnp.bfloat16),
            row_grad,
            preferred_element_type=jnp.float32,
        )
        score_part_grad = attn_probs * (
            probs_grad - jnp.sum(attn_probs * probs_grad, axis=-1, keepdims=True)
        )
        rounded = score_part_grad.astype(jnp.bfloat16)
        query_grad = jnp.einsum(
            "hst,thd->shd", rounded, row_key, preferred_element_type=jnp.float32
        )
        key_grad = jnp.einsum(
            "hst,shd->thd", rounded, row_query, preferred_element_type=jnp.float32
        )
        return (
            bias_total + score_part_grad,
            (
                query_grad.astype(jnp.bfloat16),
                key_grad.astype(jnp.bfloat16),
                value_grad.astype(jnp.bfloat16),
            ),
        )

    bias_total, head_grads = lax.scan(
        backward_row,
        jnp.zeros((head_count, seq_len, seq_len), jnp.float32),
        (
            split_heads(query_proj),
            split_heads(key_proj),
            split_heads(value_proj),
            segments,
            log_norms,
            split_heads(attended_grad),
        ),
    )
    query_grad = head_grads[0].reshape(token_count, model_width)
    key_grad = head_grads[1].reshape(token_count, model_width)
    value_grad = head_grads[2].reshape(token_count, model_width)
    table_local = jnp.einsum(
        "ib,hi->bh", onehot, diagonal_sums(bias_total, seq_len), precision=exact
    )
    query_w_grad = contract_rows(normed_one, query_grad)
    key_w_grad = contract_rows(normed_one, key_grad)
    value_w_grad = contract_rows(normed_one, value_grad)
    one_grad = (
        contract_cols(query_grad, w_query)
        + contract_cols(key_grad, w_key)
        + contract_cols(value_grad, w_value)
    )
    attn_gain_grad = jnp.sum(one_grad * unit_one, axis=0)
    input_grad = middle_grad + rms_back(one_grad * gain_one, unit_one, inverse_one)
    table_grad = lax.psum(table_local, ("tower", "rows"))
    shares = (
        lax.psum_scatter(attn_gain_grad, "rows", scatter_dimension=0, tiled=True),
        lax.psum_scatter(query_w_grad, "rows", scatter_dimension=0, tiled=True),
        lax.psum_scatter(key_w_grad, "rows", scatter_dimension=0, tiled=True),
        lax.psum_scatter(value_w_grad, "rows", scatter_dimension=0, tiled=True),
        lax.psum_scatter(attn_out_grad, "rows", scatter_dimension=0, tiled=True),
        lax.psum_scatter(ffn_gain_grad, "rows", scatter_dimension=0, tiled=True),
        lax.psum_scatter(ffn_in_grad, "rows", scatter_dimension=0, tiled=True),
        lax.psum_scatter(ffn_out_grad, "rows", scatter_dimension=0, tiled=True),
        lax.psum_scatter(final_gain_grad, "rows", scatter_dimension=0, tiled=True),
    )
    summed_grads = lax.psum(
        (
            shares[0],
            shares[1],
            shares[2],
            shares[3],
            shares[4],
            shares[5],
            shares[6],
            shares[7],
            shares[8],
        ),
        "tower",
    )
    return (
        encoded_vector_list[None],
        losses.reshape(1, 1, half_items),
        input_grad.reshape(hidden_in.shape),
        summed_grads[0],
        summed_grads[1],
        summed_grads[2],
        summed_grads[3],
        summed_grads[4],
        table_grad,
        summed_grads[5],
        summed_grads[6],
        summed_grads[7],
        summed_grads[8],
    )


def solution(mesh):
    in_specs = (
        P("tower", "rows", None, None),
        P("tower", "rows", None),
        P("rows"),
        P(),
        P(),
        P(),
        P(),
        P(),
        P(),
        P(),
        P(),
        P(),
        P(),
    )
    out_specs = (
        P("tower", "rows", None),
        P("rows", "tower", None),
        P("tower", "rows", None, None),
        P("rows"),
        P("rows", None),
        P("rows", None),
        P("rows", None),
        P("rows", None),
        P(),
        P("rows"),
        P("rows", None),
        P("rows", None),
        P("rows"),
    )
    axes = rows_axes(mesh)
    sized = mesh.shape["tower"] == 2 and tuple(ax.size for ax in axes) == STEPS_SIZES
    body = functools.partial(fused, axes) if sized else on_device
    return jax.shard_map(
        body, mesh=mesh, in_specs=in_specs, out_specs=out_specs, check_vma=False
    )
```
